768 devices in a mesh: dp: 48 (over x, z), shuffle: 16 (over y, core).
Axes of the slice: x: 4, y: 8, z: 12, core: 2. Of those that a mesh axis runs over, the one named last changes fastest.
Arguments:
- history_rows: bfloat16 [196608, 512], P(('dp', 'shuffle')), may hold values from -6 to 6
- cotangent: bfloat16 [196608, 512], P(('dp', 'shuffle')), may hold values from -6 to 6
- dest_device: int32 [768, 8], P(('dp', 'shuffle')), may hold values from 0 to 15, as said below
- source_device: int32 [768, 8], P(('dp', 'shuffle')), may hold values from 0 to 15, as said below
- source_offset: int32 [768, 8], P(('dp', 'shuffle')), may hold values from 0 to 1, as said below
- segments: int32 [768, 256], P(('dp', 'shuffle')), may hold values from 0 to 3, as said below
- row_valid: int32 [768, 256], P(('dp', 'shuffle')), may hold values from 0 to 1, as said below
- joined_weight: bfloat16 [512, 2048], replicated, may hold values from -0.25 to 0.25
- output_weight: bfloat16 [512, 512], replicated, may hold values from -0.25 to 0.25
Outputs:
- row_grad: bfloat16 [196608, 512], P(('dp', 'shuffle'))
- joined_grad: float32 [512, 2048], P('shuffle')
- output_grad: float32 [512, 512], P('shuffle')
The draws below stay inside these ranges and needn't reach their ends.
Inputs may be any that keep to these rules, and one draw needn't show every extreme that they name: `dest_device`: each device sends its 8 blocks to devices of its own dp index, at most 2 to any one device, and in every group some device sends exactly 2 to one device; every device receives exactly 8 blocks. Consistent with dest_device: the pairs (source_device, source_offset) of one device are distinct and name exactly the blocks sent to it. `source_offset`: see source_device. `segments`: in each aligned window of 128 rows the numbers start at 0, never fall and rise by one between histories; each history fills whole blocks. `row_valid`: every block but a history's last is all ones; a history's last block has 1 to 32 leading ones, then zeros.
All inputs are finite; a program needn't handle non-finite values.
Results may differ from the reference program's by a relative error of at most 0.025.
Values may be sent and summed in bfloat16 or wider, within the bound.
No kernel may reach another device: no remote copies, remote signals or barrier semaphores. Data moves between devices by JAX's collectives and lax.ppermute only.
A program may use at most 64 MiB of HBM per device.

```python
import math
import jax
import jax.numpy as jnp
from jax import lax

D = 512
HEADS = 8
BLOCK = 32
WIN_BLK = 4
BLK_DEV = 8
ROWS_DEV = 256
WIN = 128
PEER_CAP = 2
TOKENS = 196608
N_DP = 48
N_SHUFFLE = 16
DEVICES = 768


def group_plan(group_key):
    first_key, second_key, third_key = jax.random.split(group_key, 3)
    lane_index = jnp.arange(N_SHUFFLE, dtype=jnp.int32)
    slot_index = jnp.arange(BLK_DEV, dtype=jnp.int32)
    peer_pick = jax.random.permutation(first_key, N_SHUFFLE).astype(jnp.int32)
    offsets = peer_pick[slot_index // PEER_CAP]
    loader_order = jax.vmap(lambda one_key: jax.random.permutation(one_key, BLK_DEV))(jax.random.split(second_key, N_SHUFFLE)).astype(jnp.int32)
    targets = (lane_index[:, None] + offsets[loader_order]) % N_SHUFFLE
    same_target = targets[:, :, None] == targets[:, None, :]
    earlier = slot_index[None, :] < slot_index[:, None]
    rank_of_slot = jnp.sum((same_target & earlier[None]).astype(jnp.int32), axis=2, dtype=jnp.int32)
    inverse_order = jnp.argsort(loader_order, axis=1).astype(jnp.int32)
    source_stream = (lane_index[:, None] - offsets[None, :]) % N_SHUFFLE
    local_slot = inverse_order[source_stream, slot_index[None, :]]
    rank_stream = rank_of_slot[source_stream, local_slot]
    worker_order = jax.vmap(lambda one_key: jax.random.permutation(one_key, BLK_DEV))(jax.random.split(third_key, N_SHUFFLE)).astype(jnp.int32)
    sources = jnp.take_along_axis(source_stream, worker_order, axis=1)
    ranks = jnp.take_along_axis(rank_stream, worker_order, axis=1)
    return (targets.astype(jnp.int32), sources.astype(jnp.int32), ranks.astype(jnp.int32))


def plan_tables(base_key):
    plan_key = jax.random.fold_in(base_key, 11)
    group_keys = jax.random.split(plan_key, DEVICES // N_SHUFFLE)
    targets, sources, ranks = jax.vmap(group_plan)(group_keys)
    return (targets.reshape(DEVICES, BLK_DEV), sources.reshape(DEVICES, BLK_DEV), ranks.reshape(DEVICES, BLK_DEV))


def window_tables(base_key):
    window_key = jax.random.fold_in(base_key, 23)
    first_key, second_key = jax.random.split(window_key)
    window_count = DEVICES * BLK_DEV // WIN_BLK
    boundaries = jax.random.randint(first_key, (window_count, WIN_BLK - 1), 0, 2, dtype=jnp.int32)
    last_fill = jax.random.randint(second_key, (window_count, WIN_BLK), 1, BLOCK + 1, dtype=jnp.int32)
    seg_blocks = jnp.concatenate([jnp.zeros((window_count, 1), jnp.int32), jnp.cumsum(boundaries, axis=1, dtype=jnp.int32)], axis=1)
    last_block = jnp.concatenate([boundaries, jnp.ones((window_count, 1), jnp.int32)], axis=1) == 1
    row_place = jnp.arange(BLOCK, dtype=jnp.int32)
    valid = jnp.where(last_block[:, :, None], row_place[None, None, :] < last_fill[:, :, None], True).astype(jnp.int32)
    seg_rows = jnp.broadcast_to(seg_blocks[:, :, None], (window_count, WIN_BLK, BLOCK))
    return (seg_rows.reshape(DEVICES, ROWS_DEV).astype(jnp.int32), valid.reshape(DEVICES, ROWS_DEV))


def draw_dest_device(key, part):
    tables = plan_tables(key)
    return tables[0]


def draw_source_device(key, part):
    tables = plan_tables(key)
    return tables[1]


def draw_source_offset(key, part):
    tables = plan_tables(key)
    return tables[2]


def draw_segments(key, part):
    tables = window_tables(key)
    return tables[0]


def draw_row_valid(key, part):
    tables = window_tables(key)
    return tables[1]


def shard_levels(stream_key, shape, cuts, smallest, largest):
    level, own = 1.0, jax.random.fold_in(stream_key, 6)
    for position, shards_of in cuts:
        draws = jnp.exp(jax.random.uniform(jax.random.fold_in(own, position), (shards_of,), jnp.float32, smallest / len(cuts), largest / len(cuts)))
        level = level * jnp.repeat(draws, shape[position] // shards_of).reshape([-1 if axis == position else 1 for axis in range(len(shape))])
    return level


def noise(key, extent, deviation, reach, pieces=(), kind=jnp.bfloat16):
    array = deviation * jax.random.normal(key, extent, jnp.float32)
    if pieces:
        array = array * shard_levels(key, extent, pieces, -0.22, 0.18)
    return jnp.clip(array, -reach, reach).astype(kind)


def setup_inputs(seed: int = 0) -> dict:
    keys = jax.random.split(jax.random.key(seed), 10)
    history_rows = noise(keys[0], (TOKENS, D), 1.0, 6.0, ((0, 768),))
    cotangent = noise(keys[1], (TOKENS, D), 1.0, 6.0, ((0, 768),))
    dest_device = draw_dest_device(jax.random.fold_in(keys[9], 71), 0)
    source_device = draw_source_device(jax.random.fold_in(keys[9], 71), 0)
    source_offset = draw_source_offset(jax.random.fold_in(keys[9], 71), 0)
    segments = draw_segments(jax.random.fold_in(keys[9], 71), 0)
    row_valid = draw_row_valid(jax.random.fold_in(keys[9], 71), 0)
    joined_weight = noise(keys[7], (D, 4 * D), D ** -0.5, 0.25)
    output_weight = noise(keys[8], (D, D), D ** -0.5, 0.25)
    return {"history_rows": history_rows, "cotangent": cotangent, "dest_device": dest_device, "source_device": source_device, "source_offset": source_offset, "segments": segments, "row_valid": row_valid, "joined_weight": joined_weight, "output_weight": output_weight}


epsilon = 1e-05

def row_norm(features):
    centred = features - lax.optimization_barrier(jnp.mean(features, axis=-1, keepdims=True))
    spread = lax.optimization_barrier(jnp.mean(centred * centred, axis=-1, keepdims=True))
    return centred * lax.rsqrt(spread + epsilon)

def middle(projected, seg_rows, valid_rows):
    active = jax.nn.silu(projected).astype(jnp.bfloat16)
    total_rows = projected.shape[0]
    feature_count = projected.shape[1] // 4
    head_size = feature_count // HEADS
    windows = total_rows // WIN
    gate_part = active[:, :feature_count]
    value_part = active[:, feature_count:2 * feature_count]
    query_part = active[:, 2 * feature_count:3 * feature_count]
    key_part = active[:, 3 * feature_count:]

    def split_heads(block_part):
        return block_part.reshape(windows, WIN, HEADS, head_size).astype(jnp.float32)
    scores = jnp.einsum('wqhe,wkhe->whqk', split_heads(query_part), split_heads(key_part)) * head_size ** (-0.5)
    seg_win = seg_rows.reshape(windows, WIN)
    valid_win = valid_rows.reshape(windows, WIN)
    places = jnp.arange(WIN, dtype=jnp.int32)
    allowed = (seg_win[:, :, None] == seg_win[:, None, :]) & (places[None, None, :] <= places[None, :, None]) & (valid_win[:, None, :] == 1)
    allowed_float = allowed.astype(jnp.float32)
    counts = lax.optimization_barrier(jnp.sum(allowed_float, axis=-1))
    weights = allowed_float / jnp.maximum(counts, 1.0)[:, :, None]
    weighting = (jax.nn.silu(scores) * weights[:, None, :, :]).astype(jnp.bfloat16)
    mixture = jnp.einsum('whqk,wkhe->wqhe', weighting.astype(jnp.float32), split_heads(value_part)).reshape(total_rows, feature_count)
    return row_norm(mixture) * gate_part.astype(jnp.float32)

def forward_pass(features, seg_rows, valid_rows, joined_weight):
    normed_full, norm_back = jax.vjp(row_norm, features.astype(jnp.float32))
    normed = normed_full.astype(jnp.bfloat16)
    projected = jnp.dot(normed, joined_weight, preferred_element_type=jnp.float32)
    gated_full, middle_back = jax.vjp(lambda projected_in: middle(projected_in, seg_rows, valid_rows), projected)
    return (normed, norm_back, gated_full.astype(jnp.bfloat16), middle_back)

def backward_pass(stored, cot_rows, valid_rows, joined_weight, output_weight):
    normed, norm_back, gated_rows, middle_back = stored
    masked = cot_rows * valid_rows[:, None].astype(jnp.bfloat16)
    gated_cot = jnp.dot(masked, output_weight.T, preferred_element_type=jnp.float32)
    proj_full, = middle_back(gated_cot)
    proj_cot = proj_full.astype(jnp.bfloat16)
    normed_cot = jnp.dot(proj_cot, joined_weight.T, preferred_element_type=jnp.float32)
    rows_cot, = norm_back(normed_cot)
    work_grad = (masked.astype(jnp.float32) + rows_cot).astype(jnp.bfloat16)
    joined_part = jnp.dot(normed.T, proj_cot, preferred_element_type=jnp.float32)
    output_part = jnp.dot(gated_rows.T, masked, preferred_element_type=jnp.float32)
    return (work_grad, joined_part, output_part)

def reference(history_rows, cotangent, dest_device, source_device, source_offset, segments, row_valid, joined_weight, output_weight):
    groups = N_DP
    lane_count = N_SHUFFLE
    loaded_rows = history_rows.reshape(groups, lane_count, BLK_DEV, BLOCK, D)
    loaded_cot = cotangent.reshape(groups, lane_count, BLK_DEV, BLOCK, D)
    dest_all = dest_device.reshape(groups, lane_count, BLK_DEV)
    source_all = source_device.reshape(groups, lane_count, BLK_DEV)
    offset_all = source_offset.reshape(groups, lane_count, BLK_DEV)
    seg_all = segments.reshape(groups, lane_count, ROWS_DEV)
    valid_all = row_valid.reshape(groups, lane_count, ROWS_DEV)
    slot_index = jnp.arange(BLK_DEV, dtype=jnp.int32)
    peer_index = jnp.arange(lane_count, dtype=jnp.int32)

    def one_worker(features, cot_rows, seg_rows, valid_rows):
        stored = forward_pass(features, seg_rows, valid_rows, joined_weight)
        return backward_pass(stored, cot_rows, valid_rows, joined_weight, output_weight)

    def one_group(totals, group_items):
        group_rows, group_cot, group_dest, group_source, group_offset, group_seg, group_valid = group_items
        same_target = group_dest[:, :, None] == group_dest[:, None, :]
        earlier = slot_index[None, :] < slot_index[:, None]
        rank_of_slot = lax.optimization_barrier(jnp.sum((same_target & earlier[None]).astype(jnp.int32), axis=2, dtype=jnp.int32))
        matching = (group_dest[group_source] == peer_index[:, None, None]) & (rank_of_slot[group_source] == group_offset[:, :, None])
        local_slot = lax.optimization_barrier(jnp.sum(matching.astype(jnp.int32) * slot_index, axis=-1, dtype=jnp.int32))
        work_rows = group_rows[group_source, local_slot].reshape(lane_count, ROWS_DEV, D)
        work_cot = group_cot[group_source, local_slot].reshape(lane_count, ROWS_DEV, D)
        work_grads, joined_parts, output_parts = jax.vmap(one_worker)(work_rows, work_cot, group_seg, group_valid)
        back_match = (group_source[group_dest] == peer_index[:, None, None]) & (group_offset[group_dest] == rank_of_slot[:, :, None])
        worker_slot = lax.optimization_barrier(jnp.sum(back_match.astype(jnp.int32) * slot_index, axis=-1, dtype=jnp.int32))
        returned = work_grads.reshape(lane_count, BLK_DEV, BLOCK, D)[group_dest, worker_slot]
        return ((totals[0] + lax.optimization_barrier(jnp.sum(joined_parts, axis=0)), totals[1] + lax.optimization_barrier(jnp.sum(output_parts, axis=0))), returned)
    initial = (jnp.zeros((D, 4 * D), jnp.float32), jnp.zeros((D, D), jnp.float32))
    totals, returned = lax.scan(one_group, initial, (loaded_rows, loaded_cot, dest_all, source_all, offset_all, seg_all, valid_all))
    scaling = 1.0 / math.sqrt(TOKENS)
    return (returned.reshape(TOKENS, D), totals[0] * scaling, totals[1] * scaling)
```

```python
import functools
import math

import jax
import jax.numpy as jnp
from jax import lax
from jax.experimental import pallas as pl
from jax.experimental.pallas import tpu as pltpu
from jax.sharding import Mesh, PartitionSpec as P

HEADS = 8
WIN = 128
epsilon = 1e-05
f32 = jnp.float32
bf16 = jnp.bfloat16
VMEM_LIMIT = 48 * 1024 * 1024
NT = (((1,), (1,)), ((), ()))
TN = (((0,), (0,)), ((), ()))


def dot(a, b, dims=(((1,), (0,)), ((), ()))):
    return lax.dot_general(a, b, dims, preferred_element_type=f32)


def row_norm(features):
    centred = features - jnp.mean(features, axis=-1, keepdims=True)
    spread = jnp.mean(centred * centred, axis=-1, keepdims=True)
    inverse = lax.rsqrt(spread + epsilon)
    return centred * inverse, inverse


def row_norm_back(cot, normed, inverse):
    mean_cot = jnp.mean(cot, axis=-1, keepdims=True)
    mean_both = jnp.mean(cot * normed, axis=-1, keepdims=True)
    return inverse * (cot - mean_cot - normed * mean_both)


def as_column(row, diagonal):
    return jnp.sum(jnp.where(diagonal, row, 0.0), axis=1, keepdims=True)


def forward_body(
    rows_ref,
    seg_ref,
    valid_ref,
    weight_ref,
    normed_ref,
    inverse_ref,
    active_ref,
    slope_ref,
    weighting_ref,
    score_slope_ref,
    mixed_ref,
    mix_inverse_ref,
    gated_ref,
):
    rows, width = rows_ref.shape
    head = width // HEADS
    pair = 2 * head
    normed, inverse = row_norm(rows_ref[...].astype(f32))
    normed = normed.astype(bf16)
    normed_ref[...] = normed
    inverse_ref[...] = inverse
    for quarter in range(4):
        columns = slice(quarter * width, (quarter + 1) * width)
        projected = dot(normed, weight_ref[:, columns])
        gate = jax.nn.sigmoid(projected)
        active_ref[:, columns] = (projected * gate).astype(bf16)
        slope_ref[:, columns] = (gate * (1.0 + projected * (1.0 - gate))).astype(bf16)
    left = lax.broadcasted_iota(jnp.int32, (WIN, pair), 1) < head
    place_i = lax.broadcasted_iota(jnp.int32, (WIN, WIN), 0)
    place_j = lax.broadcasted_iota(jnp.int32, (WIN, WIN), 1)
    zero = jnp.zeros((), bf16)

    def stacked(block):
        return jnp.concatenate([jnp.where(left, block, zero), jnp.where(left, zero, block)], axis=0)

    for window in range(rows // WIN):
        span = slice(window * WIN, (window + 1) * WIN)
        seg_row = seg_ref[:, span].astype(f32)
        seg_col = as_column(seg_row, place_i == place_j)
        allowed = (seg_col == seg_row) & (place_j <= place_i) & (valid_ref[:, span] == 1)
        allowed = jnp.where(allowed, 1.0, 0.0)
        weights = allowed / jnp.maximum(jnp.sum(allowed, axis=1, keepdims=True), 1.0)
        weights = jnp.concatenate([weights, weights], axis=1)
        mixture = []
        for p in range(HEADS // 2):
            at = p * pair
            value = active_ref[span, width + at : width + at + pair]
            query = active_ref[span, 2 * width + at : 2 * width + at + pair]
            key = active_ref[span, 3 * width + at : 3 * width + at + pair]
            scores = dot(query, stacked(key), NT) * head**-0.5
            gate = jax.nn.sigmoid(scores)
            weighting = (scores * gate * weights).astype(bf16)
            slot = window * (HEADS // 2) + p
            weighting_ref[slot] = weighting
            score_slope_ref[slot] = (
                gate * (1.0 + scores * (1.0 - gate)) * (weights * head**-0.5)
            ).astype(bf16)
            mixture.append(dot(weighting, stacked(value)))
        mixed, mix_inverse = row_norm(jnp.concatenate(mixture, axis=1))
        mixed_ref[span, :] = mixed
        mix_inverse_ref[span, :] = mix_inverse
        gated_ref[span, :] = (mixed * active_ref[span, :width].astype(f32)).astype(bf16)


def backward_body(
    rows_ref,
    cot_ref,
    valid_ref,
    weight_ref,
    out_weight_ref,
    normed_ref,
    inverse_ref,
    active_ref,
    slope_ref,
    weighting_ref,
    score_slope_ref,
    mixed_ref,
    mix_inverse_ref,
    gated_ref,
    proj_cot_ref,
    spread,
    keep_ref,
    send_ref,
):
    rows, width = rows_ref.shape
    head = width // HEADS
    pair = 2 * head
    place_i = lax.broadcasted_iota(jnp.int32, (rows, rows), 0)
    place_j = lax.broadcasted_iota(jnp.int32, (rows, rows), 1)
    valid_col = as_column(valid_ref[...].astype(f32), place_i == place_j)
    masked_f = cot_ref[...].astype(f32) * valid_col
    masked = masked_f.astype(bf16)
    side = width // 2

    def put_grad(factor, cot, at):
        grad = dot(factor, cot).astype(bf16)
        keep_ref[:, at : at + width] = grad[:side]
        send_ref[:, at : at + width] = grad[side:]

    put_grad(permute(spread, gated_ref[...], NT), masked, 4 * width)
    gated_cot = dot(masked, out_weight_ref[...], NT)
    mixed = mixed_ref[...]
    gate_cot = (gated_cot * mixed).astype(bf16).astype(f32)
    proj_cot_ref[:, :width] = (gate_cot * slope_ref[:, :width].astype(f32)).astype(bf16)
    mixture_cot = row_norm_back(
        gated_cot * active_ref[:, :width].astype(f32), mixed, mix_inverse_ref[...]
    ).astype(bf16)
    left = lax.broadcasted_iota(jnp.int32, (WIN, pair), 1) < head
    zero = jnp.zeros((), bf16)

    def stacked(block):
        return jnp.concatenate([jnp.where(left, block, zero), jnp.where(left, zero, block)], axis=0)

    def folded(block):
        return jnp.where(left, block[:WIN], block[WIN:])

    for window in range(rows // WIN):
        span = slice(window * WIN, (window + 1) * WIN)
        for p in range(HEADS // 2):
            at = p * pair
            slot = window * (HEADS // 2) + p

            def put(quarter, cot):
                columns = slice(quarter * width + at, quarter * width + at + pair)
                slope = slope_ref[span, columns].astype(f32)
                proj_cot_ref[span, columns] = (cot.astype(bf16).astype(f32) * slope).astype(bf16)

            value = active_ref[span, width + at : width + at + pair]
            query = active_ref[span, 2 * width + at : 2 * width + at + pair]
            key = active_ref[span, 3 * width + at : 3 * width + at + pair]
            mix_cot = mixture_cot[span, at : at + pair]
            put(1, folded(dot(weighting_ref[slot], mix_cot, TN)))
            weighting_cot = dot(mix_cot, stacked(value), NT).astype(bf16).astype(f32)
            score_cot = (weighting_cot * score_slope_ref[slot].astype(f32)).astype(bf16)
            put(2, dot(score_cot, stacked(key)))
            put(3, folded(dot(score_cot, query, TN)))
    normed_t = permute(spread, normed_ref[...], NT)
    normed_cot = jnp.zeros((rows, width), f32)
    for quarter in range(4):
        columns = slice(quarter * width, (quarter + 1) * width)
        proj_cot = proj_cot_ref[:, columns]
        put_grad(normed_t, proj_cot, quarter * width)
        normed_cot += dot(proj_cot, weight_ref[:, columns], NT)
    features = rows_ref[...].astype(f32)
    inverse = inverse_ref[...]
    normed_f = (features - jnp.mean(features, axis=-1, keepdims=True)) * inverse
    rows_cot = row_norm_back(normed_cot, normed_f, inverse)
    return (masked_f + rows_cot).astype(bf16)


def permute(order, block, dims=(((1,), (0,)), ((), ()))):
    return dot(order, block, dims).astype(bf16)


def pack_kernel(lanes, dest_ref, rows_ref, cot_ref, out_ref):
    rows, width = rows_ref.shape
    blocks = dest_ref.shape[1]
    chunk = rows // lanes
    half = chunk // blocks
    place = lax.broadcasted_iota(jnp.int32, (rows, rows), 0)
    loaded = lax.broadcasted_iota(jnp.int32, (rows, rows), 1)
    source = place % blocks * (rows // blocks) + place // blocks % half * lanes + place // chunk
    order = jnp.where(source == loaded, 1.0, 0.0).astype(bf16)
    out_ref[:, :width] = permute(order, rows_ref[...])
    out_ref[:, width : 2 * width] = permute(order, cot_ref[...])
    extra = out_ref.shape[1] - 2 * width
    block = lax.broadcasted_iota(jnp.int32, (rows, extra), 0) % blocks
    dest = jnp.zeros((rows, extra), f32)
    for j in range(blocks):
        dest = jnp.where(block == j, dest_ref[0, j].astype(f32), dest)
    out_ref[:, 2 * width :] = dest.astype(bf16)


def route_kernel(lanes, in_ref, out_ref, order_ref):
    rows, double = out_ref.shape
    chunk = rows // lanes
    blocks = chunk // 2
    extra = in_ref.shape[1] - double
    place = lax.broadcasted_iota(jnp.int32, (rows, rows), 0)
    other = lax.broadcasted_iota(jnp.int32, (rows, rows), 1)
    lane = lax.broadcasted_iota(jnp.int32, (rows, extra), 1)
    dest = in_ref[:, double:].astype(f32)
    chosen = jnp.where(dest == lane.astype(f32), 1.0, 0.0)
    same_half = place // blocks % 2 == other // blocks % 2
    earlier = jnp.where(same_half & (other < place), 1.0, 0.0).astype(bf16)
    rank = jnp.sum(dot(earlier, chosen.astype(bf16)) * chosen, axis=1, keepdims=True)
    row = lax.broadcasted_iota(jnp.int32, (rows, 1), 0)
    target = dest[:, :1] * chunk + (row // blocks % 2 * blocks).astype(f32) + rank
    order = jnp.where(target == other.astype(f32), 1.0, 0.0).astype(bf16)
    order_ref[...] = order
    out_ref[...] = permute(order, in_ref[:, :double], TN)


def gather_order(lanes, sources_ref, offsets_ref, order_ref):
    rows = order_ref.shape[0]
    blocks = sources_ref.shape[1]
    chunk = rows // lanes
    half = chunk // blocks
    span = rows // blocks
    inside = lax.broadcasted_iota(jnp.int32, (span, rows), 0)
    column = lax.broadcasted_iota(jnp.int32, (span, rows), 1)
    base = inside % lanes * chunk + inside // lanes % half * blocks
    keys = [sources_ref[0, t] * 2 + offsets_ref[0, t] for t in range(blocks)]
    for t in range(blocks):
        slot = sum(jnp.where(keys[u] < keys[t], 1, 0) for u in range(blocks) if u != t)
        order = jnp.where(column == base + slot, 1.0, 0.0)
        order_ref[t * span : (t + 1) * span, :] = order.astype(bf16)


def spread_order(parts, core, width):
    xs, ys = parts
    out = lax.broadcasted_iota(jnp.int32, (width, width), 0)
    column = lax.broadcasted_iota(jnp.int32, (width, width), 1)
    side = width // 2
    block = width // ys // 2
    piece = block // xs
    y = out // piece % ys
    x = out % side // (piece * ys)
    parity = (out // side + core) % 2
    source = y * (2 * block) + parity * block + x * piece + out % piece
    return jnp.where(source == column, 1.0, 0.0).astype(bf16)


def layer_kernel(
    lanes,
    parts,
    core_ref,
    sources_ref,
    offsets_ref,
    in_ref,
    seg_ref,
    valid_ref,
    weight_ref,
    out_weight_ref,
    leave_ref,
    keep_ref,
    send_ref,
    order_ref,
    rows_ref,
    cot_ref,
    normed_ref,
    inverse_ref,
    active_ref,
    slope_ref,
    weighting_ref,
    score_slope_ref,
    mixed_ref,
    mix_inverse_ref,
    gated_ref,
    proj_cot_ref,
):
    rows, width = rows_ref.shape
    gather_order(lanes, sources_ref, offsets_ref, order_ref)
    rows_ref[...] = permute(order_ref[...], in_ref[:, :width])
    cot_ref[...] = permute(order_ref[...], in_ref[:, width:])
    stored = (
        normed_ref,
        inverse_ref,
        active_ref,
        slope_ref,
        weighting_ref,
        score_slope_ref,
        mixed_ref,
        mix_inverse_ref,
        gated_ref,
    )
    forward_body(rows_ref, seg_ref, valid_ref, weight_ref, *stored)
    spread = spread_order(parts, core_ref[0], width)
    work_grad = backward_body(
        rows_ref,
        cot_ref,
        valid_ref,
        weight_ref,
        out_weight_ref,
        *stored,
        proj_cot_ref,
        spread,
        keep_ref,
        send_ref,
    )
    leave_ref[...] = permute(order_ref[...], work_grad, TN)


def return_kernel(order_ref, in_ref, out_ref):
    out_ref[...] = permute(order_ref[...], in_ref[...])


def unpack_kernel(lanes, blocks, in_ref, out_ref):
    rows = in_ref.shape[0]
    chunk = rows // lanes
    half = chunk // blocks
    loaded = lax.broadcasted_iota(jnp.int32, (rows, rows), 0)
    place = lax.broadcasted_iota(jnp.int32, (rows, rows), 1)
    source = place % blocks * (rows // blocks) + place // blocks % half * lanes + place // chunk
    order = jnp.where(source == loaded, 1.0, 0.0).astype(bf16)
    out_ref[...] = permute(order, in_ref[...])


def split_kernel(in_ref, out_ref):
    pieces, piece = out_ref.shape[1], out_ref.shape[3]
    for k in range(pieces):
        if (k + 1) * piece <= in_ref.shape[2]:
            out_ref[:, k] = in_ref[:, :, k * piece : (k + 1) * piece]
        else:
            out_ref[:, k] = jnp.zeros(out_ref.shape[:1] + out_ref.shape[2:], bf16)


def total_kernel(scaling, in_ref, out_ref):
    total = jnp.sum(in_ref[...].astype(f32), axis=0, keepdims=True) * scaling
    out_ref[...] = jnp.broadcast_to(total.astype(bf16), out_ref.shape)


def result_kernel(in_ref, joined_ref, output_ref):
    xs, zs, piece_rows, piece = in_ref.shape
    split = joined_ref.shape[1]
    step = math.gcd(piece, split)
    for x in range(xs):
        span = slice(x * piece_rows, (x + 1) * piece_rows)
        for at in range(0, split + output_ref.shape[1], step):
            block = in_ref[x, at // piece, :, at % piece : at % piece + step].astype(f32)
            if at < split:
                joined_ref[span, at : at + step] = block
            else:
                output_ref[span, at - split : at - split + step] = block


def call(kernel, name, out_shape, operands, flops=0, scalars=0, scratch=()):
    moved = sum(math.prod(a.shape) * a.dtype.itemsize for a in (*operands, *out_shape))
    smem = pl.BlockSpec(memory_space=pltpu.SMEM)
    vmem = pl.BlockSpec(memory_space=pltpu.VMEM)
    return pl.pallas_call(
        kernel,
        out_shape=tuple(out_shape),
        in_specs=[smem] * scalars + [vmem] * (len(operands) - scalars),
        out_specs=tuple(vmem for _ in out_shape),
        scratch_shapes=list(scratch),
        compiler_params=pltpu.CompilerParams(vmem_limit_bytes=VMEM_LIMIT),
        cost_estimate=pl.CostEstimate(flops=flops, bytes_accessed=moved, transcendentals=0),
        name=name,
    )(*operands)


def on_device(
    history_rows,
    cotangent,
    dest_device,
    source_device,
    source_offset,
    segments,
    row_valid,
    joined_weight,
    output_weight,
):
    shape = jax.ShapeDtypeStruct
    xs, zs, ys = lax.axis_size("x"), lax.axis_size("z"), lax.axis_size("y")
    lanes = ys * lax.axis_size("c")
    rows, width = history_rows.shape
    blocks = dest_device.shape[1]
    core = lax.axis_index("c").astype(jnp.int32).reshape(1)
    scaling = 1.0 / math.sqrt(rows * lanes * xs * zs)

    def exchange(block):
        chunks = block.reshape(lanes, rows // lanes, block.shape[1])
        return lax.all_to_all(chunks, ("y", "c"), 0, 0, tiled=True).reshape(block.shape)

    square = 2 * rows * rows * width
    (packed,) = call(
        functools.partial(pack_kernel, lanes),
        "pack",
        [shape((rows, 2 * width + 128), bf16)],
        (dest_device, history_rows, cotangent),
        2 * square,
        1,
    )
    routed, route = call(
        functools.partial(route_kernel, lanes),
        "route",
        [shape((rows, 2 * width), bf16), shape((rows, rows), bf16)],
        (exchange(packed),),
        2 * square,
    )
    slots = rows // WIN * HEADS // 2
    total = width * 5
    vmem = pltpu.VMEM
    leaving, keep, send = call(
        functools.partial(layer_kernel, lanes, (xs, ys)),
        "layer",
        [shape((rows, width), bf16), shape((width // 2, total), bf16), shape((width // 2, total), bf16)],
        (
            core,
            source_device,
            source_offset,
            exchange(routed),
            segments,
            row_valid,
            joined_weight,
            output_weight,
        ),
        2 * rows * width * width * 18,
        3,
        (
            vmem((rows, rows), bf16),
            vmem((rows, width), bf16),
            vmem((rows, width), bf16),
            vmem((rows, width), bf16),
            vmem((rows, 1), f32),
            vmem((rows, 4 * width), bf16),
            vmem((rows, 4 * width), bf16),
            vmem((slots, WIN, 2 * WIN), bf16),
            vmem((slots, WIN, 2 * WIN), bf16),
            vmem((rows, width), f32),
            vmem((rows, 1), f32),
            vmem((rows, width), bf16),
            vmem((rows, 4 * width), bf16),
        ),
    )
    arrived = lax.ppermute(send, "c", [(0, 1), (1, 0)])
    summed = (keep.astype(f32) + arrived.astype(f32)).astype(bf16)
    summed, leaving = lax.optimization_barrier((summed, leaving))
    partial = lax.psum_scatter(summed, "x", scatter_dimension=0, tiled=True)

    (returning,) = call(
        return_kernel, "back", [shape((rows, width), bf16)], (route, exchange(leaving)), square
    )
    (row_grad,) = call(
        functools.partial(unpack_kernel, lanes, blocks),
        "unpack",
        [shape((rows, width), bf16)],
        (exchange(returning),),
        square,
    )

    own = width // (lanes * xs)
    piece = -(-total // (zs * 128)) * 128
    (pieces,) = call(
        split_kernel, "split", [shape((ys, zs, own, piece), bf16)], (partial.reshape(ys, own, total),)
    )
    pieces = lax.all_to_all(pieces.reshape(ys * zs, own, piece), ("y", "z"), 0, 0, tiled=True)
    (spread,) = call(
        functools.partial(total_kernel, scaling), "total", [shape((xs * zs, own, piece), bf16)], (pieces,)
    )
    spread = lax.all_to_all(spread, ("x", "z"), 0, 0, tiled=True)
    joined_grad, output_grad = call(
        result_kernel,
        "result",
        [shape((width // lanes, 4 * width), f32), shape((width // lanes, width), f32)],
        (spread.reshape(xs, zs, own, piece),),
    )
    return (row_grad, joined_grad, output_grad)


def solution(mesh):
    torus = Mesh(mesh.devices.reshape(4, 12, 8, 2), ("x", "z", "y", "c"))
    everywhere = P(("x", "z", "y", "c"), None)
    return jax.shard_map(
        on_device,
        mesh=torus,
        in_specs=(everywhere,) * 7 + (P(), P()),
        out_specs=(everywhere, P(("y", "c"), None), P(("y", "c"), None)),
        check_vma=False,
    )
```

```python
import functools
import math

import jax
import jax.numpy as jnp
from jax import lax
from jax.experimental import pallas as pl
from jax.experimental.pallas import tpu as pltpu
from jax.sharding import Mesh, PartitionSpec as P

HEADS = 8
WIN = 128
epsilon = 1e-05
f32 = jnp.float32
bf16 = jnp.bfloat16
VMEM_LIMIT = 48 * 1024 * 1024
VMEM_MOST = 62 * 1024 * 1024
NT = (((1,), (1,)), ((), ()))
TN = (((0,), (0,)), ((), ()))


def dot(a, b, dims=(((1,), (0,)), ((), ()))):
    return lax.dot_general(a, b, dims, preferred_element_type=f32)


def row_norm(features):
    centred = features - jnp.mean(features, axis=-1, keepdims=True)
    spread = jnp.mean(centred * centred, axis=-1, keepdims=True)
    inverse = lax.rsqrt(spread + epsilon)
    return centred * inverse, inverse


def row_norm_back(cot, normed, inverse):
    mean_cot = jnp.mean(cot, axis=-1, keepdims=True)
    mean_both = jnp.mean(cot * normed, axis=-1, keepdims=True)
    return inverse * (cot - mean_cot - normed * mean_both)


def as_column(row, diagonal):
    return jnp.sum(jnp.where(diagonal, row, 0.0), axis=1, keepdims=True)


def forward_body(
    rows_ref,
    seg_ref,
    valid_ref,
    weight_ref,
    normed_ref,
    inverse_ref,
    active_ref,
    slope_ref,
    weighting_ref,
    score_slope_ref,
    mixed_ref,
    mix_inverse_ref,
    gated_ref,
):
    rows, width = rows_ref.shape
    head = width // HEADS
    pair = 2 * head
    normed, inverse = row_norm(rows_ref[...].astype(f32))
    normed = normed.astype(bf16)
    normed_ref[...] = normed
    inverse_ref[...] = inverse
    for quarter in range(4):
        columns = slice(quarter * width, (quarter + 1) * width)
        projected = dot(normed, weight_ref[:, columns])
        gate = jax.nn.sigmoid(projected)
        active_ref[:, columns] = (projected * gate).astype(bf16)
        slope_ref[:, columns] = (gate * (1.0 + projected * (1.0 - gate))).astype(bf16)
    left = lax.broadcasted_iota(jnp.int32, (WIN, pair), 1) < head
    place_i = lax.broadcasted_iota(jnp.int32, (WIN, WIN), 0)
    place_j = lax.broadcasted_iota(jnp.int32, (WIN, WIN), 1)
    zero = jnp.zeros((), bf16)

    def stacked(block):
        return jnp.concatenate([jnp.where(left, block, zero), jnp.where(left, zero, block)], axis=0)

    for window in range(rows // WIN):
        span = slice(window * WIN, (window + 1) * WIN)
        seg_row = seg_ref[:, span].astype(f32)
        seg_col = as_column(seg_row, place_i == place_j)
        allowed = (seg_col == seg_row) & (place_j <= place_i) & (valid_ref[:, span] == 1)
        allowed = jnp.where(allowed, 1.0, 0.0)
        weights = allowed / jnp.maximum(jnp.sum(allowed, axis=1, keepdims=True), 1.0)
        weights = jnp.concatenate([weights, weights], axis=1)
        mixture = []
        for p in range(HEADS // 2):
            at = p * pair
            value = active_ref[span, width + at : width + at + pair]
            query = active_ref[span, 2 * width + at : 2 * width + at + pair]
            key = active_ref[span, 3 * width + at : 3 * width + at + pair]
            scores = dot(query, stacked(key), NT) * head**-0.5
            gate = jax.nn.sigmoid(scores)
            weighting = (scores * gate * weights).astype(bf16)
            slot = window * (HEADS // 2) + p
            weighting_ref[slot] = weighting
            score_slope_ref[slot] = (
                gate * (1.0 + scores * (1.0 - gate)) * (weights * head**-0.5)
            ).astype(bf16)
            mixture.append(dot(weighting, stacked(value)))
        mixed, mix_inverse = row_norm(jnp.concatenate(mixture, axis=1))
        mixed_ref[span, :] = mixed
        mix_inverse_ref[span, :] = mix_inverse
        gated_ref[span, :] = (mixed * active_ref[span, :width].astype(f32)).astype(bf16)


def backward_body(
    rows_ref,
    cot_ref,
    valid_ref,
    weight_ref,
    out_weight_ref,
    normed_ref,
    inverse_ref,
    active_ref,
    slope_ref,
    weighting_ref,
    score_slope_ref,
    mixed_ref,
    mix_inverse_ref,
    gated_ref,
    proj_cot_ref,
    spread,
    keep_ref,
    send_ref,
):
    rows, width = rows_ref.shape
    head = width // HEADS
    pair = 2 * head
    place_i = lax.broadcasted_iota(jnp.int32, (rows, rows), 0)
    place_j = lax.broadcasted_iota(jnp.int32, (rows, rows), 1)
    valid_col = as_column(valid_ref[...].astype(f32), place_i == place_j)
    masked_f = cot_ref[...].astype(f32) * valid_col
    masked = masked_f.astype(bf16)
    side = width // 2

    def put_grad(factor, cot, at):
        grad = dot(factor, cot).astype(bf16)
        keep_ref[:, at : at + width] = grad[:side]
        send_ref[:, at : at + width] = grad[side:]

    put_grad(permute(spread, gated_ref[...], NT), masked, 4 * width)
    gated_cot = dot(masked, out_weight_ref[...], NT)
    mixed = mixed_ref[...]
    gate_cot = (gated_cot * mixed).astype(bf16).astype(f32)
    proj_cot_ref[:, :width] = (gate_cot * slope_ref[:, :width].astype(f32)).astype(bf16)
    mixture_cot = row_norm_back(
        gated_cot * active_ref[:, :width].astype(f32), mixed, mix_inverse_ref[...]
    ).astype(bf16)
    left = lax.broadcasted_iota(jnp.int32, (WIN, pair), 1) < head
    zero = jnp.zeros((), bf16)

    def stacked(block):
        return jnp.concatenate([jnp.where(left, block, zero), jnp.where(left, zero, block)], axis=0)

    def folded(block):
        return jnp.where(left, block[:WIN], block[WIN:])

    for window in range(rows // WIN):
        span = slice(window * WIN, (window + 1) * WIN)
        for p in range(HEADS // 2):
            at = p * pair
            slot = window * (HEADS // 2) + p

            def put(quarter, cot):
                columns = slice(quarter * width + at, quarter * width + at + pair)
                slope = slope_ref[span, columns].astype(f32)
                proj_cot_ref[span, columns] = (cot.astype(bf16).astype(f32) * slope).astype(bf16)

            value = active_ref[span, width + at : width + at + pair]
            query = active_ref[span, 2 * width + at : 2 * width + at + pair]
            key = active_ref[span, 3 * width + at : 3 * width + at + pair]
            mix_cot = mixture_cot[span, at : at + pair]
            put(1, folded(dot(weighting_ref[slot], mix_cot, TN)))
            weighting_cot = dot(mix_cot, stacked(value), NT).astype(bf16).astype(f32)
            score_cot = (weighting_cot * score_slope_ref[slot].astype(f32)).astype(bf16)
            put(2, dot(score_cot, stacked(key)))
            put(3, folded(dot(score_cot, query, TN)))
    normed_t = permute(spread, normed_ref[...], NT)
    normed_cot = jnp.zeros((rows, width), f32)
    for quarter in range(4):
        columns = slice(quarter * width, (quarter + 1) * width)
        proj_cot = proj_cot_ref[:, columns]
        put_grad(normed_t, proj_cot, quarter * width)
        normed_cot += dot(proj_cot, weight_ref[:, columns], NT)
    features = rows_ref[...].astype(f32)
    inverse = inverse_ref[...]
    normed_f = (features - jnp.mean(features, axis=-1, keepdims=True)) * inverse
    rows_cot = row_norm_back(normed_cot, normed_f, inverse)
    return (masked_f + rows_cot).astype(bf16)


def permute(order, block, dims=(((1,), (0,)), ((), ()))):
    return dot(order, block, dims).astype(bf16)


def pack_kernel(lanes, dest_ref, rows_hbm, cot_hbm, out_ref, rows_ref, cot_ref, sems):
    copies = [
        pltpu.make_async_copy(rows_hbm, rows_ref, sems.at[0]),
        pltpu.make_async_copy(cot_hbm, cot_ref, sems.at[1]),
    ]
    for copy in copies:
        copy.start()
    rows, width = rows_ref.shape
    blocks = dest_ref.shape[1]
    chunk = rows // lanes
    half = chunk // blocks
    place = lax.broadcasted_iota(jnp.int32, (rows, rows), 0)
    loaded = lax.broadcasted_iota(jnp.int32, (rows, rows), 1)
    source = place % blocks * (rows // blocks) + place // blocks % half * lanes + place // chunk
    order = jnp.where(source == loaded, 1.0, 0.0).astype(bf16)
    extra = out_ref.shape[1] - 2 * width
    block = lax.broadcasted_iota(jnp.int32, (rows, extra), 0) % blocks
    dest = jnp.zeros((rows, extra), f32)
    for j in range(blocks):
        dest = jnp.where(block == j, dest_ref[0, j].astype(f32), dest)
    out_ref[:, 2 * width :] = dest.astype(bf16)
    copies[0].wait()
    out_ref[:, :width] = permute(order, rows_ref[...])
    copies[1].wait()
    out_ref[:, width : 2 * width] = permute(order, cot_ref[...])


def route_kernel(lanes, in_ref, out_ref, order_ref):
    rows, double = out_ref.shape
    chunk = rows // lanes
    blocks = chunk // 2
    extra = in_ref.shape[1] - double
    place = lax.broadcasted_iota(jnp.int32, (rows, rows), 0)
    other = lax.broadcasted_iota(jnp.int32, (rows, rows), 1)
    lane = lax.broadcasted_iota(jnp.int32, (rows, extra), 1)
    dest = in_ref[:, double:].astype(f32)
    chosen = jnp.where(dest == lane.astype(f32), 1.0, 0.0)
    same_half = place // blocks % 2 == other // blocks % 2
    earlier = jnp.where(same_half & (other < place), 1.0, 0.0).astype(bf16)
    rank = jnp.sum(dot(earlier, chosen.astype(bf16)) * chosen, axis=1, keepdims=True)
    row = lax.broadcasted_iota(jnp.int32, (rows, 1), 0)
    target = dest[:, :1] * chunk + (row // blocks % 2 * blocks).astype(f32) + rank
    order = jnp.where(target == other.astype(f32), 1.0, 0.0).astype(bf16)
    order_ref[...] = order
    out_ref[...] = permute(order, in_ref[:, :double], TN)


def gather_order(lanes, sources_ref, offsets_ref, order_ref):
    rows = order_ref.shape[0]
    blocks = sources_ref.shape[1]
    chunk = rows // lanes
    half = chunk // blocks
    span = rows // blocks
    inside = lax.broadcasted_iota(jnp.int32, (span, rows), 0)
    column = lax.broadcasted_iota(jnp.int32, (span, rows), 1)
    base = inside % lanes * chunk + inside // lanes % half * blocks
    keys = [sources_ref[0, t] * 2 + offsets_ref[0, t] for t in range(blocks)]
    for t in range(blocks):
        slot = sum(jnp.where(keys[u] < keys[t], 1, 0) for u in range(blocks) if u != t)
        order = jnp.where(column == base + slot, 1.0, 0.0)
        order_ref[t * span : (t + 1) * span, :] = order.astype(bf16)


def spread_order(parts, core, width):
    xs, ys = parts
    out = lax.broadcasted_iota(jnp.int32, (width, width), 0)
    column = lax.broadcasted_iota(jnp.int32, (width, width), 1)
    side = width // 2
    block = width // ys // 2
    piece = block // xs
    y = out // piece % ys
    x = out % side // (piece * ys)
    parity = (out // side + core) % 2
    source = y * (2 * block) + parity * block + x * piece + out % piece
    return jnp.where(source == column, 1.0, 0.0).astype(bf16)


def layer_kernel(
    lanes,
    parts,
    core_ref,
    sources_ref,
    offsets_ref,
    in_ref,
    seg_ref,
    valid_ref,
    weight_ref,
    out_weight_ref,
    leave_ref,
    keep_ref,
    send_ref,
    order_ref,
    rows_ref,
    cot_ref,
    normed_ref,
    inverse_ref,
    active_ref,
    slope_ref,
    weighting_ref,
    score_slope_ref,
    mixed_ref,
    mix_inverse_ref,
    gated_ref,
    proj_cot_ref,
):
    rows, width = rows_ref.shape
    gather_order(lanes, sources_ref, offsets_ref, order_ref)
    rows_ref[...] = permute(order_ref[...], in_ref[:, :width])
    cot_ref[...] = permute(order_ref[...], in_ref[:, width:])
    stored = (
        normed_ref,
        inverse_ref,
        active_ref,
        slope_ref,
        weighting_ref,
        score_slope_ref,
        mixed_ref,
        mix_inverse_ref,
        gated_ref,
    )
    forward_body(rows_ref, seg_ref, valid_ref, weight_ref, *stored)
    spread = spread_order(parts, core_ref[0], width)
    work_grad = backward_body(
        rows_ref,
        cot_ref,
        valid_ref,
        weight_ref,
        out_weight_ref,
        *stored,
        proj_cot_ref,
        spread,
        keep_ref,
        send_ref,
    )
    leave_ref[...] = permute(order_ref[...], work_grad, TN)


def return_kernel(order_ref, in_ref, out_ref):
    out_ref[...] = permute(order_ref[...], in_ref[...])


def unpack_kernel(lanes, blocks, in_ref, partial_ref, out_ref, same_partial_ref):
    del partial_ref, same_partial_ref
    rows = in_ref.shape[0]
    chunk = rows // lanes
    half = chunk // blocks
    loaded = lax.broadcasted_iota(jnp.int32, (rows, rows), 0)
    place = lax.broadcasted_iota(jnp.int32, (rows, rows), 1)
    source = place % blocks * (rows // blocks) + place // blocks % half * lanes + place // chunk
    order = jnp.where(source == loaded, 1.0, 0.0).astype(bf16)
    out_ref[...] = permute(order, in_ref[...])


def fold_kernel(in_ref, out_ref):
    pieces, _, piece = out_ref.shape
    total = in_ref.shape[2]
    folded = jnp.sum(in_ref[...].astype(f32), axis=0).astype(bf16)
    for k in range(pieces):
        at, end = k * piece, min((k + 1) * piece, total)
        if at < total:
            out_ref[k, :, : end - at] = folded[:, at:end]
        if end - at < piece:
            rest = max(end - at, 0)
            out_ref[k, :, rest:] = jnp.zeros((out_ref.shape[1], piece - rest), bf16)


def total_kernel(scaling, in_ref, out_ref):
    total = jnp.sum(in_ref[...].astype(f32), axis=0, keepdims=True) * scaling
    out_ref[...] = jnp.broadcast_to(total.astype(bf16), out_ref.shape)


def result_kernel(in_ref, joined_ref, output_ref):
    xs, zs, piece_rows, piece = in_ref.shape
    split = joined_ref.shape[1]
    step = math.gcd(piece, split)
    for x in range(xs):
        span = slice(x * piece_rows, (x + 1) * piece_rows)
        for at in range(0, split + output_ref.shape[1], step):
            block = in_ref[x, at // piece, :, at % piece : at % piece + step].astype(f32)
            if at < split:
                joined_ref[span, at : at + step] = block
            else:
                output_ref[span, at - split : at - split + step] = block


def call(kernel, name, out_shape, operands, flops=0, scalars=0, scratch=(), unmoved=0, aliases=None):
    moved = sum(math.prod(a.shape) * a.dtype.itemsize for a in (*operands, *out_shape))
    smem = pl.BlockSpec(memory_space=pltpu.SMEM)
    vmem = pl.BlockSpec(memory_space=pltpu.VMEM)
    stay = pl.BlockSpec(memory_space=pl.ANY)
    aliases = aliases or {}
    blocked = len(operands) - scalars - unmoved
    return pl.pallas_call(
        kernel,
        out_shape=tuple(out_shape),
        in_specs=[smem] * scalars + [vmem] * blocked + [stay] * unmoved,
        out_specs=tuple(stay if k in aliases.values() else vmem for k in range(len(out_shape))),
        input_output_aliases=aliases,
        scratch_shapes=list(scratch),
        compiler_params=pltpu.CompilerParams(vmem_limit_bytes=VMEM_MOST if unmoved else VMEM_LIMIT),
        cost_estimate=pl.CostEstimate(flops=flops, bytes_accessed=moved, transcendentals=0),
        name=name,
    )(*operands)


def on_device(
    history_rows,
    cotangent,
    dest_device,
    source_device,
    source_offset,
    segments,
    row_valid,
    joined_weight,
    output_weight,
):
    shape = jax.ShapeDtypeStruct
    xs, zs, ys = lax.axis_size("x"), lax.axis_size("z"), lax.axis_size("y")
    lanes = ys * lax.axis_size("c")
    rows, width = history_rows.shape
    blocks = dest_device.shape[1]
    core = lax.axis_index("c").astype(jnp.int32).reshape(1)
    scaling = 1.0 / math.sqrt(rows * lanes * xs * zs)

    def exchange(block):
        chunks = block.reshape(lanes, rows // lanes, block.shape[1])
        return lax.all_to_all(chunks, ("y", "c"), 0, 0, tiled=True).reshape(block.shape)

    square = 2 * rows * rows * width
    (packed,) = call(
        functools.partial(pack_kernel, lanes),
        "pack",
        [shape((rows, 2 * width + 128), bf16)],
        (dest_device, history_rows, cotangent),
        2 * square,
        1,
        (
            pltpu.VMEM((rows, width), bf16),
            pltpu.VMEM((rows, width), bf16),
            pltpu.SemaphoreType.DMA((2,)),
        ),
        2,
    )
    routed, route = call(
        functools.partial(route_kernel, lanes),
        "route",
        [shape((rows, 2 * width), bf16), shape((rows, rows), bf16)],
        (exchange(packed),),
        2 * square,
    )
    slots = rows // WIN * HEADS // 2
    total = width * 5
    vmem = pltpu.VMEM
    leaving, keep, send = call(
        functools.partial(layer_kernel, lanes, (xs, ys)),
        "layer",
        [shape((rows, width), bf16), shape((width // 2, total), bf16), shape((width // 2, total), bf16)],
        (
            core,
            source_device,
            source_offset,
            exchange(routed),
            segments,
            row_valid,
            joined_weight,
            output_weight,
        ),
        2 * rows * width * width * 18,
        3,
        (
            vmem((rows, rows), bf16),
            vmem((rows, width), bf16),
            vmem((rows, width), bf16),
            vmem((rows, width), bf16),
            vmem((rows, 1), f32),
            vmem((rows, 4 * width), bf16),
            vmem((rows, 4 * width), bf16),
            vmem((slots, WIN, 2 * WIN), bf16),
            vmem((slots, WIN, 2 * WIN), bf16),
            vmem((rows, width), f32),
            vmem((rows, 1), f32),
            vmem((rows, width), bf16),
            vmem((rows, 4 * width), bf16),
        ),
    )
    arrived = lax.ppermute(send, "c", [(0, 1), (1, 0)])
    summed = (keep.astype(f32) + arrived.astype(f32)).astype(bf16)
    summed, leaving = lax.optimization_barrier((summed, leaving))
    partial = lax.psum_scatter(summed, "x", scatter_dimension=0, tiled=True)

    (returning,) = call(
        return_kernel, "back", [shape((rows, width), bf16)], (route, exchange(leaving)), square
    )
    row_grad, partial = call(
        functools.partial(unpack_kernel, lanes, blocks),
        "unpack",
        [shape((rows, width), bf16), shape(partial.shape, bf16)],
        (exchange(returning), partial),
        square,
        unmoved=1,
        aliases={1: 1},
    )

    own = width // (lanes * xs)
    piece = -(-total // (zs * 128)) * 128
    partial = lax.all_to_all(partial.reshape(ys, own, total), "y", 0, 0, tiled=True)
    (pieces,) = call(fold_kernel, "fold", [shape((zs, own, piece), bf16)], (partial,))
    pieces = lax.all_to_all(pieces, "z", 0, 0, tiled=True)
    (spread,) = call(
        functools.partial(total_kernel, scaling), "total", [shape((xs * zs, own, piece), bf16)], (pieces,)
    )
    spread = lax.all_to_all(spread, ("x", "z"), 0, 0, tiled=True)
    joined_grad, output_grad = call(
        result_kernel,
        "result",
        [shape((width // lanes, 4 * width), f32), shape((width // lanes, width), f32)],
        (spread.reshape(xs, zs, own, piece),),
    )
    return (row_grad, joined_grad, output_grad)


def solution(mesh):
    torus = Mesh(mesh.devices.reshape(4, 12, 8, 2), ("x", "z", "y", "c"))
    everywhere = P(("x", "z", "y", "c"), None)
    return jax.shard_map(
        on_device,
        mesh=torus,
        in_specs=(everywhere,) * 7 + (P(), P()),
        out_specs=(everywhere, P(("y", "c"), None), P(("y", "c"), None)),
        check_vma=False,
    )
```

```python
import functools
import math

import jax
import jax.numpy as jnp
from jax import lax
from jax.experimental import pallas as pl
from jax.experimental.pallas import tpu as pltpu
from jax.sharding import Mesh, PartitionSpec as P

HEADS = 8
WIN = 128
epsilon = 1e-05
f32 = jnp.float32
bf16 = jnp.bfloat16
VMEM_LIMIT = 48 * 1024 * 1024
VMEM_MOST = 62 * 1024 * 1024
NT = (((1,), (1,)), ((), ()))
TN = (((0,), (0,)), ((), ()))


def dot(a, b, dims=(((1,), (0,)), ((), ()))):
    return lax.dot_general(a, b, dims, preferred_element_type=f32)


def row_norm(features):
    centred = features - jnp.mean(features, axis=-1, keepdims=True)
    spread = jnp.mean(centred * centred, axis=-1, keepdims=True)
    inverse = lax.rsqrt(spread + epsilon)
    return centred * inverse, inverse


def row_norm_back(cot, normed, inverse):
    mean_cot = jnp.mean(cot, axis=-1, keepdims=True)
    mean_both = jnp.mean(cot * normed, axis=-1, keepdims=True)
    return inverse * (cot - mean_cot - normed * mean_both)


def as_column(row, diagonal):
    return jnp.sum(jnp.where(diagonal, row, 0.0), axis=1, keepdims=True)


def forward_body(
    rows_ref,
    seg_ref,
    valid_ref,
    weight_ref,
    normed_ref,
    inverse_ref,
    active_ref,
    slope_ref,
    weighting_ref,
    score_slope_ref,
    mixed_ref,
    mix_inverse_ref,
    gated_ref,
):
    rows, width = rows_ref.shape
    head = width // HEADS
    pair = 2 * head
    normed, inverse = row_norm(rows_ref[...].astype(f32))
    normed = normed.astype(bf16)
    normed_ref[...] = normed
    inverse_ref[...] = inverse
    for quarter in range(4):
        columns = slice(quarter * width, (quarter + 1) * width)
        projected = dot(normed, weight_ref[:, columns])
        gate = jax.nn.sigmoid(projected)
        active_ref[:, columns] = (projected * gate).astype(bf16)
        slope_ref[:, columns] = (gate * (1.0 + projected * (1.0 - gate))).astype(bf16)
    left = lax.broadcasted_iota(jnp.int32, (WIN, pair), 1) < head
    place_i = lax.broadcasted_iota(jnp.int32, (WIN, WIN), 0)
    place_j = lax.broadcasted_iota(jnp.int32, (WIN, WIN), 1)
    zero = jnp.zeros((), bf16)

    def stacked(block):
        return jnp.concatenate([jnp.where(left, block, zero), jnp.where(left, zero, block)], axis=0)

    for window in range(rows // WIN):
        span = slice(window * WIN, (window + 1) * WIN)
        seg_row = seg_ref[:, span].astype(f32)
        seg_col = as_column(seg_row, place_i == place_j)
        allowed = (seg_col == seg_row) & (place_j <= place_i) & (valid_ref[:, span] == 1)
        allowed = jnp.where(allowed, 1.0, 0.0)
        weights = allowed / jnp.maximum(jnp.sum(allowed, axis=1, keepdims=True), 1.0)
        weights = jnp.concatenate([weights, weights], axis=1)
        mixture = []
        for p in range(HEADS // 2):
            at = p * pair
            value = active_ref[span, width + at : width + at + pair]
            query = active_ref[span, 2 * width + at : 2 * width + at + pair]
            key = active_ref[span, 3 * width + at : 3 * width + at + pair]
            scores = dot(query, stacked(key), NT) * head**-0.5
            gate = jax.nn.sigmoid(scores)
            weighting = (scores * gate * weights).astype(bf16)
            slot = window * (HEADS // 2) + p
            weighting_ref[slot] = weighting
            score_slope_ref[slot] = (
                gate * (1.0 + scores * (1.0 - gate)) * (weights * head**-0.5)
            ).astype(bf16)
            mixture.append(dot(weighting, stacked(value)))
        mixed, mix_inverse = row_norm(jnp.concatenate(mixture, axis=1))
        mixed_ref[span, :] = mixed
        mix_inverse_ref[span, :] = mix_inverse
        gated_ref[span, :] = (mixed * active_ref[span, :width].astype(f32)).astype(bf16)


def backward_body(
    rows_ref,
    cot_ref,
    valid_ref,
    weight_ref,
    out_weight_ref,
    normed_ref,
    inverse_ref,
    active_ref,
    slope_ref,
    weighting_ref,
    score_slope_ref,
    mixed_ref,
    mix_inverse_ref,
    gated_ref,
    proj_cot_ref,
    spread,
    keep_ref,
    send_ref,
):
    rows, width = rows_ref.shape
    head = width // HEADS
    pair = 2 * head
    place_i = lax.broadcasted_iota(jnp.int32, (rows, rows), 0)
    place_j = lax.broadcasted_iota(jnp.int32, (rows, rows), 1)
    valid_col = as_column(valid_ref[...].astype(f32), place_i == place_j)
    masked_f = cot_ref[...].astype(f32) * valid_col
    masked = masked_f.astype(bf16)
    side = width // 2

    def put_grad(factor, cot, at):
        grad = dot(factor, cot).astype(bf16)
        keep_ref[:, at : at + width] = grad[:side]
        send_ref[:, at : at + width] = grad[side:]

    put_grad(permute(spread, gated_ref[...], NT), masked, 4 * width)
    gated_cot = dot(masked, out_weight_ref[...], NT)
    mixed = mixed_ref[...]
    gate_cot = (gated_cot * mixed).astype(bf16).astype(f32)
    proj_cot_ref[:, :width] = (gate_cot * slope_ref[:, :width].astype(f32)).astype(bf16)
    mixture_cot = row_norm_back(
        gated_cot * active_ref[:, :width].astype(f32), mixed, mix_inverse_ref[...]
    ).astype(bf16)
    left = lax.broadcasted_iota(jnp.int32, (WIN, pair), 1) < head
    zero = jnp.zeros((), bf16)

    def stacked(block):
        return jnp.concatenate([jnp.where(left, block, zero), jnp.where(left, zero, block)], axis=0)

    def folded(block):
        return jnp.where(left, block[:WIN], block[WIN:])

    for window in range(rows // WIN):
        span = slice(window * WIN, (window + 1) * WIN)
        for p in range(HEADS // 2):
            at = p * pair
            slot = window * (HEADS // 2) + p

            def put(quarter, cot):
                columns = slice(quarter * width + at, quarter * width + at + pair)
                slope = slope_ref[span, columns].astype(f32)
                proj_cot_ref[span, columns] = (cot.astype(bf16).astype(f32) * slope).astype(bf16)

            value = active_ref[span, width + at : width + at + pair]
            query = active_ref[span, 2 * width + at : 2 * width + at + pair]
            key = active_ref[span, 3 * width + at : 3 * width + at + pair]
            mix_cot = mixture_cot[span, at : at + pair]
            put(1, folded(dot(weighting_ref[slot], mix_cot, TN)))
            weighting_cot = dot(mix_cot, stacked(value), NT).astype(bf16).astype(f32)
            score_cot = (weighting_cot * score_slope_ref[slot].astype(f32)).astype(bf16)
            put(2, dot(score_cot, stacked(key)))
            put(3, folded(dot(score_cot, query, TN)))
    normed_t = permute(spread, normed_ref[...], NT)
    normed_cot = jnp.zeros((rows, width), f32)
    for quarter in range(4):
        columns = slice(quarter * width, (quarter + 1) * width)
        proj_cot = proj_cot_ref[:, columns]
        put_grad(normed_t, proj_cot, quarter * width)
        normed_cot += dot(proj_cot, weight_ref[:, columns], NT)
    features = rows_ref[...].astype(f32)
    inverse = inverse_ref[...]
    normed_f = (features - jnp.mean(features, axis=-1, keepdims=True)) * inverse
    rows_cot = row_norm_back(normed_cot, normed_f, inverse)
    return (masked_f + rows_cot).astype(bf16)


def permute(order, block, dims=(((1,), (0,)), ((), ()))):
    return dot(order, block, dims).astype(bf16)


def pack_kernel(lanes, dest_ref, rows_hbm, cot_hbm, out_ref, rows_ref, cot_ref, sems):
    copies = [
        pltpu.make_async_copy(rows_hbm, rows_ref, sems.at[0]),
        pltpu.make_async_copy(cot_hbm, cot_ref, sems.at[1]),
    ]
    for copy in copies:
        copy.start()
    rows, width = rows_ref.shape
    blocks = dest_ref.shape[1]
    chunk = rows // lanes
    half = chunk // blocks
    place = lax.broadcasted_iota(jnp.int32, (rows, rows), 0)
    loaded = lax.broadcasted_iota(jnp.int32, (rows, rows), 1)
    source = place % blocks * (rows // blocks) + place // blocks % half * lanes + place // chunk
    order = jnp.where(source == loaded, 1.0, 0.0).astype(bf16)
    extra = out_ref.shape[1] - 2 * width
    block = lax.broadcasted_iota(jnp.int32, (rows, extra), 0) % blocks
    dest = jnp.zeros((rows, extra), f32)
    for j in range(blocks):
        dest = jnp.where(block == j, dest_ref[0, j].astype(f32), dest)
    out_ref[:, 2 * width :] = dest.astype(bf16)
    copies[0].wait()
    out_ref[:, :width] = permute(order, rows_ref[...])
    copies[1].wait()
    out_ref[:, width : 2 * width] = permute(order, cot_ref[...])


def route_kernel(lanes, me_ref, in_ref, out_ref, places_ref, rank_ref):
    rows, double = out_ref.shape
    chunk = rows // lanes
    blocks = chunk // 2
    extra = in_ref.shape[1] - double
    place = lax.broadcasted_iota(jnp.int32, (rows, rows), 0)
    other = lax.broadcasted_iota(jnp.int32, (rows, rows), 1)
    lane = lax.broadcasted_iota(jnp.int32, (rows, extra), 1)
    dest = in_ref[:, double:].astype(f32)
    chosen = jnp.where(dest == lane.astype(f32), 1.0, 0.0)
    same_half = place // blocks % 2 == other // blocks % 2
    earlier = jnp.where(same_half & (other < place), 1.0, 0.0).astype(bf16)
    rank = jnp.sum(dot(earlier, chosen.astype(bf16)) * chosen, axis=1, keepdims=True)
    row = lax.broadcasted_iota(jnp.int32, (rows, 1), 0)
    target = dest[:, :1] * chunk + (row // blocks % 2 * blocks).astype(f32) + rank
    order = jnp.where(target == other.astype(f32), 1.0, 0.0).astype(bf16)
    out_ref[...] = permute(order, in_ref[:, :double], TN)
    rank_ref[...] = jnp.broadcast_to(rank, rank_ref.shape)
    own = pl.multiple_of(me_ref[0] * chunk, chunk)
    places_ref[...] = rank_ref[pl.ds(own, blocks), :].astype(jnp.int32)


def gather_order(lanes, sources_ref, offsets_ref, order_ref):
    rows = order_ref.shape[0]
    blocks = sources_ref.shape[1]
    chunk = rows // lanes
    half = chunk // blocks
    span = rows // blocks
    inside = lax.broadcasted_iota(jnp.int32, (span, rows), 0)
    column = lax.broadcasted_iota(jnp.int32, (span, rows), 1)
    base = inside % lanes * chunk + inside // lanes % half * blocks
    keys = [sources_ref[0, t] * 2 + offsets_ref[0, t] for t in range(blocks)]
    slots = []
    for t in range(blocks):
        slot = sum(jnp.where(keys[u] < keys[t], 1, 0) for u in range(blocks) if u != t)
        order = jnp.where(column == base + slot, 1.0, 0.0)
        order_ref[t * span : (t + 1) * span, :] = order.astype(bf16)
        slots.append(slot)
    return slots


def spread_order(parts, core, width):
    xs, ys = parts
    out = lax.broadcasted_iota(jnp.int32, (width, width), 0)
    column = lax.broadcasted_iota(jnp.int32, (width, width), 1)
    side = width // 2
    block = width // ys // 2
    piece = block // xs
    y = out // piece % ys
    x = out % side // (piece * ys)
    parity = (out // side + core) % 2
    source = y * (2 * block) + parity * block + x * piece + out % piece
    return jnp.where(source == column, 1.0, 0.0).astype(bf16)


def layer_kernel(
    lanes,
    parts,
    me_ref,
    sources_ref,
    offsets_ref,
    in_ref,
    seg_ref,
    valid_ref,
    weight_ref,
    out_weight_ref,
    leave_ref,
    keep_ref,
    send_ref,
    order_ref,
    rows_ref,
    cot_ref,
    normed_ref,
    inverse_ref,
    active_ref,
    slope_ref,
    weighting_ref,
    score_slope_ref,
    mixed_ref,
    mix_inverse_ref,
    gated_ref,
    proj_cot_ref,
):
    rows, width = rows_ref.shape
    slots = gather_order(lanes, sources_ref, offsets_ref, order_ref)
    rows_ref[...] = permute(order_ref[...], in_ref[:, :width])
    cot_ref[...] = permute(order_ref[...], in_ref[:, width:])
    stored = (
        normed_ref,
        inverse_ref,
        active_ref,
        slope_ref,
        weighting_ref,
        score_slope_ref,
        mixed_ref,
        mix_inverse_ref,
        gated_ref,
    )
    forward_body(rows_ref, seg_ref, valid_ref, weight_ref, *stored)
    spread = spread_order(parts, me_ref[0] % 2, width)
    work_grad = backward_body(
        rows_ref,
        cot_ref,
        valid_ref,
        weight_ref,
        out_weight_ref,
        *stored,
        proj_cot_ref,
        spread,
        keep_ref,
        send_ref,
    )
    span = rows // len(slots)
    for t, slot in enumerate(slots):
        at = pl.multiple_of(slot * span, span)
        leave_ref[pl.ds(at, span), :] = work_grad[t * span : (t + 1) * span]


def collect_kernel(block_rows, dest_ref, places_ref, in_ref, out_ref, sems):
    blocks = dest_ref.shape[1]
    copies = []
    for j in range(blocks):
        at = pl.multiple_of((dest_ref[0, j] * blocks + places_ref[j, 0]) * block_rows, block_rows)
        copies.append(
            pltpu.make_async_copy(
                in_ref.at[pl.ds(at, block_rows)],
                out_ref.at[pl.ds(j * block_rows, block_rows)],
                sems.at[j],
            )
        )
    for copy in copies:
        copy.start()
    for copy in copies:
        copy.wait()


def sum_kernel(in_ref, out_ref):
    total = in_ref[0].astype(f32)
    for k in range(1, in_ref.shape[0]):
        total += in_ref[k].astype(f32)
    out_ref[...] = total.astype(bf16)


def fold_kernel(in_ref, out_ref):
    pieces, _, piece = out_ref.shape
    total = in_ref.shape[2]
    folded = jnp.sum(in_ref[...].astype(f32), axis=0).astype(bf16)
    for k in range(pieces):
        at, end = k * piece, min((k + 1) * piece, total)
        if at < total:
            out_ref[k, :, : end - at] = folded[:, at:end]
        if end - at < piece:
            rest = max(end - at, 0)
            out_ref[k, :, rest:] = jnp.zeros((out_ref.shape[1], piece - rest), bf16)


def total_kernel(scaling, in_ref, out_ref):
    total = jnp.sum(in_ref[...].astype(f32), axis=0, keepdims=True) * scaling
    out_ref[...] = jnp.broadcast_to(total.astype(bf16), out_ref.shape)


def result_kernel(in_ref, joined_ref, output_ref):
    xs, zs, piece_rows, piece = in_ref.shape
    split = joined_ref.shape[1]
    step = math.gcd(piece, split)
    for x in range(xs):
        span = slice(x * piece_rows, (x + 1) * piece_rows)
        for at in range(0, split + output_ref.shape[1], step):
            block = in_ref[x, at // piece, :, at % piece : at % piece + step].astype(f32)
            if at < split:
                joined_ref[span, at : at + step] = block
            else:
                output_ref[span, at - split : at - split + step] = block


def call(kernel, name, out_shape, operands, flops=0, scalars=0, scratch=(), unmoved=0, kept=False):
    moved = sum(math.prod(a.shape) * a.dtype.itemsize for a in (*operands, *out_shape))
    smem = pl.BlockSpec(memory_space=pltpu.SMEM)
    vmem = pl.BlockSpec(memory_space=pltpu.VMEM)
    stay = pl.BlockSpec(memory_space=pl.ANY)
    blocked = len(operands) - scalars - unmoved
    return pl.pallas_call(
        kernel,
        out_shape=tuple(out_shape),
        in_specs=[smem] * scalars + [vmem] * blocked + [stay] * unmoved,
        out_specs=tuple(stay if kept else vmem for _ in out_shape),
        scratch_shapes=list(scratch),
        compiler_params=pltpu.CompilerParams(vmem_limit_bytes=VMEM_MOST if unmoved else VMEM_LIMIT),
        cost_estimate=pl.CostEstimate(flops=flops, bytes_accessed=moved, transcendentals=0),
        name=name,
    )(*operands)


def on_device(
    history_rows,
    cotangent,
    dest_device,
    source_device,
    source_offset,
    segments,
    row_valid,
    joined_weight,
    output_weight,
):
    shape = jax.ShapeDtypeStruct
    xs, zs, ys = lax.axis_size("x"), lax.axis_size("z"), lax.axis_size("y")
    lanes = ys * lax.axis_size("c")
    rows, width = history_rows.shape
    blocks = dest_device.shape[1]
    me = lax.axis_index(("y", "c")).astype(jnp.int32).reshape(1)
    scaling = 1.0 / math.sqrt(rows * lanes * xs * zs)

    def exchange(block):
        chunks = block.reshape(lanes, rows // lanes, block.shape[1])
        return lax.all_to_all(chunks, ("y", "c"), 0, 0, tiled=True).reshape(block.shape)

    square = 2 * rows * rows * width
    (packed,) = call(
        functools.partial(pack_kernel, lanes),
        "pack",
        [shape((rows, 2 * width + 128), bf16)],
        (dest_device, history_rows, cotangent),
        2 * square,
        1,
        (
            pltpu.VMEM((rows, width), bf16),
            pltpu.VMEM((rows, width), bf16),
            pltpu.SemaphoreType.DMA((2,)),
        ),
        2,
    )
    routed, places = call(
        functools.partial(route_kernel, lanes),
        "route",
        [shape((rows, 2 * width), bf16), shape((blocks, 128), jnp.int32)],
        (me, exchange(packed)),
        2 * square,
        1,
        (pltpu.VMEM((rows, 128), f32),),
    )
    slots = rows // WIN * HEADS // 2
    total = width * 5
    vmem = pltpu.VMEM
    leaving, keep, send = call(
        functools.partial(layer_kernel, lanes, (xs, ys)),
        "layer",
        [shape((rows, width), bf16), shape((width // 2, total), bf16), shape((width // 2, total), bf16)],
        (
            me,
            source_device,
            source_offset,
            exchange(routed),
            segments,
            row_valid,
            joined_weight,
            output_weight,
        ),
        2 * rows * width * width * 18,
        3,
        (
            vmem((rows, rows), bf16),
            vmem((rows, width), bf16),
            vmem((rows, width), bf16),
            vmem((rows, width), bf16),
            vmem((rows, 1), f32),
            vmem((rows, 4 * width), bf16),
            vmem((rows, 4 * width), bf16),
            vmem((slots, WIN, 2 * WIN), bf16),
            vmem((slots, WIN, 2 * WIN), bf16),
            vmem((rows, width), f32),
            vmem((rows, 1), f32),
            vmem((rows, width), bf16),
            vmem((rows, 4 * width), bf16),
        ),
    )
    gathered = lax.all_gather(leaving, ("y", "c"), axis=0, tiled=True)
    arrived = lax.ppermute(send, "c", [(0, 1), (1, 0)])
    summed = (keep.astype(f32) + arrived.astype(f32)).astype(bf16)
    own = width // (lanes * xs)
    piece = -(-total // (zs * 128)) * 128
    summed = lax.all_to_all(summed.reshape(xs, ys * own, total), "x", 0, 0, tiled=True)
    (partial,) = call(sum_kernel, "sum", [shape((ys * own, total), bf16)], (summed,))
    partial = lax.all_to_all(partial.reshape(ys, own, total), "y", 0, 0, tiled=True)
    (pieces,) = call(fold_kernel, "fold", [shape((zs, own, piece), bf16)], (partial,))
    pieces = lax.all_to_all(pieces, "z", 0, 0, tiled=True)
    (spread,) = call(
        functools.partial(total_kernel, scaling), "total", [shape((xs * zs, own, piece), bf16)], (pieces,)
    )
    spread = lax.all_to_all(spread, ("x", "z"), 0, 0, tiled=True)
    (row_grad,) = call(
        functools.partial(collect_kernel, rows // blocks),
        "collect",
        [shape((rows, width), bf16)],
        (dest_device, places, gathered),
        scalars=2,
        scratch=(pltpu.SemaphoreType.DMA((blocks,)),),
        unmoved=1,
        kept=True,
    )
    joined_grad, output_grad = call(
        result_kernel,
        "result",
        [shape((width // lanes, 4 * width), f32), shape((width // lanes, width), f32)],
        (spread.reshape(xs, zs, own, piece),),
    )
    return (row_grad, joined_grad, output_grad)


def solution(mesh):
    torus = Mesh(mesh.devices.reshape(4, 12, 8, 2), ("x", "z", "y", "c"))
    everywhere = P(("x", "z", "y", "c"), None)
    return jax.shard_map(
        on_device,
        mesh=torus,
        in_specs=(everywhere,) * 7 + (P(), P()),
        out_specs=(everywhere, P(("y", "c"), None), P(("y", "c"), None)),
        check_vma=False,
    )
```

```python
import functools
import math

import jax
import jax.numpy as jnp
from jax import lax
from jax.experimental import pallas as pl
from jax.experimental.pallas import tpu as pltpu
from jax.sharding import Mesh, PartitionSpec as P

HEADS = 8
WIN = 128
epsilon = 1e-05
f32 = jnp.float32
bf16 = jnp.bfloat16
VMEM_LIMIT = 16 * 1024 * 1024
VMEM_MOST = 60 * 1024 * 1024
NT = (((1,), (1,)), ((), ()))
TN = (((0,), (0,)), ((), ()))


def dot(a, b, dims=(((1,), (0,)), ((), ()))):
    return lax.dot_general(a, b, dims, preferred_element_type=f32)


def row_norm(features):
    centred = features - jnp.mean(features, axis=-1, keepdims=True)
    spread = jnp.mean(centred * centred, axis=-1, keepdims=True)
    inverse = lax.rsqrt(spread + epsilon)
    return centred * inverse, inverse


def row_norm_back(cot, normed, inverse):
    mean_cot = jnp.mean(cot, axis=-1, keepdims=True)
    mean_both = jnp.mean(cot * normed, axis=-1, keepdims=True)
    return inverse * (cot - mean_cot - normed * mean_both)


def as_column(row, diagonal):
    return jnp.sum(jnp.where(diagonal, row, 0.0), axis=1, keepdims=True)


def forward_body(
    rows_ref,
    seg_ref,
    valid_ref,
    weight_ref,
    normed_ref,
    inverse_ref,
    active_ref,
    slope_ref,
    weighting_ref,
    score_slope_ref,
    mixed_ref,
    mix_inverse_ref,
    gated_ref,
):
    rows, width = rows_ref.shape
    head = width // HEADS
    pair = 2 * head
    normed, inverse = row_norm(rows_ref[...].astype(f32))
    normed = normed.astype(bf16)
    normed_ref[...] = normed
    inverse_ref[...] = inverse
    for quarter in range(4):
        columns = slice(quarter * width, (quarter + 1) * width)
        projected = dot(normed, weight_ref[:, columns])
        gate = jax.nn.sigmoid(projected)
        active_ref[:, columns] = (projected * gate).astype(bf16)
        slope_ref[:, columns] = (gate * (1.0 + projected * (1.0 - gate))).astype(bf16)
    left = lax.broadcasted_iota(jnp.int32, (WIN, pair), 1) < head
    place_i = lax.broadcasted_iota(jnp.int32, (WIN, WIN), 0)
    place_j = lax.broadcasted_iota(jnp.int32, (WIN, WIN), 1)
    zero = jnp.zeros((), bf16)

    def stacked(block):
        return jnp.concatenate([jnp.where(left, block, zero), jnp.where(left, zero, block)], axis=0)

    for window in range(rows // WIN):
        span = slice(window * WIN, (window + 1) * WIN)
        seg_row = seg_ref[:, span].astype(f32)
        seg_col = as_column(seg_row, place_i == place_j)
        allowed = (seg_col == seg_row) & (place_j <= place_i) & (valid_ref[:, span] == 1)
        allowed = jnp.where(allowed, 1.0, 0.0)
        weights = allowed / jnp.maximum(jnp.sum(allowed, axis=1, keepdims=True), 1.0)
        weights = jnp.concatenate([weights, weights], axis=1)
        mixture = []
        for p in range(HEADS // 2):
            at = p * pair
            value = active_ref[span, width + at : width + at + pair]
            query = active_ref[span, 2 * width + at : 2 * width + at + pair]
            key = active_ref[span, 3 * width + at : 3 * width + at + pair]
            scores = dot(query, stacked(key), NT) * head**-0.5
            gate = jax.nn.sigmoid(scores)
            weighting = (scores * gate * weights).astype(bf16)
            slot = window * (HEADS // 2) + p
            weighting_ref[slot] = weighting
            score_slope_ref[slot] = (
                gate * (1.0 + scores * (1.0 - gate)) * (weights * head**-0.5)
            ).astype(bf16)
            mixture.append(dot(weighting, stacked(value)))
        mixed, mix_inverse = row_norm(jnp.concatenate(mixture, axis=1))
        mixed_ref[span, :] = mixed
        mix_inverse_ref[span, :] = mix_inverse
        gated_ref[span, :] = (mixed * active_ref[span, :width].astype(f32)).astype(bf16)


def backward_body(
    cot_ref,
    valid_ref,
    out_weight_ref,
    normed_ref,
    active_ref,
    slope_ref,
    weighting_ref,
    score_slope_ref,
    mixed_ref,
    mix_inverse_ref,
    gated_ref,
    proj_cot_ref,
    masked_ref,
    normed_t_ref,
    gated_t_ref,
    spread,
    send_ref,
):
    rows, width = cot_ref.shape
    head = width // HEADS
    pair = 2 * head
    place_i = lax.broadcasted_iota(jnp.int32, (rows, rows), 0)
    place_j = lax.broadcasted_iota(jnp.int32, (rows, rows), 1)
    valid_col = as_column(valid_ref[...].astype(f32), place_i == place_j)
    masked = (cot_ref[...].astype(f32) * valid_col).astype(bf16)
    masked_ref[...] = masked
    side = width // 2
    gated_t = permute(spread, gated_ref[...], NT)
    gated_t_ref[...] = gated_t[:side]
    send_ref[:, 4 * width :] = permute(gated_t[side:], masked)
    normed_t = permute(spread, normed_ref[...], NT)
    normed_t_ref[...] = normed_t[:side]
    gated_cot = dot(masked, out_weight_ref[...], NT)
    mixed = mixed_ref[...]
    gate_cot = (gated_cot * mixed).astype(bf16).astype(f32)
    proj_cot_ref[:, :width] = (gate_cot * slope_ref[:, :width].astype(f32)).astype(bf16)
    mixture_cot = row_norm_back(
        gated_cot * active_ref[:, :width].astype(f32), mixed, mix_inverse_ref[...]
    ).astype(bf16)
    left = lax.broadcasted_iota(jnp.int32, (WIN, pair), 1) < head
    zero = jnp.zeros((), bf16)

    def stacked(block):
        return jnp.concatenate([jnp.where(left, block, zero), jnp.where(left, zero, block)], axis=0)

    def folded(block):
        return jnp.where(left, block[:WIN], block[WIN:])

    for window in range(rows // WIN):
        span = slice(window * WIN, (window + 1) * WIN)
        for p in range(HEADS // 2):
            at = p * pair
            slot = window * (HEADS // 2) + p

            def put(quarter, cot):
                columns = slice(quarter * width + at, quarter * width + at + pair)
                slope = slope_ref[span, columns].astype(f32)
                proj_cot_ref[span, columns] = (cot.astype(bf16).astype(f32) * slope).astype(bf16)

            value = active_ref[span, width + at : width + at + pair]
            query = active_ref[span, 2 * width + at : 2 * width + at + pair]
            key = active_ref[span, 3 * width + at : 3 * width + at + pair]
            mix_cot = mixture_cot[span, at : at + pair]
            put(1, folded(dot(weighting_ref[slot], mix_cot, TN)))
            weighting_cot = dot(mix_cot, stacked(value), NT).astype(bf16).astype(f32)
            score_cot = (weighting_cot * score_slope_ref[slot].astype(f32)).astype(bf16)
            put(2, dot(score_cot, stacked(key)))
            put(3, folded(dot(score_cot, query, TN)))
    for quarter in range(4):
        columns = slice(quarter * width, (quarter + 1) * width)
        send_ref[:, columns] = permute(normed_t[side:], proj_cot_ref[:, columns])


def permute(order, block, dims=(((1,), (0,)), ((), ()))):
    return dot(order, block, dims).astype(bf16)


def pack_kernel(lanes, dest_ref, me_ref, own_x_ref, rows_hbm, cot_hbm, out_ref, rows_ref, cot_ref, sems):
    del me_ref, own_x_ref
    copies = [
        pltpu.make_async_copy(rows_hbm, rows_ref, sems.at[0]),
        pltpu.make_async_copy(cot_hbm, cot_ref, sems.at[1]),
    ]
    for copy in copies:
        copy.start()
    rows, width = rows_ref.shape
    blocks = dest_ref.shape[1]
    chunk = rows // lanes
    half = chunk // blocks
    place = lax.broadcasted_iota(jnp.int32, (rows, rows), 0)
    loaded = lax.broadcasted_iota(jnp.int32, (rows, rows), 1)
    source = place % blocks * (rows // blocks) + place // blocks % half * lanes + place // chunk
    order = jnp.where(source == loaded, 1.0, 0.0).astype(bf16)
    extra = out_ref.shape[1] - 2 * width
    block = lax.broadcasted_iota(jnp.int32, (rows, extra), 0) % blocks
    dest = jnp.zeros((rows, extra), f32)
    for j in range(blocks):
        dest = jnp.where(block == j, dest_ref[0, j].astype(f32), dest)
    out_ref[:, 2 * width :] = dest.astype(bf16)
    copies[0].wait()
    out_ref[:, :width] = permute(order, rows_ref[...])
    copies[1].wait()
    out_ref[:, width : 2 * width] = permute(order, cot_ref[...])


def route_kernel(lanes, in_ref, out_ref, order_ref):
    rows, double = out_ref.shape
    chunk = rows // lanes
    blocks = chunk // 2
    extra = in_ref.shape[1] - double
    place = lax.broadcasted_iota(jnp.int32, (rows, rows), 0)
    other = lax.broadcasted_iota(jnp.int32, (rows, rows), 1)
    lane = lax.broadcasted_iota(jnp.int32, (rows, extra), 1)
    dest = in_ref[:, double:].astype(f32)
    chosen = jnp.where(dest == lane.astype(f32), 1.0, 0.0)
    same_half = place // blocks % 2 == other // blocks % 2
    earlier = jnp.where(same_half & (other < place), 1.0, 0.0).astype(bf16)
    rank = jnp.sum(dot(earlier, chosen.astype(bf16)) * chosen, axis=1, keepdims=True)
    row = lax.broadcasted_iota(jnp.int32, (rows, 1), 0)
    target = dest[:, :1] * chunk + (row // blocks % 2 * blocks).astype(f32) + rank
    order = jnp.where(target == other.astype(f32), 1.0, 0.0).astype(bf16)
    order_ref[...] = order
    out_ref[...] = permute(order, in_ref[:, :double], TN)


def slots_of(sources_ref, offsets_ref):
    blocks = sources_ref.shape[1]
    keys = [sources_ref[0, t] * 2 + offsets_ref[0, t] for t in range(blocks)]
    return [
        sum(jnp.where(keys[u] < keys[t], 1, 0) for u in range(blocks) if u != t) for t in range(blocks)
    ]


def gather_order(lanes, sources_ref, offsets_ref, order_ref):
    rows = order_ref.shape[0]
    blocks = sources_ref.shape[1]
    chunk = rows // lanes
    half = chunk // blocks
    span = rows // blocks
    inside = lax.broadcasted_iota(jnp.int32, (span, rows), 0)
    column = lax.broadcasted_iota(jnp.int32, (span, rows), 1)
    base = inside % lanes * chunk + inside // lanes % half * blocks
    for t, slot in enumerate(slots_of(sources_ref, offsets_ref)):
        order = jnp.where(column == base + slot, 1.0, 0.0)
        order_ref[t * span : (t + 1) * span, :] = order.astype(bf16)


def spread_order(parts, core, own_x, width):
    xs, ys = parts
    out = lax.broadcasted_iota(jnp.int32, (width, width), 0)
    column = lax.broadcasted_iota(jnp.int32, (width, width), 1)
    side = width // 2
    block = width // ys // 2
    piece = block // xs
    y = out // piece % ys
    x = (out % side // (piece * ys) + own_x) % xs
    parity = (out // side + core) % 2
    source = y * (2 * block) + parity * block + x * piece + out % piece
    return jnp.where(source == column, 1.0, 0.0).astype(bf16)


def layer_kernel(
    lanes,
    parts,
    me_ref,
    own_x_ref,
    sources_ref,
    offsets_ref,
    in_ref,
    seg_ref,
    valid_ref,
    weight_ref,
    out_weight_ref,
    send_ref,
    proj_cot_ref,
    normed_t_ref,
    gated_t_ref,
    masked_ref,
    rows_ref,
    inverse_ref,
    order_ref,
    cot_ref,
    normed_ref,
    active_ref,
    slope_ref,
    weighting_ref,
    score_slope_ref,
    mixed_ref,
    mix_inverse_ref,
    gated_ref,
):
    width = rows_ref.shape[1]
    gather_order(lanes, sources_ref, offsets_ref, order_ref)
    rows_ref[...] = permute(order_ref[...], in_ref[:, :width])
    cot_ref[...] = permute(order_ref[...], in_ref[:, width:])
    stored = (
        active_ref,
        slope_ref,
        weighting_ref,
        score_slope_ref,
        mixed_ref,
        mix_inverse_ref,
        gated_ref,
    )
    forward_body(rows_ref, seg_ref, valid_ref, weight_ref, normed_ref, inverse_ref, *stored)
    backward_body(
        cot_ref,
        valid_ref,
        out_weight_ref,
        normed_ref,
        *stored,
        proj_cot_ref,
        masked_ref,
        normed_t_ref,
        gated_t_ref,
        spread_order(parts, me_ref[0] % 2, own_x_ref[0], width),
        send_ref,
    )


def finish_kernel(
    weight_ref,
    proj_cot_ref,
    normed_t_ref,
    gated_t_ref,
    masked_ref,
    rows_ref,
    inverse_ref,
    order_ref,
    leave_ref,
    *keep_refs,
):
    rows, width = rows_ref.shape

    def put(grad, columns):
        size = keep_refs[0].shape[0]
        for k, keep_ref in enumerate(keep_refs):
            keep_ref[:, columns] = grad[k * size : (k + 1) * size]

    normed_cot = jnp.zeros((rows, width), f32)
    for quarter in range(4):
        columns = slice(quarter * width, (quarter + 1) * width)
        proj_cot = proj_cot_ref[:, columns]
        normed_cot += dot(proj_cot, weight_ref[:, columns], NT)
        put(permute(normed_t_ref[...], proj_cot), columns)
    masked = masked_ref[...]
    put(permute(gated_t_ref[...], masked), slice(4 * width, 5 * width))
    features = rows_ref[...].astype(f32)
    inverse = inverse_ref[...]
    normed_f = (features - jnp.mean(features, axis=-1, keepdims=True)) * inverse
    rows_cot = row_norm_back(normed_cot, normed_f, inverse)
    work_grad = (masked.astype(f32) + rows_cot).astype(bf16)
    leave_ref[...] = permute(order_ref[...], work_grad, TN)


def add_kernel(arrived_ref, *refs):
    keep_refs, out_refs = refs[: len(refs) // 2], refs[len(refs) // 2 :]
    for k, out_ref in enumerate(out_refs):
        span = slice(k * out_ref.shape[0], (k + 1) * out_ref.shape[0])
        added = keep_refs[k][...].astype(f32) + arrived_ref[span, :].astype(f32)
        out_ref[...] = added.astype(bf16)


def merge_kernel(order_ref, back_ref, *refs):
    *part_refs, out_ref = refs
    ys, own, _ = out_ref.shape
    total = part_refs[0].shape[1]
    partial = sum(part_ref[...].astype(f32) for part_ref in part_refs)
    out_ref[:, :, :total] = partial.reshape(ys, own, total).astype(bf16)
    rows, width = back_ref.shape
    groups = rows // (ys * own)
    back = dot(order_ref[...], back_ref[...]).reshape(ys, groups, own, width)
    for g in range(groups):
        at = total + g * width
        out_ref[:, :, at : at + width] = back[:, g].astype(bf16)


def fold_kernel(me_ref, in_ref, out_ref, mine_ref, other_ref):
    pieces, own, piece = out_ref.shape
    ys = in_ref.shape[0]
    width = mine_ref.shape[1]
    halves = mine_ref.shape[0] // (ys * own)
    total = in_ref.shape[2] - 2 * halves * width
    folded = jnp.sum(in_ref[:, :, :total].astype(f32), axis=0).astype(bf16)
    for k in range(pieces):
        at, end = k * piece, min((k + 1) * piece, total)
        if at < total:
            out_ref[k, :, : end - at] = folded[:, at:end]
        if end - at < piece:
            rest = max(end - at, 0)
            out_ref[k, :, rest:] = jnp.zeros((own, piece - rest), bf16)
    first = me_ref[0] % 2 == 0
    for r in range(halves):
        span = slice(r * ys * own, (r + 1) * ys * own)
        sets = []
        for g in (r, halves + r):
            at = total + g * width
            sets.append(in_ref[:, :, at : at + width].astype(f32).reshape(ys * own, width))
        mine_ref[span, :] = jnp.where(first, sets[0], sets[1]).astype(bf16)
        other_ref[span, :] = jnp.where(first, sets[1], sets[0]).astype(bf16)


def unpack_kernel(lanes, blocks, me_ref, mine_ref, arrived_ref, out_ref, token_ref):
    token_ref[...] = jnp.zeros_like(token_ref)
    rows = out_ref.shape[0]
    side = rows // 2
    out = lax.broadcasted_iota(jnp.int32, (rows, rows), 0)
    column = lax.broadcasted_iota(jnp.int32, (rows, rows), 1)
    block = out // (rows // blocks)
    half = out // lanes % (rows // blocks // lanes)
    piece = out % lanes
    place = half * (blocks * lanes // 2) + piece // 2 * blocks + block
    place += (piece + me_ref[0]) % 2 * side
    order = jnp.where(place == column, 1.0, 0.0).astype(bf16)
    got = dot(order[:, :side], mine_ref[...]) + dot(order[:, side:], arrived_ref[...])
    out_ref[...] = got.astype(bf16)


def total_kernel(scaling, in_ref, out_ref):
    total = jnp.sum(in_ref[...].astype(f32), axis=0, keepdims=True) * scaling
    out_ref[...] = jnp.broadcast_to(total.astype(bf16), out_ref.shape)


def result_kernel(in_ref, after_ref, joined_ref, output_ref):
    del after_ref
    xs, zs, piece_rows, piece = in_ref.shape
    split = joined_ref.shape[1]
    step = math.gcd(piece, split)
    for x in range(xs):
        span = slice(x * piece_rows, (x + 1) * piece_rows)
        for at in range(0, split + output_ref.shape[1], step):
            block = in_ref[x, at // piece, :, at % piece : at % piece + step].astype(f32)
            if at < split:
                joined_ref[span, at : at + step] = block
            else:
                output_ref[span, at - split : at - split + step] = block


def call(kernel, name, out_shape, operands, flops=0, scalars=0, scratch=(), unmoved=0, aliases=None):
    moved = sum(math.prod(a.shape) * a.dtype.itemsize for a in (*operands, *out_shape))
    smem = pl.BlockSpec(memory_space=pltpu.SMEM)
    vmem = pl.BlockSpec(memory_space=pltpu.VMEM)
    stay = pl.BlockSpec(memory_space=pl.ANY)
    blocked = len(operands) - scalars - unmoved
    return pl.pallas_call(
        kernel,
        out_shape=tuple(out_shape),
        in_specs=[smem] * scalars + [vmem] * blocked + [stay] * unmoved,
        out_specs=tuple(vmem for _ in out_shape),
        scratch_shapes=list(scratch),
        input_output_aliases=aliases or {},
        compiler_params=pltpu.CompilerParams(vmem_limit_bytes=VMEM_MOST if unmoved else VMEM_LIMIT),
        cost_estimate=pl.CostEstimate(flops=flops, bytes_accessed=moved, transcendentals=0),
        name=name,
    )(*operands)


def on_device(
    history_rows,
    cotangent,
    dest_device,
    source_device,
    source_offset,
    segments,
    row_valid,
    joined_weight,
    output_weight,
):
    shape = jax.ShapeDtypeStruct
    xs, zs, ys = lax.axis_size("x"), lax.axis_size("z"), lax.axis_size("y")
    lanes = ys * lax.axis_size("c")
    rows, width = history_rows.shape
    blocks = dest_device.shape[1]
    me = lax.axis_index(("y", "c")).astype(jnp.int32).reshape(1)
    own_x = lax.axis_index("x").astype(jnp.int32).reshape(1)
    scaling = 1.0 / math.sqrt(rows * lanes * xs * zs)

    def exchange(block):
        chunks = block.reshape(lanes, rows // lanes, block.shape[1])
        return lax.all_to_all(chunks, ("y", "c"), 0, 0, tiled=True).reshape(block.shape)

    square = 2 * rows * rows * width
    (packed,) = call(
        functools.partial(pack_kernel, lanes),
        "pack",
        [shape((rows, 2 * width + 128), bf16)],
        (dest_device, me, own_x, history_rows, cotangent),
        2 * square,
        3,
        (
            pltpu.VMEM((rows, width), bf16),
            pltpu.VMEM((rows, width), bf16),
            pltpu.SemaphoreType.DMA((2,)),
        ),
        2,
    )
    routed, route = call(
        functools.partial(route_kernel, lanes),
        "route",
        [shape((rows, 2 * width), bf16), shape((rows, rows), bf16)],
        (exchange(packed),),
        2 * square,
    )
    slots = rows // WIN * HEADS // 2
    total = width * 5
    vmem = pltpu.VMEM
    side = width // 2
    send, *stored = call(
        functools.partial(layer_kernel, lanes, (xs, ys)),
        "layer",
        [
            shape((side, total), bf16),
            shape((rows, 4 * width), bf16),
            shape((side, rows), bf16),
            shape((side, rows), bf16),
            shape((rows, width), bf16),
            shape((rows, width), bf16),
            shape((rows, 1), f32),
            shape((rows, rows), bf16),
        ],
        (
            me,
            own_x,
            source_device,
            source_offset,
            exchange(routed),
            segments,
            row_valid,
            joined_weight,
            output_weight,
        ),
        2 * rows * width * width * 10,
        4,
        (
            vmem((rows, width), bf16),
            vmem((rows, width), bf16),
            vmem((rows, 4 * width), bf16),
            vmem((rows, 4 * width), bf16),
            vmem((slots, WIN, 2 * WIN), bf16),
            vmem((slots, WIN, 2 * WIN), bf16),
            vmem((rows, width), f32),
            vmem((rows, 1), f32),
            vmem((rows, width), bf16),
        ),
    )
    own = width // (lanes * xs)
    quarters = [shape((ys * own, total), bf16)] * xs
    leaving, *keep = call(
        finish_kernel,
        "finish",
        [shape((rows, width), bf16)] + quarters,
        (joined_weight, *stored),
        2 * rows * width * width * 8,
    )
    swap = [(0, 1), (1, 0)]
    arrived = lax.ppermute(send, "c", swap)
    parts = call(
        add_kernel, "add", quarters, (arrived, *keep), aliases={k + 1: k for k in range(xs)}
    )
    parts = [
        parts[k] if k == 0 else lax.ppermute(parts[k], "x", [(i, (i + k) % xs) for i in range(xs)])
        for k in range(xs)
    ]
    (merged,) = call(
        merge_kernel,
        "merge",
        [shape((ys, own, total + rows // (ys * own) * width), bf16)],
        (route, exchange(leaving), *parts),
        square,
    )
    merged = lax.all_to_all(merged, "y", 0, 0, tiled=True)
    piece = -(-total // (zs * 128)) * 128
    pieces, mine, other = call(
        fold_kernel,
        "fold",
        [shape((zs, own, piece), bf16)] + [shape((rows // 2, width), bf16)] * 2,
        (me, merged),
        0,
        1,
    )
    row_grad, token = call(
        functools.partial(unpack_kernel, lanes, blocks),
        "unpack",
        [shape((rows, width), bf16), shape((8, 128), f32)],
        (me, mine, lax.ppermute(other, "c", swap)),
        square,
        1,
    )
    pieces = lax.all_to_all(pieces, "z", 0, 0, tiled=True)
    (spread,) = call(
        functools.partial(total_kernel, scaling), "total", [shape((xs * zs, own, piece), bf16)], (pieces,)
    )
    spread = lax.all_to_all(spread, ("x", "z"), 0, 0, tiled=True)
    joined_grad, output_grad = call(
        result_kernel,
        "result",
        [shape((width // lanes, 4 * width), f32), shape((width // lanes, width), f32)],
        (spread.reshape(xs, zs, own, piece), token),
    )
    return (row_grad, joined_grad, output_grad)


def solution(mesh):
    torus = Mesh(mesh.devices.reshape(4, 12, 8, 2), ("x", "z", "y", "c"))
    everywhere = P(("x", "z", "y", "c"), None)
    return jax.shard_map(
        on_device,
        mesh=torus,
        in_specs=(everywhere,) * 7 + (P(), P()),
        out_specs=(everywhere, P(("y", "c"), None), P(("y", "c"), None)),
        check_vma=False,
    )
```

```python
import functools
import math

import jax
import jax.numpy as jnp
from jax import lax
from jax.experimental import pallas as pl
from jax.experimental.pallas import tpu as pltpu
from jax.sharding import Mesh, PartitionSpec as P

HEADS = 8
WIN = 128
epsilon = 1e-05
f32 = jnp.float32
bf16 = jnp.bfloat16
VMEM_LIMIT = 16 * 1024 * 1024
VMEM_MOST = 60 * 1024 * 1024
NT = (((1,), (1,)), ((), ()))
TN = (((0,), (0,)), ((), ()))


def dot(a, b, dims=(((1,), (0,)), ((), ()))):
    return lax.dot_general(a, b, dims, preferred_element_type=f32)


def row_norm(features):
    centred = features - jnp.mean(features, axis=-1, keepdims=True)
    spread = jnp.mean(centred * centred, axis=-1, keepdims=True)
    inverse = lax.rsqrt(spread + epsilon)
    return centred * inverse, inverse


def row_norm_back(cot, normed, inverse):
    mean_cot = jnp.mean(cot, axis=-1, keepdims=True)
    mean_both = jnp.mean(cot * normed, axis=-1, keepdims=True)
    return inverse * (cot - mean_cot - normed * mean_both)


def as_column(row, diagonal):
    return jnp.sum(jnp.where(diagonal, row, 0.0), axis=1, keepdims=True)


def forward_body(
    rows_ref,
    seg_ref,
    valid_ref,
    weight_ref,
    normed_ref,
    inverse_ref,
    active_ref,
    slope_ref,
    weighting_ref,
    score_slope_ref,
    mixed_ref,
    mix_inverse_ref,
    gated_ref,
):
    rows, width = rows_ref.shape
    head = width // HEADS
    pair = 2 * head
    normed, inverse = row_norm(rows_ref[...].astype(f32))
    normed = normed.astype(bf16)
    normed_ref[...] = normed
    inverse_ref[...] = inverse
    for quarter in range(4):
        columns = slice(quarter * width, (quarter + 1) * width)
        projected = dot(normed, weight_ref[:, columns])
        gate = jax.nn.sigmoid(projected)
        active_ref[:, columns] = (projected * gate).astype(bf16)
        slope_ref[:, columns] = (gate * (1.0 + projected * (1.0 - gate))).astype(bf16)
    left = lax.broadcasted_iota(jnp.int32, (WIN, pair), 1) < head
    place_i = lax.broadcasted_iota(jnp.int32, (WIN, WIN), 0)
    place_j = lax.broadcasted_iota(jnp.int32, (WIN, WIN), 1)
    zero = jnp.zeros((), bf16)

    def stacked(block):
        return jnp.concatenate([jnp.where(left, block, zero), jnp.where(left, zero, block)], axis=0)

    for window in range(rows // WIN):
        span = slice(window * WIN, (window + 1) * WIN)
        seg_row = seg_ref[:, span].astype(f32)
        seg_col = as_column(seg_row, place_i == place_j)
        allowed = (seg_col == seg_row) & (place_j <= place_i) & (valid_ref[:, span] == 1)
        allowed = jnp.where(allowed, 1.0, 0.0)
        weights = allowed / jnp.maximum(jnp.sum(allowed, axis=1, keepdims=True), 1.0)
        weights = jnp.concatenate([weights, weights], axis=1)
        mixture = []
        for p in range(HEADS // 2):
            at = p * pair
            value = active_ref[span, width + at : width + at + pair]
            query = active_ref[span, 2 * width + at : 2 * width + at + pair]
            key = active_ref[span, 3 * width + at : 3 * width + at + pair]
            scores = dot(query, stacked(key), NT) * head**-0.5
            gate = jax.nn.sigmoid(scores)
            weighting = (scores * gate * weights).astype(bf16)
            slot = window * (HEADS // 2) + p
            weighting_ref[slot] = weighting
            score_slope_ref[slot] = (
                gate * (1.0 + scores * (1.0 - gate)) * (weights * head**-0.5)
            ).astype(bf16)
            mixture.append(dot(weighting, stacked(value)))
        mixed, mix_inverse = row_norm(jnp.concatenate(mixture, axis=1))
        mixed_ref[span, :] = mixed
        mix_inverse_ref[span, :] = mix_inverse
        gated_ref[span, :] = (mixed * active_ref[span, :width].astype(f32)).astype(bf16)


def backward_body(
    cot_ref,
    valid_ref,
    out_weight_ref,
    normed_ref,
    active_ref,
    slope_ref,
    weighting_ref,
    score_slope_ref,
    mixed_ref,
    mix_inverse_ref,
    gated_ref,
    proj_cot_ref,
    masked_ref,
    normed_t_ref,
    gated_t_ref,
    spread,
    send_ref,
):
    rows, width = cot_ref.shape
    head = width // HEADS
    pair = 2 * head
    place_i = lax.broadcasted_iota(jnp.int32, (rows, rows), 0)
    place_j = lax.broadcasted_iota(jnp.int32, (rows, rows), 1)
    valid_col = as_column(valid_ref[...].astype(f32), place_i == place_j)
    masked = (cot_ref[...].astype(f32) * valid_col).astype(bf16)
    masked_ref[...] = masked
    side = width // 2
    gated_t = permute(spread, gated_ref[...], NT)
    gated_t_ref[...] = gated_t[:side]
    send_ref[:, 4 * width :] = permute(gated_t[side:], masked)
    normed_t = permute(spread, normed_ref[...], NT)
    normed_t_ref[...] = normed_t[:side]
    gated_cot = dot(masked, out_weight_ref[...], NT)
    mixed = mixed_ref[...]
    gate_cot = (gated_cot * mixed).astype(bf16).astype(f32)
    proj_cot_ref[:, :width] = (gate_cot * slope_ref[:, :width].astype(f32)).astype(bf16)
    mixture_cot = row_norm_back(
        gated_cot * active_ref[:, :width].astype(f32), mixed, mix_inverse_ref[...]
    ).astype(bf16)
    left = lax.broadcasted_iota(jnp.int32, (WIN, pair), 1) < head
    zero = jnp.zeros((), bf16)

    def stacked(block):
        return jnp.concatenate([jnp.where(left, block, zero), jnp.where(left, zero, block)], axis=0)

    def folded(block):
        return jnp.where(left, block[:WIN], block[WIN:])

    for window in range(rows // WIN):
        span = slice(window * WIN, (window + 1) * WIN)
        for p in range(HEADS // 2):
            at = p * pair
            slot = window * (HEADS // 2) + p

            def put(quarter, cot):
                columns = slice(quarter * width + at, quarter * width + at + pair)
                slope = slope_ref[span, columns].astype(f32)
                proj_cot_ref[span, columns] = (cot.astype(bf16).astype(f32) * slope).astype(bf16)

            value = active_ref[span, width + at : width + at + pair]
            query = active_ref[span, 2 * width + at : 2 * width + at + pair]
            key = active_ref[span, 3 * width + at : 3 * width + at + pair]
            mix_cot = mixture_cot[span, at : at + pair]
            put(1, folded(dot(weighting_ref[slot], mix_cot, TN)))
            weighting_cot = dot(mix_cot, stacked(value), NT).astype(bf16).astype(f32)
            score_cot = (weighting_cot * score_slope_ref[slot].astype(f32)).astype(bf16)
            put(2, dot(score_cot, stacked(key)))
            put(3, folded(dot(score_cot, query, TN)))
    for quarter in range(4):
        columns = slice(quarter * width, (quarter + 1) * width)
        send_ref[:, columns] = permute(normed_t[side:], proj_cot_ref[:, columns])


def permute(order, block, dims=(((1,), (0,)), ((), ()))):
    return dot(order, block, dims).astype(bf16)


def pack_kernel(lanes, dest_ref, me_ref, own_x_ref, rows_hbm, cot_hbm, out_ref, rows_ref, cot_ref, sems):
    del me_ref, own_x_ref
    copies = [
        pltpu.make_async_copy(rows_hbm, rows_ref, sems.at[0]),
        pltpu.make_async_copy(cot_hbm, cot_ref, sems.at[1]),
    ]
    for copy in copies:
        copy.start()
    rows, width = rows_ref.shape
    blocks = dest_ref.shape[1]
    units = lanes * blocks
    halves = rows // units
    place = lax.broadcasted_iota(jnp.int32, (units, rows), 0)
    loaded = lax.broadcasted_iota(jnp.int32, (units, rows), 1)
    orders = []
    for r in range(halves):
        source = place % blocks * (rows // blocks) + r * lanes + place // blocks
        orders.append(jnp.where(source == loaded, 1.0, 0.0).astype(bf16))
    extra = out_ref.shape[1] - 2 * halves * width
    block = lax.broadcasted_iota(jnp.int32, (units, extra), 0) % blocks
    dest = jnp.zeros((units, extra), f32)
    for j in range(blocks):
        dest = jnp.where(block == j, dest_ref[0, j].astype(f32), dest)
    out_ref[:, 2 * halves * width :] = dest.astype(bf16)
    for k, block_ref in enumerate((rows_ref, cot_ref)):
        copies[k].wait()
        for r in range(halves):
            at = (2 * r + k) * width
            out_ref[:, at : at + width] = permute(orders[r], block_ref[...])


def route_kernel(lanes, in_ref, out_ref, order_ref):
    units, payload = out_ref.shape
    blocks = units // lanes
    extra = in_ref.shape[1] - payload
    place = lax.broadcasted_iota(jnp.int32, (units, units), 0)
    other = lax.broadcasted_iota(jnp.int32, (units, units), 1)
    lane = lax.broadcasted_iota(jnp.int32, (units, extra), 1)
    dest = in_ref[:, payload:].astype(f32)
    chosen = jnp.where(dest == lane.astype(f32), 1.0, 0.0)
    earlier = jnp.where(other < place, 1.0, 0.0).astype(bf16)
    rank = jnp.sum(dot(earlier, chosen.astype(bf16)) * chosen, axis=1, keepdims=True)
    target = dest[:, :1] * blocks + rank
    order = jnp.where(target == other.astype(f32), 1.0, 0.0).astype(bf16)
    order_ref[...] = order
    out_ref[...] = permute(order, in_ref[:, :payload], TN)


def slots_of(sources_ref, offsets_ref):
    blocks = sources_ref.shape[1]
    keys = [sources_ref[0, t] * 2 + offsets_ref[0, t] for t in range(blocks)]
    return [
        sum(jnp.where(keys[u] < keys[t], 1, 0) for u in range(blocks) if u != t) for t in range(blocks)
    ]


def gather_order(lanes, sources_ref, offsets_ref, order_ref):
    units = order_ref.shape[0]
    blocks = sources_ref.shape[1]
    inside = lax.broadcasted_iota(jnp.int32, (lanes, units), 0)
    column = lax.broadcasted_iota(jnp.int32, (lanes, units), 1)
    for t, slot in enumerate(slots_of(sources_ref, offsets_ref)):
        order = jnp.where(column == inside * blocks + slot, 1.0, 0.0)
        order_ref[t * lanes : (t + 1) * lanes, :] = order.astype(bf16)


def spread_order(parts, core, own_x, width):
    xs, ys = parts
    out = lax.broadcasted_iota(jnp.int32, (width, width), 0)
    column = lax.broadcasted_iota(jnp.int32, (width, width), 1)
    side = width // 2
    block = width // ys // 2
    piece = block // xs
    y = out // piece % ys
    x = out % side // (piece * ys) ^ own_x
    parity = (out // side + core) % 2
    source = y * (2 * block) + parity * block + x * piece + out % piece
    return jnp.where(source == column, 1.0, 0.0).astype(bf16)


def layer_kernel(
    lanes,
    parts,
    me_ref,
    own_x_ref,
    sources_ref,
    offsets_ref,
    in_ref,
    seg_ref,
    valid_ref,
    weight_ref,
    out_weight_ref,
    send_ref,
    proj_cot_ref,
    normed_t_ref,
    gated_t_ref,
    masked_ref,
    rows_ref,
    inverse_ref,
    order_ref,
    cot_ref,
    normed_ref,
    active_ref,
    slope_ref,
    weighting_ref,
    score_slope_ref,
    mixed_ref,
    mix_inverse_ref,
    gated_ref,
):
    width = rows_ref.shape[1]
    gather_order(lanes, sources_ref, offsets_ref, order_ref)
    halves = in_ref.shape[1] // (2 * width)
    for k, block_ref in enumerate((rows_ref, cot_ref)):
        for r in range(halves):
            at = (2 * r + k) * width
            block = permute(order_ref[...], in_ref[:, at : at + width])
            for t in range(order_ref.shape[0] // lanes):
                to = (t * halves + r) * lanes
                block_ref[to : to + lanes, :] = block[t * lanes : (t + 1) * lanes]
    stored = (
        active_ref,
        slope_ref,
        weighting_ref,
        score_slope_ref,
        mixed_ref,
        mix_inverse_ref,
        gated_ref,
    )
    forward_body(rows_ref, seg_ref, valid_ref, weight_ref, normed_ref, inverse_ref, *stored)
    backward_body(
        cot_ref,
        valid_ref,
        out_weight_ref,
        normed_ref,
        *stored,
        proj_cot_ref,
        masked_ref,
        normed_t_ref,
        gated_t_ref,
        spread_order(parts, me_ref[0] % 2, own_x_ref[0], width),
        send_ref,
    )


def finish_kernel(
    lanes,
    weight_ref,
    proj_cot_ref,
    normed_t_ref,
    gated_t_ref,
    masked_ref,
    rows_ref,
    inverse_ref,
    order_ref,
    leave_ref,
    *keep_refs,
):
    rows, width = rows_ref.shape

    def put(grad, columns):
        size = keep_refs[0].shape[0]
        for k, keep_ref in enumerate(keep_refs):
            keep_ref[:, columns] = grad[k * size : (k + 1) * size]

    normed_cot = jnp.zeros((rows, width), f32)
    for quarter in range(4):
        columns = slice(quarter * width, (quarter + 1) * width)
        proj_cot = proj_cot_ref[:, columns]
        normed_cot += dot(proj_cot, weight_ref[:, columns], NT)
        put(permute(normed_t_ref[...], proj_cot), columns)
    masked = masked_ref[...]
    put(permute(gated_t_ref[...], masked), slice(4 * width, 5 * width))
    features = rows_ref[...].astype(f32)
    inverse = inverse_ref[...]
    normed_f = (features - jnp.mean(features, axis=-1, keepdims=True)) * inverse
    rows_cot = row_norm_back(normed_cot, normed_f, inverse)
    work_grad = (masked.astype(f32) + rows_cot).astype(bf16)
    units = order_ref.shape[0]
    halves = rows // units
    for r in range(halves):
        parts = [
            work_grad[(t * halves + r) * lanes : (t * halves + r + 1) * lanes]
            for t in range(units // lanes)
        ]
        grad = permute(order_ref[...], jnp.concatenate(parts, axis=0), TN)
        leave_ref[:, r * width : (r + 1) * width] = grad


def add_kernel(arrived_ref, *refs):
    keep_refs, out_refs = refs[: len(refs) // 2], refs[len(refs) // 2 :]
    for k, out_ref in enumerate(out_refs):
        span = slice(k * out_ref.shape[0], (k + 1) * out_ref.shape[0])
        added = keep_refs[k][...].astype(f32) + arrived_ref[span, :].astype(f32)
        out_ref[...] = added.astype(bf16)


def merge_kernel(order_ref, back_ref, *refs):
    *part_refs, out_ref = refs
    ys, own, _ = out_ref.shape
    total = part_refs[0].shape[1]
    partial = sum(part_ref[...].astype(f32) for part_ref in part_refs)
    out_ref[:, :, :total] = partial.reshape(ys, own, total).astype(bf16)
    units, width = back_ref.shape
    groups = units // (ys * own)
    back = dot(order_ref[...], back_ref[...]).reshape(ys, groups, own, width)
    for g in range(groups):
        at = total + g * width
        out_ref[:, :, at : at + width] = back[:, g].astype(bf16)


def fold_kernel(me_ref, in_ref, out_ref, mine_ref, other_ref):
    pieces, own, piece = out_ref.shape
    ys = in_ref.shape[0]
    width = mine_ref.shape[1]
    halves = mine_ref.shape[0] // (ys * own)
    total = in_ref.shape[2] - 2 * halves * width
    folded = jnp.sum(in_ref[:, :, :total].astype(f32), axis=0).astype(bf16)
    for k in range(pieces):
        at, end = k * piece, min((k + 1) * piece, total)
        if at < total:
            out_ref[k, :, : end - at] = folded[:, at:end]
        if end - at < piece:
            rest = max(end - at, 0)
            out_ref[k, :, rest:] = jnp.zeros((own, piece - rest), bf16)
    first = me_ref[0] % 2 == 0
    for r in range(halves):
        span = slice(r * ys * own, (r + 1) * ys * own)
        sets = []
        for g in (r, halves + r):
            at = total + g * width
            sets.append(in_ref[:, :, at : at + width].astype(f32).reshape(ys * own, width))
        mine_ref[span, :] = jnp.where(first, sets[0], sets[1]).astype(bf16)
        other_ref[span, :] = jnp.where(first, sets[1], sets[0]).astype(bf16)


def unpack_kernel(lanes, blocks, me_ref, mine_ref, arrived_ref, out_ref, token_ref):
    token_ref[...] = jnp.zeros_like(token_ref)
    rows = out_ref.shape[0]
    side = rows // 2
    out = lax.broadcasted_iota(jnp.int32, (rows, rows), 0)
    column = lax.broadcasted_iota(jnp.int32, (rows, rows), 1)
    block = out // (rows // blocks)
    half = out // lanes % (rows // blocks // lanes)
    piece = out % lanes
    place = half * (blocks * lanes // 2) + piece // 2 * blocks + block
    place += (piece + me_ref[0]) % 2 * side
    order = jnp.where(place == column, 1.0, 0.0).astype(bf16)
    got = dot(order[:, :side], mine_ref[...]) + dot(order[:, side:], arrived_ref[...])
    out_ref[...] = got.astype(bf16)


def total_kernel(scaling, in_ref, out_ref):
    total = jnp.sum(in_ref[...].astype(f32), axis=0, keepdims=True) * scaling
    out_ref[...] = jnp.broadcast_to(total.astype(bf16), out_ref.shape)


def result_kernel(in_ref, after_ref, joined_ref, output_ref):
    del after_ref
    xs, zs, piece_rows, piece = in_ref.shape
    split = joined_ref.shape[1]
    step = math.gcd(piece, split)
    for x in range(xs):
        span = slice(x * piece_rows, (x + 1) * piece_rows)
        for at in range(0, split + output_ref.shape[1], step):
            block = in_ref[x, at // piece, :, at % piece : at % piece + step].astype(f32)
            if at < split:
                joined_ref[span, at : at + step] = block
            else:
                output_ref[span, at - split : at - split + step] = block


def call(kernel, name, out_shape, operands, flops=0, scalars=0, scratch=(), unmoved=0, aliases=None):
    moved = sum(math.prod(a.shape) * a.dtype.itemsize for a in (*operands, *out_shape))
    smem = pl.BlockSpec(memory_space=pltpu.SMEM)
    vmem = pl.BlockSpec(memory_space=pltpu.VMEM)
    stay = pl.BlockSpec(memory_space=pl.ANY)
    blocked = len(operands) - scalars - unmoved
    return pl.pallas_call(
        kernel,
        out_shape=tuple(out_shape),
        in_specs=[smem] * scalars + [vmem] * blocked + [stay] * unmoved,
        out_specs=tuple(vmem for _ in out_shape),
        scratch_shapes=list(scratch),
        input_output_aliases=aliases or {},
        compiler_params=pltpu.CompilerParams(vmem_limit_bytes=VMEM_MOST if unmoved else VMEM_LIMIT),
        cost_estimate=pl.CostEstimate(flops=flops, bytes_accessed=moved, transcendentals=0),
        name=name,
    )(*operands)


def on_device(
    history_rows,
    cotangent,
    dest_device,
    source_device,
    source_offset,
    segments,
    row_valid,
    joined_weight,
    output_weight,
):
    shape = jax.ShapeDtypeStruct
    xs, zs, ys = lax.axis_size("x"), lax.axis_size("z"), lax.axis_size("y")
    lanes = ys * lax.axis_size("c")
    rows, width = history_rows.shape
    blocks = dest_device.shape[1]
    me = lax.axis_index(("y", "c")).astype(jnp.int32).reshape(1)
    own_x = lax.axis_index("x").astype(jnp.int32).reshape(1)
    scaling = 1.0 / math.sqrt(rows * lanes * xs * zs)

    def exchange(block):
        chunks = block.reshape(lanes, blocks, block.shape[1])
        return lax.all_to_all(chunks, ("y", "c"), 0, 0, tiled=True).reshape(block.shape)

    units = lanes * blocks
    halves = rows // units
    square = 2 * rows * units * width
    (packed,) = call(
        functools.partial(pack_kernel, lanes),
        "pack",
        [shape((units, 2 * halves * width + 128), bf16)],
        (dest_device, me, own_x, history_rows, cotangent),
        2 * square,
        3,
        (
            pltpu.VMEM((rows, width), bf16),
            pltpu.VMEM((rows, width), bf16),
            pltpu.SemaphoreType.DMA((2,)),
        ),
        2,
    )
    routed, route = call(
        functools.partial(route_kernel, lanes),
        "route",
        [shape((units, 2 * halves * width), bf16), shape((units, units), bf16)],
        (exchange(packed),),
        2 * square,
    )
    slots = rows // WIN * HEADS // 2
    total = width * 5
    vmem = pltpu.VMEM
    side = width // 2
    send, *stored = call(
        functools.partial(layer_kernel, lanes, (xs, ys)),
        "layer",
        [
            shape((side, total), bf16),
            shape((rows, 4 * width), bf16),
            shape((side, rows), bf16),
            shape((side, rows), bf16),
            shape((rows, width), bf16),
            shape((rows, width), bf16),
            shape((rows, 1), f32),
            shape((units, units), bf16),
        ],
        (
            me,
            own_x,
            source_device,
            source_offset,
            exchange(routed),
            segments,
            row_valid,
            joined_weight,
            output_weight,
        ),
        2 * rows * width * width * 10,
        4,
        (
            vmem((rows, width), bf16),
            vmem((rows, width), bf16),
            vmem((rows, 4 * width), bf16),
            vmem((rows, 4 * width), bf16),
            vmem((slots, WIN, 2 * WIN), bf16),
            vmem((slots, WIN, 2 * WIN), bf16),
            vmem((rows, width), f32),
            vmem((rows, 1), f32),
            vmem((rows, width), bf16),
        ),
    )
    own = width // (lanes * xs)
    quarters = [shape((ys * own, total), bf16)] * xs
    leaving, *keep = call(
        functools.partial(finish_kernel, lanes),
        "finish",
        [shape((units, halves * width), bf16)] + quarters,
        (joined_weight, *stored),
        2 * rows * width * width * 8,
    )
    swap = [(0, 1), (1, 0)]
    arrived = lax.ppermute(send, "c", swap)
    parts = call(
        add_kernel, "add", quarters, (arrived, *keep), aliases={k + 1: k for k in range(xs)}
    )
    arriving = {
        k: lax.ppermute(parts[k], "x", [(i, i ^ k) for i in range(xs)]) for k in sorted(range(1, xs), key=lambda k: (-(k & 2), k & 1))
    }
    parts = [parts[0], *arriving.values()]
    (merged,) = call(
        merge_kernel,
        "merge",
        [shape((ys, own, total + rows // (ys * own) * width), bf16)],
        (route, exchange(leaving), *parts),
        square,
    )
    merged = lax.all_to_all(merged, "y", 0, 0, tiled=True)
    piece = -(-total // (zs * 128)) * 128
    pieces, mine, other = call(
        fold_kernel,
        "fold",
        [shape((zs, own, piece), bf16)] + [shape((rows // 2, width), bf16)] * 2,
        (me, merged),
        0,
        1,
    )
    row_grad, token = call(
        functools.partial(unpack_kernel, lanes, blocks),
        "unpack",
        [shape((rows, width), bf16), shape((8, 128), f32)],
        (me, mine, lax.ppermute(other, "c", swap)),
        square,
        1,
    )
    pieces = lax.all_to_all(pieces, "z", 0, 0, tiled=True)
    (spread,) = call(
        functools.partial(total_kernel, scaling), "total", [shape((xs * zs, own, piece), bf16)], (pieces,)
    )
    spread = lax.all_to_all(spread, ("x", "z"), 0, 0, tiled=True)
    joined_grad, output_grad = call(
        result_kernel,
        "result",
        [shape((width // lanes, 4 * width), f32), shape((width // lanes, width), f32)],
        (spread.reshape(xs, zs, own, piece), token),
    )
    return (row_grad, joined_grad, output_grad)


def solution(mesh):
    torus = Mesh(mesh.devices.reshape(4, 12, 8, 2), ("x", "z", "y", "c"))
    everywhere = P(("x", "z", "y", "c"), None)
    return jax.shard_map(
        on_device,
        mesh=torus,
        in_specs=(everywhere,) * 7 + (P(), P()),
        out_specs=(everywhere, P(("y", "c"), None), P(("y", "c"), None)),
        check_vma=False,
    )
```

```python
import functools
import math

import jax
import jax.numpy as jnp
from jax import lax
from jax.experimental import pallas as pl
from jax.experimental.pallas import tpu as pltpu
from jax.sharding import Mesh, PartitionSpec as P

HEADS = 8
WIN = 128
epsilon = 1e-05
f32 = jnp.float32
bf16 = jnp.bfloat16
VMEM_LIMIT = 16 * 1024 * 1024
VMEM_MOST = 60 * 1024 * 1024
NT = (((1,), (1,)), ((), ()))
TN = (((0,), (0,)), ((), ()))


def dot(a, b, dims=(((1,), (0,)), ((), ()))):
    return lax.dot_general(a, b, dims, preferred_element_type=f32)


def row_norm(features):
    centred = features - jnp.mean(features, axis=-1, keepdims=True)
    spread = jnp.mean(centred * centred, axis=-1, keepdims=True)
    inverse = lax.rsqrt(spread + epsilon)
    return centred * inverse, inverse


def row_norm_back(cot, normed, inverse):
    mean_cot = jnp.mean(cot, axis=-1, keepdims=True)
    mean_both = jnp.mean(cot * normed, axis=-1, keepdims=True)
    return inverse * (cot - mean_cot - normed * mean_both)


def as_column(row, diagonal):
    return jnp.sum(jnp.where(diagonal, row, 0.0), axis=1, keepdims=True)


def forward_body(
    rows_ref,
    seg_ref,
    valid_ref,
    weight_ref,
    normed_ref,
    inverse_ref,
    active_ref,
    slope_ref,
    weighting_ref,
    score_slope_ref,
    mixed_ref,
    mix_inverse_ref,
    gated_ref,
):
    rows, width = rows_ref.shape
    head = width // HEADS
    pair = 2 * head
    normed, inverse = row_norm(rows_ref[...].astype(f32))
    normed = normed.astype(bf16)
    normed_ref[...] = normed
    inverse_ref[...] = inverse
    for quarter in range(4):
        columns = slice(quarter * width, (quarter + 1) * width)
        projected = dot(normed, weight_ref[:, columns])
        gate = jax.nn.sigmoid(projected)
        active_ref[:, columns] = (projected * gate).astype(bf16)
        slope_ref[:, columns] = (gate * (1.0 + projected * (1.0 - gate))).astype(bf16)
    left = lax.broadcasted_iota(jnp.int32, (WIN, pair), 1) < head
    place_i = lax.broadcasted_iota(jnp.int32, (WIN, WIN), 0)
    place_j = lax.broadcasted_iota(jnp.int32, (WIN, WIN), 1)
    zero = jnp.zeros((), bf16)

    def stacked(block):
        return jnp.concatenate([jnp.where(left, block, zero), jnp.where(left, zero, block)], axis=0)

    for window in range(rows // WIN):
        span = slice(window * WIN, (window + 1) * WIN)
        seg_row = seg_ref[:, span].astype(f32)
        seg_col = as_column(seg_row, place_i == place_j)
        allowed = (seg_col == seg_row) & (place_j <= place_i) & (valid_ref[:, span] == 1)
        allowed = jnp.where(allowed, 1.0, 0.0)
        weights = allowed / jnp.maximum(jnp.sum(allowed, axis=1, keepdims=True), 1.0)
        weights = jnp.concatenate([weights, weights], axis=1)
        mixture, kept = [], []
        for p in range(HEADS // 2):
            at = p * pair
            value = active_ref[span, width + at : width + at + pair]
            query = active_ref[span, 2 * width + at : 2 * width + at + pair]
            key = active_ref[span, 3 * width + at : 3 * width + at + pair]
            scores = dot(query, stacked(key), NT) * head**-0.5
            gate = jax.nn.sigmoid(scores)
            weighting = (scores * gate * weights).astype(bf16)
            slope = gate * (1.0 + scores * (1.0 - gate)) * (weights * head**-0.5)
            kept.append((weighting, slope.astype(bf16)))
            mixture.append(dot(weighting, stacked(value)))
        for p, (weighting, slope) in enumerate(kept):
            slot = window * (HEADS // 2) + p
            weighting_ref[slot] = weighting
            score_slope_ref[slot] = slope
        mixed, mix_inverse = row_norm(jnp.concatenate(mixture, axis=1))
        mixed_ref[span, :] = mixed
        mix_inverse_ref[span, :] = mix_inverse
        gated_ref[span, :] = (mixed * active_ref[span, :width].astype(f32)).astype(bf16)


def backward_body(
    cot_ref,
    valid_ref,
    out_weight_ref,
    normed_ref,
    active_ref,
    slope_ref,
    weighting_ref,
    score_slope_ref,
    mixed_ref,
    mix_inverse_ref,
    gated_ref,
    proj_cot_ref,
    masked_ref,
    normed_t_ref,
    gated_t_ref,
    spread,
    send,
):
    rows, width = cot_ref.shape
    head = width // HEADS
    pair = 2 * head
    place_i = lax.broadcasted_iota(jnp.int32, (rows, rows), 0)
    place_j = lax.broadcasted_iota(jnp.int32, (rows, rows), 1)
    valid_col = as_column(valid_ref[...].astype(f32), place_i == place_j)
    masked = (cot_ref[...].astype(f32) * valid_col).astype(bf16)
    masked_ref[...] = masked
    side = width // 2
    gated_t = permute(spread, gated_ref[...], NT)
    gated_t_ref[...] = gated_t[:side]
    send(4, permute(gated_t[side:], masked))
    normed_t = permute(spread, normed_ref[...], NT)
    normed_t_ref[...] = normed_t[:side]
    gated_cot = dot(masked, out_weight_ref[...], NT)
    mixed = mixed_ref[...]
    gate_cot = (gated_cot * mixed).astype(bf16).astype(f32)
    proj_cot_ref[:, :width] = (gate_cot * slope_ref[:, :width].astype(f32)).astype(bf16)
    send(0, permute(normed_t[side:], proj_cot_ref[:, :width]))
    mixture_cot = row_norm_back(
        gated_cot * active_ref[:, :width].astype(f32), mixed, mix_inverse_ref[...]
    ).astype(bf16)
    left = lax.broadcasted_iota(jnp.int32, (WIN, pair), 1) < head
    zero = jnp.zeros((), bf16)

    def stacked(block):
        return jnp.concatenate([jnp.where(left, block, zero), jnp.where(left, zero, block)], axis=0)

    def folded(block):
        return jnp.where(left, block[:WIN], block[WIN:])

    for window in range(rows // WIN):
        span = slice(window * WIN, (window + 1) * WIN)
        cots = []
        for p in range(HEADS // 2):
            at = p * pair
            slot = window * (HEADS // 2) + p
            value = active_ref[span, width + at : width + at + pair]
            query = active_ref[span, 2 * width + at : 2 * width + at + pair]
            key = active_ref[span, 3 * width + at : 3 * width + at + pair]
            mix_cot = mixture_cot[span, at : at + pair]
            weighting_cot = dot(mix_cot, stacked(value), NT).astype(bf16).astype(f32)
            score_cot = (weighting_cot * score_slope_ref[slot].astype(f32)).astype(bf16)
            value_cot = folded(dot(weighting_ref[slot], mix_cot, TN))
            query_cot = dot(score_cot, stacked(key))
            key_cot = folded(dot(score_cot, query, TN))
            for quarter, cot in ((1, value_cot), (2, query_cot), (3, key_cot)):
                columns = slice(quarter * width + at, quarter * width + at + pair)
                slope = slope_ref[span, columns].astype(f32)
                cots.append((columns, (cot.astype(bf16).astype(f32) * slope).astype(bf16)))
        for columns, cot in cots:
            proj_cot_ref[span, columns] = cot
    for quarter in range(1, 4):
        columns = slice(quarter * width, (quarter + 1) * width)
        send(quarter, permute(normed_t[side:], proj_cot_ref[:, columns]))


def permute(order, block, dims=(((1,), (0,)), ((), ()))):
    return dot(order, block, dims).astype(bf16)


def pack_kernel(lanes, dest_ref, me_ref, own_x_ref, rows_hbm, cot_hbm, out_ref, rows_ref, cot_ref, sems):
    del me_ref, own_x_ref
    copies = [
        pltpu.make_async_copy(rows_hbm, rows_ref, sems.at[0]),
        pltpu.make_async_copy(cot_hbm, cot_ref, sems.at[1]),
    ]
    for copy in copies:
        copy.start()
    rows, width = rows_ref.shape
    blocks = dest_ref.shape[1]
    units = lanes * blocks
    halves = rows // units
    place = lax.broadcasted_iota(jnp.int32, (units, 1), 0)
    loaded = lax.broadcasted_iota(jnp.int32, (units, rows), 1)
    orders = []
    for r in range(halves):
        source = place % blocks * (rows // blocks) + r * lanes + place // blocks
        orders.append(jnp.where(source == loaded, 1.0, 0.0).astype(bf16))
    extra = out_ref.shape[1] - 2 * halves * width
    block = lax.broadcasted_iota(jnp.int32, (units, extra), 0) % blocks
    dest = jnp.zeros((units, extra), f32)
    for j in range(blocks):
        dest = jnp.where(block == j, dest_ref[0, j].astype(f32), dest)
    out_ref[:, 2 * halves * width :] = dest.astype(bf16)
    for k, block_ref in enumerate((rows_ref, cot_ref)):
        copies[k].wait()
        for r in range(halves):
            at = (2 * r + k) * width
            out_ref[:, at : at + width] = permute(orders[r], block_ref[...])


def route_kernel(lanes, in_ref, out_ref, order_ref):
    units, payload = out_ref.shape
    blocks = units // lanes
    extra = in_ref.shape[1] - payload
    place = lax.broadcasted_iota(jnp.int32, (units, units), 0)
    other = lax.broadcasted_iota(jnp.int32, (units, units), 1)
    lane = lax.broadcasted_iota(jnp.int32, (units, extra), 1)
    dest = in_ref[:, payload:].astype(f32)
    chosen = jnp.where(dest == lane.astype(f32), 1.0, 0.0)
    earlier = jnp.where(other < place, 1.0, 0.0).astype(bf16)
    rank = jnp.sum(dot(earlier, chosen.astype(bf16)) * chosen, axis=1, keepdims=True)
    target = dest[:, :1] * blocks + rank
    order = jnp.where(target == other.astype(f32), 1.0, 0.0).astype(bf16)
    order_ref[...] = order
    out_ref[...] = permute(order, in_ref[:, :payload], TN)


def slots_of(sources_ref, offsets_ref):
    blocks = sources_ref.shape[1]
    keys = [sources_ref[0, t] * 2 + offsets_ref[0, t] for t in range(blocks)]
    return [
        sum(jnp.where(keys[u] < keys[t], 1, 0) for u in range(blocks) if u != t) for t in range(blocks)
    ]


def gather_order(lanes, sources_ref, offsets_ref, order_ref):
    units = order_ref.shape[0]
    blocks = sources_ref.shape[1]
    inside = lax.broadcasted_iota(jnp.int32, (lanes, 1), 0)
    column = lax.broadcasted_iota(jnp.int32, (lanes, units), 1)
    for t, slot in enumerate(slots_of(sources_ref, offsets_ref)):
        order = jnp.where(column == inside * blocks + slot, 1.0, 0.0)
        order_ref[t * lanes : (t + 1) * lanes, :] = order.astype(bf16)


def spread_order(parts, core, own_x, width):
    xs, ys = parts
    out = lax.broadcasted_iota(jnp.int32, (width, 1), 0)
    column = lax.broadcasted_iota(jnp.int32, (width, width), 1)
    side = width // 2
    block = width // ys // 2
    piece = block // xs
    y = out // piece % ys
    x = out % side // (piece * ys) ^ own_x
    parity = (out // side + core) % 2
    source = y * (2 * block) + parity * block + x * piece + out % piece
    return jnp.where(source == column, 1.0, 0.0).astype(bf16)


def layer_kernel(
    lanes,
    parts,
    me_ref,
    own_x_ref,
    sources_ref,
    offsets_ref,
    in_ref,
    seg_ref,
    valid_ref,
    weight_ref,
    out_weight_ref,
    send_ref,
    proj_cot_ref,
    normed_t_ref,
    gated_t_ref,
    masked_ref,
    rows_ref,
    inverse_ref,
    order_ref,
    cot_ref,
    normed_ref,
    active_ref,
    slope_ref,
    weighting_ref,
    score_slope_ref,
    mixed_ref,
    mix_inverse_ref,
    gated_ref,
    held_ref,
    sems,
):
    width = rows_ref.shape[1]
    copies = []

    def send(quarter, grad):
        columns = slice(quarter * width, (quarter + 1) * width)
        held_ref[:, columns] = grad
        copies.append(
            pltpu.make_async_copy(held_ref.at[:, columns], send_ref.at[:, columns], sems.at[quarter])
        )
        copies[-1].start()

    gather_order(lanes, sources_ref, offsets_ref, order_ref)
    halves = in_ref.shape[1] // (2 * width)
    for k, block_ref in enumerate((rows_ref, cot_ref)):
        for r in range(halves):
            at = (2 * r + k) * width
            block = permute(order_ref[...], in_ref[:, at : at + width])
            for t in range(order_ref.shape[0] // lanes):
                to = (t * halves + r) * lanes
                block_ref[to : to + lanes, :] = block[t * lanes : (t + 1) * lanes]
    stored = (
        active_ref,
        slope_ref,
        weighting_ref,
        score_slope_ref,
        mixed_ref,
        mix_inverse_ref,
        gated_ref,
    )
    forward_body(rows_ref, seg_ref, valid_ref, weight_ref, normed_ref, inverse_ref, *stored)
    backward_body(
        cot_ref,
        valid_ref,
        out_weight_ref,
        normed_ref,
        *stored,
        proj_cot_ref,
        masked_ref,
        normed_t_ref,
        gated_t_ref,
        spread_order(parts, me_ref[0] % 2, own_x_ref[0], width),
        send,
    )
    for copy in copies:
        copy.wait()


def finish_kernel(
    lanes,
    weight_ref,
    proj_cot_ref,
    normed_t_ref,
    gated_t_ref,
    masked_ref,
    rows_ref,
    inverse_ref,
    order_ref,
    leave_ref,
    *keep_refs,
):
    rows, width = rows_ref.shape

    def put(grad, columns):
        size = keep_refs[0].shape[0]
        for k, keep_ref in enumerate(keep_refs):
            keep_ref[:, columns] = grad[k * size : (k + 1) * size]

    normed_cot = jnp.zeros((rows, width), f32)
    for quarter in range(4):
        columns = slice(quarter * width, (quarter + 1) * width)
        proj_cot = proj_cot_ref[:, columns]
        normed_cot += dot(proj_cot, weight_ref[:, columns], NT)
        put(permute(normed_t_ref[...], proj_cot), columns)
    masked = masked_ref[...]
    put(permute(gated_t_ref[...], masked), slice(4 * width, 5 * width))
    features = rows_ref[...].astype(f32)
    inverse = inverse_ref[...]
    normed_f = (features - jnp.mean(features, axis=-1, keepdims=True)) * inverse
    rows_cot = row_norm_back(normed_cot, normed_f, inverse)
    work_grad = (masked.astype(f32) + rows_cot).astype(bf16)
    units = order_ref.shape[0]
    halves = rows // units
    for r in range(halves):
        parts = [
            work_grad[(t * halves + r) * lanes : (t * halves + r + 1) * lanes]
            for t in range(units // lanes)
        ]
        grad = permute(order_ref[...], jnp.concatenate(parts, axis=0), TN)
        leave_ref[:, r * width : (r + 1) * width] = grad


def add_kernel(arrived_ref, *refs):
    keep_refs, out_refs = refs[: len(refs) // 2], refs[len(refs) // 2 :]
    for k, out_ref in enumerate(out_refs):
        span = slice(k * out_ref.shape[0], (k + 1) * out_ref.shape[0])
        out_ref[...] = keep_refs[k][...] + arrived_ref[span, :]


def merge_kernel(order_ref, back_ref, *refs):
    *part_refs, out_ref = refs
    ys, own, _ = out_ref.shape
    total = part_refs[0].shape[1]
    partial = sum(part_ref[...].astype(f32) for part_ref in part_refs)
    out_ref[:, :, :total] = partial.reshape(ys, own, total).astype(bf16)
    units, width = back_ref.shape
    groups = units // (ys * own)
    back = dot(order_ref[...], back_ref[...]).reshape(ys, groups, own, width)
    for g in range(groups):
        at = total + g * width
        out_ref[:, :, at : at + width] = back[:, g].astype(bf16)


def fold_kernel(me_ref, in_ref, out_ref, mine_ref, other_ref):
    pieces, own, piece = out_ref.shape
    ys = in_ref.shape[0]
    width = mine_ref.shape[1]
    halves = mine_ref.shape[0] // (ys * own)
    total = in_ref.shape[2] - 2 * halves * width
    folded = jnp.sum(in_ref[:, :, :total].astype(f32), axis=0).astype(bf16)
    for k in range(pieces):
        at, end = k * piece, min((k + 1) * piece, total)
        if at < total:
            out_ref[k, :, : end - at] = folded[:, at:end]
        if end - at < piece:
            rest = max(end - at, 0)
            out_ref[k, :, rest:] = jnp.zeros((own, piece - rest), bf16)
    first = me_ref[0] % 2 == 0
    for r in range(halves):
        span = slice(r * ys * own, (r + 1) * ys * own)
        sets = []
        for g in (r, halves + r):
            at = total + g * width
            sets.append(in_ref[:, :, at : at + width].astype(f32).reshape(ys * own, width))
        mine_ref[span, :] = jnp.where(first, sets[0], sets[1]).astype(bf16)
        other_ref[span, :] = jnp.where(first, sets[1], sets[0]).astype(bf16)


def unpack_kernel(lanes, blocks, me_ref, mine_ref, arrived_ref, out_ref, token_ref):
    token_ref[...] = jnp.zeros_like(token_ref)
    rows = out_ref.shape[0]
    side = rows // 2
    out = lax.broadcasted_iota(jnp.int32, (rows, 1), 0)
    column = lax.broadcasted_iota(jnp.int32, (rows, rows), 1)
    block = out // (rows // blocks)
    half = out // lanes % (rows // blocks // lanes)
    piece = out % lanes
    place = half * (blocks * lanes // 2) + piece // 2 * blocks + block
    place += (piece + me_ref[0]) % 2 * side
    order = jnp.where(place == column, 1.0, 0.0).astype(bf16)
    got = dot(order[:, :side], mine_ref[...]) + dot(order[:, side:], arrived_ref[...])
    out_ref[...] = got.astype(bf16)


def total_kernel(scaling, in_ref, out_ref):
    total = jnp.sum(in_ref[...].astype(f32), axis=0, keepdims=True) * scaling
    out_ref[...] = jnp.broadcast_to(total.astype(bf16), out_ref.shape)


def result_kernel(in_ref, after_ref, joined_ref, output_ref):
    del after_ref
    xs, zs, piece_rows, piece = in_ref.shape
    split = joined_ref.shape[1]
    step = math.gcd(piece, split)
    for x in range(xs):
        span = slice(x * piece_rows, (x + 1) * piece_rows)
        for at in range(0, split + output_ref.shape[1], step):
            block = in_ref[x, at // piece, :, at % piece : at % piece + step].astype(f32)
            if at < split:
                joined_ref[span, at : at + step] = block
            else:
                output_ref[span, at - split : at - split + step] = block


def call(kernel, name, out_shape, operands, flops=0, scalars=0, scratch=(), unmoved=0, aliases=None, loose=0):
    moved = sum(math.prod(a.shape) * a.dtype.itemsize for a in (*operands, *out_shape))
    smem = pl.BlockSpec(memory_space=pltpu.SMEM)
    vmem = pl.BlockSpec(memory_space=pltpu.VMEM)
    stay = pl.BlockSpec(memory_space=pl.ANY)
    blocked = len(operands) - scalars - unmoved
    return pl.pallas_call(
        kernel,
        out_shape=tuple(out_shape),
        in_specs=[smem] * scalars + [vmem] * blocked + [stay] * unmoved,
        out_specs=tuple(stay if k < loose else vmem for k in range(len(out_shape))),
        scratch_shapes=list(scratch),
        input_output_aliases=aliases or {},
        compiler_params=pltpu.CompilerParams(vmem_limit_bytes=VMEM_MOST if unmoved else VMEM_LIMIT),
        cost_estimate=pl.CostEstimate(flops=flops, bytes_accessed=moved, transcendentals=0),
        name=name,
    )(*operands)


def on_device(
    history_rows,
    cotangent,
    dest_device,
    source_device,
    source_offset,
    segments,
    row_valid,
    joined_weight,
    output_weight,
):
    shape = jax.ShapeDtypeStruct
    xs, zs, ys = lax.axis_size("x"), lax.axis_size("z"), lax.axis_size("y")
    lanes = ys * lax.axis_size("c")
    rows, width = history_rows.shape
    blocks = dest_device.shape[1]
    me = lax.axis_index(("y", "c")).astype(jnp.int32).reshape(1)
    own_x = lax.axis_index("x").astype(jnp.int32).reshape(1)
    scaling = 1.0 / math.sqrt(rows * lanes * xs * zs)

    def exchange(block):
        chunks = block.reshape(lanes, blocks, block.shape[1])
        return lax.all_to_all(chunks, ("y", "c"), 0, 0, tiled=True).reshape(block.shape)

    units = lanes * blocks
    halves = rows // units
    square = 2 * rows * units * width
    (packed,) = call(
        functools.partial(pack_kernel, lanes),
        "pack",
        [shape((units, 2 * halves * width + 128), bf16)],
        (dest_device, me, own_x, history_rows, cotangent),
        2 * square,
        3,
        (
            pltpu.VMEM((rows, width), bf16),
            pltpu.VMEM((rows, width), bf16),
            pltpu.SemaphoreType.DMA((2,)),
        ),
        2,
    )
    routed, route = call(
        functools.partial(route_kernel, lanes),
        "route",
        [shape((units, 2 * halves * width), bf16), shape((units, units), bf16)],
        (exchange(packed),),
        2 * square,
    )
    slots = rows // WIN * HEADS // 2
    total = width * 5
    vmem = pltpu.VMEM
    side = width // 2
    send, *stored = call(
        functools.partial(layer_kernel, lanes, (xs, ys)),
        "layer",
        [
            shape((side, total), bf16),
            shape((rows, 4 * width), bf16),
            shape((side, rows), bf16),
            shape((side, rows), bf16),
            shape((rows, width), bf16),
            shape((rows, width), bf16),
            shape((rows, 1), f32),
            shape((units, units), bf16),
        ],
        (
            me,
            own_x,
            source_device,
            source_offset,
            exchange(routed),
            segments,
            row_valid,
            joined_weight,
            output_weight,
        ),
        2 * rows * width * width * 10,
        4,
        (
            vmem((rows, width), bf16),
            vmem((rows, width), bf16),
            vmem((rows, 4 * width), bf16),
            vmem((rows, 4 * width), bf16),
            vmem((slots, WIN, 2 * WIN), bf16),
            vmem((slots, WIN, 2 * WIN), bf16),
            vmem((rows, width), f32),
            vmem((rows, 1), f32),
            vmem((rows, width), bf16),
            vmem((side, total), bf16),
            pltpu.SemaphoreType.DMA((5,)),
        ),
        loose=1,
    )
    own = width // (lanes * xs)
    quarters = [shape((ys * own, total), bf16)] * xs
    leaving, *keep = call(
        functools.partial(finish_kernel, lanes),
        "finish",
        [shape((units, halves * width), bf16)] + quarters,
        (joined_weight, *stored),
        2 * rows * width * width * 8,
    )
    swap = [(0, 1), (1, 0)]
    arrived = lax.ppermute(send, "c", swap)
    parts = call(
        add_kernel, "add", quarters, (arrived, *keep), aliases={k + 1: k for k in range(xs)}
    )
    arriving = {
        k: lax.ppermute(parts[k], "x", [(i, i ^ k) for i in range(xs)]) for k in sorted(range(1, xs), key=lambda k: (-(k & 2), k & 1))
    }
    parts = [parts[0], *arriving.values()]
    (merged,) = call(
        merge_kernel,
        "merge",
        [shape((ys, own, total + rows // (ys * own) * width), bf16)],
        (route, exchange(leaving), *parts),
        square,
    )
    merged = lax.all_to_all(merged, "y", 0, 0, tiled=True)
    piece = -(-total // (zs * 128)) * 128
    pieces, mine, other = call(
        fold_kernel,
        "fold",
        [shape((zs, own, piece), bf16)] + [shape((rows // 2, width), bf16)] * 2,
        (me, merged),
        0,
        1,
    )
    row_grad, token = call(
        functools.partial(unpack_kernel, lanes, blocks),
        "unpack",
        [shape((rows, width), bf16), shape((8, 128), f32)],
        (me, mine, lax.ppermute(other, "c", swap)),
        square,
        1,
    )
    pieces = lax.all_to_all(pieces, "z", 0, 0, tiled=True)
    (spread,) = call(
        functools.partial(total_kernel, scaling), "total", [shape((xs * zs, own, piece), bf16)], (pieces,)
    )
    spread = lax.all_to_all(spread, ("x", "z"), 0, 0, tiled=True)
    joined_grad, output_grad = call(
        result_kernel,
        "result",
        [shape((width // lanes, 4 * width), f32), shape((width // lanes, width), f32)],
        (spread.reshape(xs, zs, own, piece), token),
    )
    return (row_grad, joined_grad, output_grad)


def solution(mesh):
    torus = Mesh(mesh.devices.reshape(4, 12, 8, 2), ("x", "z", "y", "c"))
    everywhere = P(("x", "z", "y", "c"), None)
    return jax.shard_map(
        on_device,
        mesh=torus,
        in_specs=(everywhere,) * 7 + (P(), P()),
        out_specs=(everywhere, P(("y", "c"), None), P(("y", "c"), None)),
        check_vma=False,
    )
```

```python
import functools
import math

import jax
import jax.numpy as jnp
from jax import lax
from jax.experimental import pallas as pl
from jax.experimental.pallas import tpu as pltpu
from jax.sharding import Mesh, PartitionSpec as P

HEADS = 8
WIN = 128
epsilon = 1e-05
f32 = jnp.float32
bf16 = jnp.bfloat16
VMEM_LIMIT = 16 * 1024 * 1024
VMEM_MOST = 60 * 1024 * 1024
NT = (((1,), (1,)), ((), ()))
TN = (((0,), (0,)), ((), ()))


def dot(a, b, dims=(((1,), (0,)), ((), ()))):
    return lax.dot_general(a, b, dims, preferred_element_type=f32)


def row_norm(features):
    centred = features - jnp.mean(features, axis=-1, keepdims=True)
    spread = jnp.mean(centred * centred, axis=-1, keepdims=True)
    inverse = lax.rsqrt(spread + epsilon)
    return centred * inverse, inverse


def row_norm_back(cot, normed, inverse):
    mean_cot = jnp.mean(cot, axis=-1, keepdims=True)
    mean_both = jnp.mean(cot * normed, axis=-1, keepdims=True)
    return inverse * (cot - mean_cot - normed * mean_both)


def as_column(row, diagonal):
    return jnp.sum(jnp.where(diagonal, row, 0.0), axis=1, keepdims=True)


def forward_body(
    rows_ref,
    seg_ref,
    valid_ref,
    weight_ref,
    normed_ref,
    inverse_ref,
    active_ref,
    slope_ref,
    weighting_ref,
    score_slope_ref,
    mixed_ref,
    mix_inverse_ref,
    gated_ref,
):
    rows, width = rows_ref.shape
    head = width // HEADS
    pair = 2 * head
    normed, inverse = row_norm(rows_ref[...].astype(f32))
    normed = normed.astype(bf16)
    normed_ref[...] = normed
    inverse_ref[...] = inverse
    for quarter in range(4):
        columns = slice(quarter * width, (quarter + 1) * width)
        projected = dot(normed, weight_ref[:, columns])
        gate = jax.nn.sigmoid(projected)
        active_ref[:, columns] = (projected * gate).astype(bf16)
        slope_ref[:, columns] = (gate * (1.0 + projected * (1.0 - gate))).astype(bf16)
    left = lax.broadcasted_iota(jnp.int32, (WIN, pair), 1) < head
    place_i = lax.broadcasted_iota(jnp.int32, (WIN, WIN), 0)
    place_j = lax.broadcasted_iota(jnp.int32, (WIN, WIN), 1)
    zero = jnp.zeros((), bf16)

    def stacked(block):
        return jnp.concatenate([jnp.where(left, block, zero), jnp.where(left, zero, block)], axis=0)

    for window in range(rows // WIN):
        span = slice(window * WIN, (window + 1) * WIN)
        seg_row = seg_ref[:, span].astype(f32)
        seg_col = as_column(seg_row, place_i == place_j)
        allowed = (seg_col == seg_row) & (place_j <= place_i) & (valid_ref[:, span] == 1)
        allowed = jnp.where(allowed, 1.0, 0.0)
        weights = allowed / jnp.maximum(jnp.sum(allowed, axis=1, keepdims=True), 1.0)
        weights = jnp.concatenate([weights, weights], axis=1)
        pairs = [slice(p * pair, (p + 1) * pair) for p in range(HEADS // 2)]
        values, queries, keys = (
            [active_ref[span, k * width + at.start : k * width + at.stop] for at in pairs]
            for k in (1, 2, 3)
        )
        scores = [dot(query, stacked(key), NT) * head**-0.5 for query, key in zip(queries, keys)]
        gates = [jax.nn.sigmoid(score) for score in scores]
        weightings = [
            (score * gate * weights).astype(bf16) for score, gate in zip(scores, gates)
        ]
        mixture = [
            dot(weighting, stacked(value)) for weighting, value in zip(weightings, values)
        ]
        for p, (score, gate) in enumerate(zip(scores, gates)):
            slot = window * (HEADS // 2) + p
            weighting_ref[slot] = weightings[p]
            slope = gate * (1.0 + score * (1.0 - gate)) * (weights * head**-0.5)
            score_slope_ref[slot] = slope.astype(bf16)
        mixed, mix_inverse = row_norm(jnp.concatenate(mixture, axis=1))
        mixed_ref[span, :] = mixed
        mix_inverse_ref[span, :] = mix_inverse
        gated_ref[span, :] = (mixed * active_ref[span, :width].astype(f32)).astype(bf16)


def backward_body(
    cot_ref,
    valid_ref,
    out_weight_ref,
    normed_ref,
    active_ref,
    slope_ref,
    weighting_ref,
    score_slope_ref,
    mixed_ref,
    mix_inverse_ref,
    gated_ref,
    proj_cot_ref,
    masked_ref,
    normed_t_ref,
    gated_t_ref,
    spread,
    send,
):
    rows, width = cot_ref.shape
    head = width // HEADS
    pair = 2 * head
    place_i = lax.broadcasted_iota(jnp.int32, (rows, rows), 0)
    place_j = lax.broadcasted_iota(jnp.int32, (rows, rows), 1)
    valid_col = as_column(valid_ref[...].astype(f32), place_i == place_j)
    masked = (cot_ref[...].astype(f32) * valid_col).astype(bf16)
    masked_ref[...] = masked
    side = width // 2
    gated_t = permute(spread, gated_ref[...], NT)
    gated_t_ref[...] = gated_t[:side]
    send(4, permute(gated_t[side:], masked))
    normed_t = permute(spread, normed_ref[...], NT)
    normed_t_ref[...] = normed_t[:side]
    gated_cot = dot(masked, out_weight_ref[...], NT)
    mixed = mixed_ref[...]
    gate_cot = (gated_cot * mixed).astype(bf16).astype(f32)
    proj_cot_ref[:, :width] = (gate_cot * slope_ref[:, :width].astype(f32)).astype(bf16)
    send(0, permute(normed_t[side:], proj_cot_ref[:, :width]))
    mixture_cot = row_norm_back(
        gated_cot * active_ref[:, :width].astype(f32), mixed, mix_inverse_ref[...]
    ).astype(bf16)
    left = lax.broadcasted_iota(jnp.int32, (WIN, pair), 1) < head
    zero = jnp.zeros((), bf16)

    def stacked(block):
        return jnp.concatenate([jnp.where(left, block, zero), jnp.where(left, zero, block)], axis=0)

    def folded(block):
        return jnp.where(left, block[:WIN], block[WIN:])

    for window in range(rows // WIN):
        span = slice(window * WIN, (window + 1) * WIN)
        cots = []
        pairs = [slice(p * pair, (p + 1) * pair) for p in range(HEADS // 2)]
        values, queries, keys = (
            [active_ref[span, k * width + at.start : k * width + at.stop] for at in pairs]
            for k in (1, 2, 3)
        )
        mix_cots = [mixture_cot[span, at] for at in pairs]
        first = window * (HEADS // 2)
        score_cots = []
        for p in range(HEADS // 2):
            weighting_cot = dot(mix_cots[p], stacked(values[p]), NT).astype(bf16).astype(f32)
            score_cots.append((weighting_cot * score_slope_ref[first + p].astype(f32)).astype(bf16))
        value_cots = [
            folded(dot(weighting_ref[first + p], mix_cots[p], TN)) for p in range(HEADS // 2)
        ]
        query_cots = [dot(score_cots[p], stacked(keys[p])) for p in range(HEADS // 2)]
        key_cots = [folded(dot(score_cots[p], queries[p], TN)) for p in range(HEADS // 2)]
        for quarter, parts in ((1, value_cots), (2, query_cots), (3, key_cots)):
            for at, cot in zip(pairs, parts):
                columns = slice(quarter * width + at.start, quarter * width + at.stop)
                slope = slope_ref[span, columns].astype(f32)
                cots.append((columns, (cot.astype(bf16).astype(f32) * slope).astype(bf16)))
        for columns, cot in cots:
            proj_cot_ref[span, columns] = cot
    for quarter in range(1, 4):
        columns = slice(quarter * width, (quarter + 1) * width)
        send(quarter, permute(normed_t[side:], proj_cot_ref[:, columns]))


def permute(order, block, dims=(((1,), (0,)), ((), ()))):
    return dot(order, block, dims).astype(bf16)


def pack_kernel(lanes, dest_ref, me_ref, own_x_ref, rows_hbm, cot_hbm, out_ref, rows_ref, cot_ref, sems):
    del me_ref, own_x_ref
    copies = [
        pltpu.make_async_copy(rows_hbm, rows_ref, sems.at[0]),
        pltpu.make_async_copy(cot_hbm, cot_ref, sems.at[1]),
    ]
    for copy in copies:
        copy.start()
    rows, width = rows_ref.shape
    blocks = dest_ref.shape[1]
    units = lanes * blocks
    halves = rows // units
    place = lax.broadcasted_iota(jnp.int32, (units, 1), 0)
    loaded = lax.broadcasted_iota(jnp.int32, (units, rows), 1)
    orders = []
    for r in range(halves):
        source = place % blocks * (rows // blocks) + r * lanes + place // blocks
        orders.append(jnp.where(source == loaded, 1.0, 0.0).astype(bf16))
    extra = out_ref.shape[1] - 2 * halves * width
    block = lax.broadcasted_iota(jnp.int32, (units, extra), 0) % blocks
    dest = jnp.zeros((units, extra), f32)
    for j in range(blocks):
        dest = jnp.where(block == j, dest_ref[0, j].astype(f32), dest)
    out_ref[:, 2 * halves * width :] = dest.astype(bf16)
    for k, block_ref in enumerate((rows_ref, cot_ref)):
        copies[k].wait()
        for r in range(halves):
            at = (2 * r + k) * width
            out_ref[:, at : at + width] = permute(orders[r], block_ref[...])


def route_kernel(lanes, in_ref, out_ref, order_ref):
    units, payload = out_ref.shape
    blocks = units // lanes
    extra = in_ref.shape[1] - payload
    place = lax.broadcasted_iota(jnp.int32, (units, units), 0)
    other = lax.broadcasted_iota(jnp.int32, (units, units), 1)
    lane = lax.broadcasted_iota(jnp.int32, (units, extra), 1)
    dest = in_ref[:, payload:].astype(f32)
    chosen = jnp.where(dest == lane.astype(f32), 1.0, 0.0)
    earlier = jnp.where(other < place, 1.0, 0.0).astype(bf16)
    rank = jnp.sum(dot(earlier, chosen.astype(bf16)) * chosen, axis=1, keepdims=True)
    target = dest[:, :1] * blocks + rank
    order = jnp.where(target == other.astype(f32), 1.0, 0.0).astype(bf16)
    order_ref[...] = order
    out_ref[...] = permute(order, in_ref[:, :payload], TN)


def slots_of(sources_ref, offsets_ref):
    blocks = sources_ref.shape[1]
    keys = [sources_ref[0, t] * 2 + offsets_ref[0, t] for t in range(blocks)]
    return [
        sum(jnp.where(keys[u] < keys[t], 1, 0) for u in range(blocks) if u != t) for t in range(blocks)
    ]


def gather_order(lanes, sources_ref, offsets_ref, order_ref):
    units = order_ref.shape[0]
    blocks = sources_ref.shape[1]
    inside = lax.broadcasted_iota(jnp.int32, (lanes, 1), 0)
    column = lax.broadcasted_iota(jnp.int32, (lanes, units), 1)
    for t, slot in enumerate(slots_of(sources_ref, offsets_ref)):
        order = jnp.where(column == inside * blocks + slot, 1.0, 0.0)
        order_ref[t * lanes : (t + 1) * lanes, :] = order.astype(bf16)


def spread_order(parts, core, own_x, width):
    xs, ys = parts
    out = lax.broadcasted_iota(jnp.int32, (width, 1), 0)
    column = lax.broadcasted_iota(jnp.int32, (width, width), 1)
    side = width // 2
    block = width // ys // 2
    piece = block // xs
    y = out // piece % ys
    x = out % side // (piece * ys) ^ own_x
    parity = (out // side + core) % 2
    source = y * (2 * block) + parity * block + x * piece + out % piece
    return jnp.where(source == column, 1.0, 0.0).astype(bf16)


def layer_kernel(
    lanes,
    parts,
    me_ref,
    own_x_ref,
    sources_ref,
    offsets_ref,
    in_ref,
    seg_ref,
    valid_ref,
    weight_ref,
    out_weight_ref,
    send_ref,
    proj_cot_ref,
    normed_t_ref,
    gated_t_ref,
    masked_ref,
    rows_ref,
    inverse_ref,
    order_ref,
    cot_ref,
    normed_ref,
    active_ref,
    slope_ref,
    weighting_ref,
    score_slope_ref,
    mixed_ref,
    mix_inverse_ref,
    gated_ref,
    held_ref,
    sems,
):
    width = rows_ref.shape[1]
    copies = []

    def send(quarter, grad):
        columns = slice(quarter * width, (quarter + 1) * width)
        held_ref[:, columns] = grad
        copies.append(
            pltpu.make_async_copy(held_ref.at[:, columns], send_ref.at[:, columns], sems.at[quarter])
        )
        copies[-1].start()

    gather_order(lanes, sources_ref, offsets_ref, order_ref)
    halves = in_ref.shape[1] // (2 * width)
    for k, block_ref in enumerate((rows_ref, cot_ref)):
        for r in range(halves):
            at = (2 * r + k) * width
            block = permute(order_ref[...], in_ref[:, at : at + width])
            for t in range(order_ref.shape[0] // lanes):
                to = (t * halves + r) * lanes
                block_ref[to : to + lanes, :] = block[t * lanes : (t + 1) * lanes]
    stored = (
        active_ref,
        slope_ref,
        weighting_ref,
        score_slope_ref,
        mixed_ref,
        mix_inverse_ref,
        gated_ref,
    )
    forward_body(rows_ref, seg_ref, valid_ref, weight_ref, normed_ref, inverse_ref, *stored)
    backward_body(
        cot_ref,
        valid_ref,
        out_weight_ref,
        normed_ref,
        *stored,
        proj_cot_ref,
        masked_ref,
        normed_t_ref,
        gated_t_ref,
        spread_order(parts, me_ref[0] % 2, own_x_ref[0], width),
        send,
    )
    for copy in copies:
        copy.wait()


def finish_kernel(
    lanes,
    weight_ref,
    proj_cot_ref,
    normed_t_ref,
    gated_t_ref,
    masked_ref,
    rows_ref,
    inverse_ref,
    order_ref,
    leave_hbm,
    *refs,
):
    *keep_refs, leave_ref, sem = refs
    rows, width = rows_ref.shape

    def put(grad, columns):
        size = keep_refs[0].shape[0]
        for k, keep_ref in enumerate(keep_refs):
            keep_ref[:, columns] = grad[k * size : (k + 1) * size]

    normed_cot = jnp.zeros((rows, width), f32)
    for quarter in range(4):
        columns = slice(quarter * width, (quarter + 1) * width)
        proj_cot = proj_cot_ref[:, columns]
        normed_cot += dot(proj_cot, weight_ref[:, columns], NT)
    masked = masked_ref[...]
    features = rows_ref[...].astype(f32)
    inverse = inverse_ref[...]
    normed_f = (features - jnp.mean(features, axis=-1, keepdims=True)) * inverse
    rows_cot = row_norm_back(normed_cot, normed_f, inverse)
    work_grad = (masked.astype(f32) + rows_cot).astype(bf16)
    units = order_ref.shape[0]
    halves = rows // units
    for r in range(halves):
        parts = [
            work_grad[(t * halves + r) * lanes : (t * halves + r + 1) * lanes]
            for t in range(units // lanes)
        ]
        grad = permute(order_ref[...], jnp.concatenate(parts, axis=0), TN)
        leave_ref[:, r * width : (r + 1) * width] = grad
    copy = pltpu.make_async_copy(leave_ref, leave_hbm, sem)
    copy.start()
    put(permute(gated_t_ref[...], masked), slice(4 * width, 5 * width))
    for quarter in range(4):
        columns = slice(quarter * width, (quarter + 1) * width)
        put(permute(normed_t_ref[...], proj_cot_ref[:, columns]), columns)
    copy.wait()


def add_kernel(arrived_ref, *refs):
    keep_refs, out_refs = refs[: len(refs) // 2], refs[len(refs) // 2 :]
    for k, out_ref in enumerate(out_refs):
        span = slice(k * out_ref.shape[0], (k + 1) * out_ref.shape[0])
        out_ref[...] = keep_refs[k][...] + arrived_ref[span, :]


def merge_kernel(order_ref, back_ref, *refs):
    *part_refs, out_ref = refs
    ys, own, _ = out_ref.shape
    total = part_refs[0].shape[1]
    partial = sum(part_ref[...].astype(f32) for part_ref in part_refs)
    out_ref[:, :, :total] = partial.reshape(ys, own, total).astype(bf16)
    units, width = back_ref.shape
    groups = units // (ys * own)
    back = dot(order_ref[...], back_ref[...]).reshape(ys, groups, own, width)
    for g in range(groups):
        at = total + g * width
        out_ref[:, :, at : at + width] = back[:, g].astype(bf16)


def fold_kernel(me_ref, in_ref, out_ref, mine_ref, other_ref):
    pieces, own, piece = out_ref.shape
    ys = in_ref.shape[0]
    width = mine_ref.shape[1]
    halves = mine_ref.shape[0] // (ys * own)
    total = in_ref.shape[2] - 2 * halves * width
    folded = jnp.sum(in_ref[:, :, :total].astype(f32), axis=0).astype(bf16)
    for k in range(pieces):
        at, end = k * piece, min((k + 1) * piece, total)
        if at < total:
            out_ref[k, :, : end - at] = folded[:, at:end]
        if end - at < piece:
            rest = max(end - at, 0)
            out_ref[k, :, rest:] = jnp.zeros((own, piece - rest), bf16)
    first = me_ref[0] % 2 == 0
    for r in range(halves):
        span = slice(r * ys * own, (r + 1) * ys * own)
        sets = []
        for g in (r, halves + r):
            at = total + g * width
            sets.append(in_ref[:, :, at : at + width].astype(f32).reshape(ys * own, width))
        mine_ref[span, :] = jnp.where(first, sets[0], sets[1]).astype(bf16)
        other_ref[span, :] = jnp.where(first, sets[1], sets[0]).astype(bf16)


def unpack_kernel(lanes, blocks, me_ref, mine_ref, arrived_ref, out_ref, token_ref):
    token_ref[...] = jnp.zeros_like(token_ref)
    rows = out_ref.shape[0]
    side = rows // 2
    out = lax.broadcasted_iota(jnp.int32, (rows, 1), 0)
    column = lax.broadcasted_iota(jnp.int32, (rows, rows), 1)
    block = out // (rows // blocks)
    half = out // lanes % (rows // blocks // lanes)
    piece = out % lanes
    place = half * (blocks * lanes // 2) + piece // 2 * blocks + block
    place += (piece + me_ref[0]) % 2 * side
    order = jnp.where(place == column, 1.0, 0.0).astype(bf16)
    got = dot(order[:, :side], mine_ref[...]) + dot(order[:, side:], arrived_ref[...])
    out_ref[...] = got.astype(bf16)


def total_kernel(scaling, in_ref, out_ref):
    total = jnp.sum(in_ref[...].astype(f32), axis=0, keepdims=True) * scaling
    out_ref[...] = jnp.broadcast_to(total.astype(bf16), out_ref.shape)


def result_kernel(in_ref, after_ref, joined_ref, output_ref):
    del after_ref
    xs, zs, piece_rows, piece = in_ref.shape
    split = joined_ref.shape[1]
    step = math.gcd(piece, split)
    for x in range(xs):
        span = slice(x * piece_rows, (x + 1) * piece_rows)
        for at in range(0, split + output_ref.shape[1], step):
            block = in_ref[x, at // piece, :, at % piece : at % piece + step].astype(f32)
            if at < split:
                joined_ref[span, at : at + step] = block
            else:
                output_ref[span, at - split : at - split + step] = block


def call(kernel, name, out_shape, operands, flops=0, scalars=0, scratch=(), unmoved=0, aliases=None, loose=0):
    moved = sum(math.prod(a.shape) * a.dtype.itemsize for a in (*operands, *out_shape))
    smem = pl.BlockSpec(memory_space=pltpu.SMEM)
    vmem = pl.BlockSpec(memory_space=pltpu.VMEM)
    stay = pl.BlockSpec(memory_space=pl.ANY)
    blocked = len(operands) - scalars - unmoved
    return pl.pallas_call(
        kernel,
        out_shape=tuple(out_shape),
        in_specs=[smem] * scalars + [vmem] * blocked + [stay] * unmoved,
        out_specs=tuple(stay if k < loose else vmem for k in range(len(out_shape))),
        scratch_shapes=list(scratch),
        input_output_aliases=aliases or {},
        compiler_params=pltpu.CompilerParams(vmem_limit_bytes=VMEM_MOST if unmoved else VMEM_LIMIT),
        cost_estimate=pl.CostEstimate(flops=flops, bytes_accessed=moved, transcendentals=0),
        name=name,
    )(*operands)


def on_device(
    history_rows,
    cotangent,
    dest_device,
    source_device,
    source_offset,
    segments,
    row_valid,
    joined_weight,
    output_weight,
):
    shape = jax.ShapeDtypeStruct
    xs, zs, ys = lax.axis_size("x"), lax.axis_size("z"), lax.axis_size("y")
    lanes = ys * lax.axis_size("c")
    rows, width = history_rows.shape
    blocks = dest_device.shape[1]
    me = lax.axis_index(("y", "c")).astype(jnp.int32).reshape(1)
    own_x = lax.axis_index("x").astype(jnp.int32).reshape(1)
    scaling = 1.0 / math.sqrt(rows * lanes * xs * zs)

    def exchange(block):
        chunks = block.reshape(lanes, blocks, block.shape[1])
        return lax.all_to_all(chunks, ("y", "c"), 0, 0, tiled=True).reshape(block.shape)

    units = lanes * blocks
    halves = rows // units
    square = 2 * rows * units * width
    (packed,) = call(
        functools.partial(pack_kernel, lanes),
        "pack",
        [shape((units, 2 * halves * width + 128), bf16)],
        (dest_device, me, own_x, history_rows, cotangent),
        2 * square,
        3,
        (
            pltpu.VMEM((rows, width), bf16),
            pltpu.VMEM((rows, width), bf16),
            pltpu.SemaphoreType.DMA((2,)),
        ),
        2,
    )
    routed, route = call(
        functools.partial(route_kernel, lanes),
        "route",
        [shape((units, 2 * halves * width), bf16), shape((units, units), bf16)],
        (exchange(packed),),
        2 * square,
    )
    slots = rows // WIN * HEADS // 2
    total = width * 5
    vmem = pltpu.VMEM
    side = width // 2
    send, *stored = call(
        functools.partial(layer_kernel, lanes, (xs, ys)),
        "layer",
        [
            shape((side, total), bf16),
            shape((rows, 4 * width), bf16),
            shape((side, rows), bf16),
            shape((side, rows), bf16),
            shape((rows, width), bf16),
            shape((rows, width), bf16),
            shape((rows, 1), f32),
            shape((units, units), bf16),
        ],
        (
            me,
            own_x,
            source_device,
            source_offset,
            exchange(routed),
            segments,
            row_valid,
            joined_weight,
            output_weight,
        ),
        2 * rows * width * width * 10,
        4,
        (
            vmem((rows, width), bf16),
            vmem((rows, width), bf16),
            vmem((rows, 4 * width), bf16),
            vmem((rows, 4 * width), bf16),
            vmem((slots, WIN, 2 * WIN), bf16),
            vmem((slots, WIN, 2 * WIN), bf16),
            vmem((rows, width), f32),
            vmem((rows, 1), f32),
            vmem((rows, width), bf16),
            vmem((side, total), bf16),
            pltpu.SemaphoreType.DMA((5,)),
        ),
        loose=1,
    )
    own = width // (lanes * xs)
    quarters = [shape((ys * own, total), bf16)] * xs
    leaving, *keep = call(
        functools.partial(finish_kernel, lanes),
        "finish",
        [shape((units, halves * width), bf16)] + quarters,
        (joined_weight, *stored),
        2 * rows * width * width * 8,
        scratch=(vmem((units, halves * width), bf16), pltpu.SemaphoreType.DMA(())),
        loose=1,
    )
    swap = [(0, 1), (1, 0)]
    arrived = lax.ppermute(send, "c", swap)
    parts = call(
        add_kernel, "add", quarters, (arrived, *keep), aliases={k + 1: k for k in range(xs)}
    )
    arriving = {
        k: lax.ppermute(parts[k], "x", [(i, i ^ k) for i in range(xs)]) for k in sorted(range(1, xs), key=lambda k: (-(k & 2), k & 1))
    }
    parts = [parts[0], *arriving.values()]
    (merged,) = call(
        merge_kernel,
        "merge",
        [shape((ys, own, total + rows // (ys * own) * width), bf16)],
        (route, exchange(leaving), *parts),
        square,
    )
    merged = lax.all_to_all(merged, "y", 0, 0, tiled=True)
    piece = -(-total // (zs * 128)) * 128
    pieces, mine, other = call(
        fold_kernel,
        "fold",
        [shape((zs, own, piece), bf16)] + [shape((rows // 2, width), bf16)] * 2,
        (me, merged),
        0,
        1,
    )
    row_grad, token = call(
        functools.partial(unpack_kernel, lanes, blocks),
        "unpack",
        [shape((rows, width), bf16), shape((8, 128), f32)],
        (me, mine, lax.ppermute(other, "c", swap)),
        square,
        1,
    )
    pieces = lax.all_to_all(pieces, "z", 0, 0, tiled=True)
    (spread,) = call(
        functools.partial(total_kernel, scaling), "total", [shape((xs * zs, own, piece), bf16)], (pieces,)
    )
    spread = lax.all_to_all(spread, ("x", "z"), 0, 0, tiled=True)
    joined_grad, output_grad = call(
        result_kernel,
        "result",
        [shape((width // lanes, 4 * width), f32), shape((width // lanes, width), f32)],
        (spread.reshape(xs, zs, own, piece), token),
    )
    return (row_grad, joined_grad, output_grad)


def solution(mesh):
    torus = Mesh(mesh.devices.reshape(4, 12, 8, 2), ("x", "z", "y", "c"))
    everywhere = P(("x", "z", "y", "c"), None)
    return jax.shard_map(
        on_device,
        mesh=torus,
        in_specs=(everywhere,) * 7 + (P(), P()),
        out_specs=(everywhere, P(("y", "c"), None), P(("y", "c"), None)),
        check_vma=False,
    )
```

```python
import functools
import math

import jax
import jax.numpy as jnp
from jax import lax
from jax.experimental import pallas as pl
from jax.experimental.pallas import tpu as pltpu
from jax.sharding import Mesh, PartitionSpec as P

HEADS = 8
WIN = 128
epsilon = 1e-05
f32 = jnp.float32
bf16 = jnp.bfloat16
VMEM_LIMIT = 16 * 1024 * 1024
VMEM_MOST = 60 * 1024 * 1024
NT = (((1,), (1,)), ((), ()))
TN = (((0,), (0,)), ((), ()))


def dot(a, b, dims=(((1,), (0,)), ((), ()))):
    return lax.dot_general(a, b, dims, preferred_element_type=f32)


def row_norm(features):
    centred = features - jnp.mean(features, axis=-1, keepdims=True)
    spread = jnp.mean(centred * centred, axis=-1, keepdims=True)
    inverse = lax.rsqrt(spread + epsilon)
    return centred * inverse, inverse


def row_norm_back(cot, normed, inverse):
    mean_cot = jnp.mean(cot, axis=-1, keepdims=True)
    mean_both = jnp.mean(cot * normed, axis=-1, keepdims=True)
    return inverse * (cot - mean_cot - normed * mean_both)


def as_column(row, diagonal):
    return jnp.sum(jnp.where(diagonal, row, 0.0), axis=1, keepdims=True)


def forward_body(
    rows_ref,
    seg_ref,
    valid_ref,
    weight_ref,
    normed_ref,
    inverse_ref,
    active_ref,
    slope_ref,
    weighting_ref,
    score_slope_ref,
    mixed_ref,
    mix_inverse_ref,
    gated_ref,
):
    rows, width = rows_ref.shape
    head = width // HEADS
    pair = 2 * head
    normed, inverse = row_norm(rows_ref[...].astype(f32))
    normed = normed.astype(bf16)
    normed_ref[...] = normed
    inverse_ref[...] = inverse
    for quarter in range(4):
        columns = slice(quarter * width, (quarter + 1) * width)
        projected = dot(normed, weight_ref[:, columns])
        gate = jax.nn.sigmoid(projected)
        active_ref[:, columns] = (projected * gate).astype(bf16)
        slope_ref[:, columns] = (gate * (1.0 + projected * (1.0 - gate))).astype(bf16)
    left = lax.broadcasted_iota(jnp.int32, (WIN, pair), 1) < head
    place_i = lax.broadcasted_iota(jnp.int32, (WIN, WIN), 0)
    place_j = lax.broadcasted_iota(jnp.int32, (WIN, WIN), 1)
    zero = jnp.zeros((), bf16)

    def stacked(block):
        return jnp.concatenate([jnp.where(left, block, zero), jnp.where(left, zero, block)], axis=0)

    for window in range(rows // WIN):
        span = slice(window * WIN, (window + 1) * WIN)
        seg_row = seg_ref[:, span].astype(f32)
        seg_col = as_column(seg_row, place_i == place_j)
        allowed = (seg_col == seg_row) & (place_j <= place_i) & (valid_ref[:, span] == 1)
        allowed = jnp.where(allowed, 1.0, 0.0)
        weights = allowed / jnp.maximum(jnp.sum(allowed, axis=1, keepdims=True), 1.0)
        weights = jnp.concatenate([weights, weights], axis=1)
        pairs = [slice(p * pair, (p + 1) * pair) for p in range(HEADS // 2)]
        values, queries, keys = (
            [active_ref[span, k * width + at.start : k * width + at.stop] for at in pairs]
            for k in (1, 2, 3)
        )
        scores = [dot(query, stacked(key), NT) * head**-0.5 for query, key in zip(queries, keys)]
        gates = [jax.nn.sigmoid(score) for score in scores]
        weightings = [
            (score * gate * weights).astype(bf16) for score, gate in zip(scores, gates)
        ]
        mixture = [
            dot(weighting, stacked(value)) for weighting, value in zip(weightings, values)
        ]
        for p, (score, gate) in enumerate(zip(scores, gates)):
            slot = window * (HEADS // 2) + p
            weighting_ref[slot] = weightings[p]
            slope = gate * (1.0 + score * (1.0 - gate)) * (weights * head**-0.5)
            score_slope_ref[slot] = slope.astype(bf16)
        mixed, mix_inverse = row_norm(jnp.concatenate(mixture, axis=1))
        mixed_ref[span, :] = mixed
        mix_inverse_ref[span, :] = mix_inverse
        gated_ref[span, :] = (mixed * active_ref[span, :width].astype(f32)).astype(bf16)


def backward_body(
    cot_ref,
    valid_ref,
    out_weight_ref,
    normed_ref,
    active_ref,
    slope_ref,
    weighting_ref,
    score_slope_ref,
    mixed_ref,
    mix_inverse_ref,
    gated_ref,
    proj_cot_ref,
    masked_ref,
    normed_t_ref,
    gated_t_ref,
    spread,
    normed_t_early,
    send,
):
    rows, width = cot_ref.shape
    head = width // HEADS
    pair = 2 * head
    place_i = lax.broadcasted_iota(jnp.int32, (rows, rows), 0)
    place_j = lax.broadcasted_iota(jnp.int32, (rows, rows), 1)
    valid_col = as_column(valid_ref[...].astype(f32), place_i == place_j)
    masked = (cot_ref[...].astype(f32) * valid_col).astype(bf16)
    masked_ref[...] = masked
    side = width // 2
    gated_t = permute(spread, gated_ref[...], NT)
    gated_t_ref[...] = gated_t[:side]
    send(4, permute(gated_t[side:], masked))
    normed_t = normed_t_early
    normed_t_ref[...] = normed_t[:side]
    gated_cot = dot(masked, out_weight_ref[...], NT)
    mixed = mixed_ref[...]
    gate_cot = (gated_cot * mixed).astype(bf16).astype(f32)
    proj_cot_ref[:, :width] = (gate_cot * slope_ref[:, :width].astype(f32)).astype(bf16)
    send(0, permute(normed_t[side:], proj_cot_ref[:, :width]))
    mixture_cot = row_norm_back(
        gated_cot * active_ref[:, :width].astype(f32), mixed, mix_inverse_ref[...]
    ).astype(bf16)
    left = lax.broadcasted_iota(jnp.int32, (WIN, pair), 1) < head
    zero = jnp.zeros((), bf16)

    def stacked(block):
        return jnp.concatenate([jnp.where(left, block, zero), jnp.where(left, zero, block)], axis=0)

    def folded(block):
        return jnp.where(left, block[:WIN], block[WIN:])

    for window in range(rows // WIN):
        span = slice(window * WIN, (window + 1) * WIN)
        cots = []
        pairs = [slice(p * pair, (p + 1) * pair) for p in range(HEADS // 2)]
        values, queries, keys = (
            [active_ref[span, k * width + at.start : k * width + at.stop] for at in pairs]
            for k in (1, 2, 3)
        )
        mix_cots = [mixture_cot[span, at] for at in pairs]
        first = window * (HEADS // 2)
        score_cots = []
        for p in range(HEADS // 2):
            weighting_cot = dot(mix_cots[p], stacked(values[p]), NT).astype(bf16).astype(f32)
            score_cots.append((weighting_cot * score_slope_ref[first + p].astype(f32)).astype(bf16))
        value_cots = [
            folded(dot(weighting_ref[first + p], mix_cots[p], TN)) for p in range(HEADS // 2)
        ]
        query_cots = [dot(score_cots[p], stacked(keys[p])) for p in range(HEADS // 2)]
        key_cots = [folded(dot(score_cots[p], queries[p], TN)) for p in range(HEADS // 2)]
        for quarter, parts in ((1, value_cots), (2, query_cots), (3, key_cots)):
            for at, cot in zip(pairs, parts):
                columns = slice(quarter * width + at.start, quarter * width + at.stop)
                slope = slope_ref[span, columns].astype(f32)
                cots.append((columns, (cot.astype(bf16).astype(f32) * slope).astype(bf16)))
        for columns, cot in cots:
            proj_cot_ref[span, columns] = cot
    for quarter in range(1, 4):
        columns = slice(quarter * width, (quarter + 1) * width)
        send(quarter, permute(normed_t[side:], proj_cot_ref[:, columns]))


def permute(order, block, dims=(((1,), (0,)), ((), ()))):
    return dot(order, block, dims).astype(bf16)


def pack_kernel(lanes, dest_ref, me_ref, own_x_ref, rows_hbm, cot_hbm, out_ref, rows_ref, cot_ref, sems):
    del me_ref, own_x_ref
    copies = [
        pltpu.make_async_copy(rows_hbm, rows_ref, sems.at[0]),
        pltpu.make_async_copy(cot_hbm, cot_ref, sems.at[1]),
    ]
    for copy in copies:
        copy.start()
    rows, width = rows_ref.shape
    blocks = dest_ref.shape[1]
    units = lanes * blocks
    halves = rows // units
    place = lax.broadcasted_iota(jnp.int32, (units, 1), 0)
    loaded = lax.broadcasted_iota(jnp.int32, (units, rows), 1)
    orders = []
    for r in range(halves):
        source = place % blocks * (rows // blocks) + r * lanes + place // blocks
        orders.append(jnp.where(source == loaded, 1.0, 0.0).astype(bf16))
    extra = out_ref.shape[1] - 2 * halves * width
    block = lax.broadcasted_iota(jnp.int32, (units, extra), 0) % blocks
    dest = jnp.zeros((units, extra), f32)
    for j in range(blocks):
        dest = jnp.where(block == j, dest_ref[0, j].astype(f32), dest)
    out_ref[:, 2 * halves * width :] = dest.astype(bf16)
    for k, block_ref in enumerate((rows_ref, cot_ref)):
        copies[k].wait()
        for r in range(halves):
            at = (2 * r + k) * width
            out_ref[:, at : at + width] = permute(orders[r], block_ref[...])


def route_kernel(lanes, in_ref, out_ref, order_ref):
    units, payload = out_ref.shape
    blocks = units // lanes
    extra = in_ref.shape[1] - payload
    place = lax.broadcasted_iota(jnp.int32, (units, units), 0)
    other = lax.broadcasted_iota(jnp.int32, (units, units), 1)
    lane = lax.broadcasted_iota(jnp.int32, (units, extra), 1)
    dest = in_ref[:, payload:].astype(f32)
    chosen = jnp.where(dest == lane.astype(f32), 1.0, 0.0)
    earlier = jnp.where(other < place, 1.0, 0.0).astype(bf16)
    rank = jnp.sum(dot(earlier, chosen.astype(bf16)) * chosen, axis=1, keepdims=True)
    target = dest[:, :1] * blocks + rank
    order = jnp.where(target == other.astype(f32), 1.0, 0.0).astype(bf16)
    order_ref[...] = order
    out_ref[...] = permute(order, in_ref[:, :payload], TN)


def slots_of(sources_ref, offsets_ref):
    blocks = sources_ref.shape[1]
    keys = [sources_ref[0, t] * 2 + offsets_ref[0, t] for t in range(blocks)]
    return [
        sum(jnp.where(keys[u] < keys[t], 1, 0) for u in range(blocks) if u != t) for t in range(blocks)
    ]


def gather_order(lanes, sources_ref, offsets_ref, order_ref):
    units = order_ref.shape[0]
    blocks = sources_ref.shape[1]
    inside = lax.broadcasted_iota(jnp.int32, (lanes, 1), 0)
    column = lax.broadcasted_iota(jnp.int32, (lanes, units), 1)
    for t, slot in enumerate(slots_of(sources_ref, offsets_ref)):
        order = jnp.where(column == inside * blocks + slot, 1.0, 0.0)
        order_ref[t * lanes : (t + 1) * lanes, :] = order.astype(bf16)


def spread_order(parts, core, own_x, width):
    xs, ys = parts
    out = lax.broadcasted_iota(jnp.int32, (width, 1), 0)
    column = lax.broadcasted_iota(jnp.int32, (width, width), 1)
    side = width // 2
    block = width // ys // 2
    piece = block // xs
    y = out // piece % ys
    x = out % side // (piece * ys) ^ own_x
    parity = (out // side + core) % 2
    source = y * (2 * block) + parity * block + x * piece + out % piece
    return jnp.where(source == column, 1.0, 0.0).astype(bf16)


def layer_kernel(
    lanes,
    parts,
    me_ref,
    own_x_ref,
    sources_ref,
    offsets_ref,
    in_ref,
    seg_ref,
    valid_ref,
    weight_ref,
    out_weight_ref,
    send_ref,
    proj_cot_ref,
    normed_t_ref,
    gated_t_ref,
    masked_ref,
    rows_ref,
    inverse_ref,
    order_ref,
    cot_ref,
    normed_ref,
    active_ref,
    slope_ref,
    weighting_ref,
    score_slope_ref,
    mixed_ref,
    mix_inverse_ref,
    gated_ref,
    held_ref,
    sems,
):
    width = rows_ref.shape[1]
    copies = []

    def send(quarter, grad):
        columns = slice(quarter * width, (quarter + 1) * width)
        held_ref[:, columns] = grad
        copies.append(
            pltpu.make_async_copy(held_ref.at[:, columns], send_ref.at[:, columns], sems.at[quarter])
        )
        copies[-1].start()

    gather_order(lanes, sources_ref, offsets_ref, order_ref)
    halves = in_ref.shape[1] // (2 * width)
    for k, block_ref in enumerate((rows_ref, cot_ref)):
        for r in range(halves):
            at = (2 * r + k) * width
            block = permute(order_ref[...], in_ref[:, at : at + width])
            for t in range(order_ref.shape[0] // lanes):
                to = (t * halves + r) * lanes
                block_ref[to : to + lanes, :] = block[t * lanes : (t + 1) * lanes]
    stored = (
        active_ref,
        slope_ref,
        weighting_ref,
        score_slope_ref,
        mixed_ref,
        mix_inverse_ref,
        gated_ref,
    )
    spread = spread_order(parts, me_ref[0] % 2, own_x_ref[0], width)
    forward_body(rows_ref, seg_ref, valid_ref, weight_ref, normed_ref, inverse_ref, *stored)
    normed_t_early = permute(spread, normed_ref[...], NT)
    backward_body(
        cot_ref,
        valid_ref,
        out_weight_ref,
        normed_ref,
        *stored,
        proj_cot_ref,
        masked_ref,
        normed_t_ref,
        gated_t_ref,
        spread,
        normed_t_early,
        send,
    )
    for copy in copies:
        copy.wait()


def finish_kernel(
    lanes,
    weight_ref,
    proj_cot_ref,
    normed_t_ref,
    gated_t_ref,
    masked_ref,
    rows_ref,
    inverse_ref,
    order_ref,
    leave_hbm,
    *refs,
):
    *keep_refs, leave_ref, sem = refs
    rows, width = rows_ref.shape

    def put(grad, columns):
        size = keep_refs[0].shape[0]
        for k, keep_ref in enumerate(keep_refs):
            keep_ref[:, columns] = grad[k * size : (k + 1) * size]

    normed_cot = jnp.zeros((rows, width), f32)
    for quarter in range(4):
        columns = slice(quarter * width, (quarter + 1) * width)
        proj_cot = proj_cot_ref[:, columns]
        normed_cot += dot(proj_cot, weight_ref[:, columns], NT)
    masked = masked_ref[...]
    features = rows_ref[...].astype(f32)
    inverse = inverse_ref[...]
    normed_f = (features - jnp.mean(features, axis=-1, keepdims=True)) * inverse
    rows_cot = row_norm_back(normed_cot, normed_f, inverse)
    work_grad = (masked.astype(f32) + rows_cot).astype(bf16)
    units = order_ref.shape[0]
    halves = rows // units
    for r in range(halves):
        parts = [
            work_grad[(t * halves + r) * lanes : (t * halves + r + 1) * lanes]
            for t in range(units // lanes)
        ]
        grad = permute(order_ref[...], jnp.concatenate(parts, axis=0), TN)
        leave_ref[:, r * width : (r + 1) * width] = grad
    copy = pltpu.make_async_copy(leave_ref, leave_hbm, sem)
    copy.start()
    put(permute(gated_t_ref[...], masked), slice(4 * width, 5 * width))
    for quarter in range(4):
        columns = slice(quarter * width, (quarter + 1) * width)
        put(permute(normed_t_ref[...], proj_cot_ref[:, columns]), columns)
    copy.wait()


def add_kernel(arrived_ref, *refs):
    keep_refs, out_refs = refs[: len(refs) // 2], refs[len(refs) // 2 :]
    for k, out_ref in enumerate(out_refs):
        span = slice(k * out_ref.shape[0], (k + 1) * out_ref.shape[0])
        out_ref[...] = keep_refs[k][...] + arrived_ref[span, :]


def merge_kernel(order_ref, back_ref, *refs):
    *part_refs, out_ref = refs
    ys, own, _ = out_ref.shape
    total = part_refs[0].shape[1]
    partial = sum(part_ref[...].astype(f32) for part_ref in part_refs)
    out_ref[:, :, :total] = partial.reshape(ys, own, total).astype(bf16)
    units, width = back_ref.shape
    groups = units // (ys * own)
    back = dot(order_ref[...], back_ref[...]).reshape(ys, groups, own, width)
    for g in range(groups):
        at = total + g * width
        out_ref[:, :, at : at + width] = back[:, g].astype(bf16)


def fold_kernel(me_ref, in_ref, out_ref, mine_ref, other_ref):
    pieces, own, piece = out_ref.shape
    ys = in_ref.shape[0]
    width = mine_ref.shape[1]
    halves = mine_ref.shape[0] // (ys * own)
    total = in_ref.shape[2] - 2 * halves * width
    folded = jnp.sum(in_ref[:, :, :total].astype(f32), axis=0).astype(bf16)
    for k in range(pieces):
        at, end = k * piece, min((k + 1) * piece, total)
        if at < total:
            out_ref[k, :, : end - at] = folded[:, at:end]
        if end - at < piece:
            rest = max(end - at, 0)
            out_ref[k, :, rest:] = jnp.zeros((own, piece - rest), bf16)
    first = me_ref[0] % 2 == 0
    for r in range(halves):
        span = slice(r * ys * own, (r + 1) * ys * own)
        sets = []
        for g in (r, halves + r):
            at = total + g * width
            sets.append(in_ref[:, :, at : at + width].astype(f32).reshape(ys * own, width))
        mine_ref[span, :] = jnp.where(first, sets[0], sets[1]).astype(bf16)
        other_ref[span, :] = jnp.where(first, sets[1], sets[0]).astype(bf16)


def unpack_kernel(lanes, blocks, me_ref, mine_ref, arrived_ref, out_ref, token_ref):
    token_ref[...] = jnp.zeros_like(token_ref)
    rows = out_ref.shape[0]
    side = rows // 2
    out = lax.broadcasted_iota(jnp.int32, (rows, 1), 0)
    column = lax.broadcasted_iota(jnp.int32, (rows, rows), 1)
    block = out // (rows // blocks)
    half = out // lanes % (rows // blocks // lanes)
    piece = out % lanes
    place = half * (blocks * lanes // 2) + piece // 2 * blocks + block
    place += (piece + me_ref[0]) % 2 * side
    order = jnp.where(place == column, 1.0, 0.0).astype(bf16)
    got = dot(order[:, :side], mine_ref[...]) + dot(order[:, side:], arrived_ref[...])
    out_ref[...] = got.astype(bf16)


def total_kernel(scaling, in_ref, out_ref):
    total = jnp.sum(in_ref[...].astype(f32), axis=0, keepdims=True) * scaling
    out_ref[...] = jnp.broadcast_to(total.astype(bf16), out_ref.shape)


def result_kernel(in_ref, after_ref, joined_ref, output_ref):
    del after_ref
    xs, zs, piece_rows, piece = in_ref.shape
    split = joined_ref.shape[1]
    step = math.gcd(piece, split)
    for x in range(xs):
        span = slice(x * piece_rows, (x + 1) * piece_rows)
        for at in range(0, split + output_ref.shape[1], step):
            block = in_ref[x, at // piece, :, at % piece : at % piece + step].astype(f32)
            if at < split:
                joined_ref[span, at : at + step] = block
            else:
                output_ref[span, at - split : at - split + step] = block


def call(kernel, name, out_shape, operands, flops=0, scalars=0, scratch=(), unmoved=0, aliases=None, loose=0):
    moved = sum(math.prod(a.shape) * a.dtype.itemsize for a in (*operands, *out_shape))
    smem = pl.BlockSpec(memory_space=pltpu.SMEM)
    vmem = pl.BlockSpec(memory_space=pltpu.VMEM)
    stay = pl.BlockSpec(memory_space=pl.ANY)
    blocked = len(operands) - scalars - unmoved
    return pl.pallas_call(
        kernel,
        out_shape=tuple(out_shape),
        in_specs=[smem] * scalars + [vmem] * blocked + [stay] * unmoved,
        out_specs=tuple(stay if k < loose else vmem for k in range(len(out_shape))),
        scratch_shapes=list(scratch),
        input_output_aliases=aliases or {},
        compiler_params=pltpu.CompilerParams(vmem_limit_bytes=VMEM_MOST if unmoved else VMEM_LIMIT),
        cost_estimate=pl.CostEstimate(flops=flops, bytes_accessed=moved, transcendentals=0),
        name=name,
    )(*operands)


def on_device(
    history_rows,
    cotangent,
    dest_device,
    source_device,
    source_offset,
    segments,
    row_valid,
    joined_weight,
    output_weight,
):
    shape = jax.ShapeDtypeStruct
    xs, zs, ys = lax.axis_size("x"), lax.axis_size("z"), lax.axis_size("y")
    lanes = ys * lax.axis_size("c")
    rows, width = history_rows.shape
    blocks = dest_device.shape[1]
    me = lax.axis_index(("y", "c")).astype(jnp.int32).reshape(1)
    own_x = lax.axis_index("x").astype(jnp.int32).reshape(1)
    scaling = 1.0 / math.sqrt(rows * lanes * xs * zs)

    def exchange(block):
        chunks = block.reshape(lanes, blocks, block.shape[1])
        return lax.all_to_all(chunks, ("y", "c"), 0, 0, tiled=True).reshape(block.shape)

    units = lanes * blocks
    halves = rows // units
    square = 2 * rows * units * width
    (packed,) = call(
        functools.partial(pack_kernel, lanes),
        "pack",
        [shape((units, 2 * halves * width + 128), bf16)],
        (dest_device, me, own_x, history_rows, cotangent),
        2 * square,
        3,
        (
            pltpu.VMEM((rows, width), bf16),
            pltpu.VMEM((rows, width), bf16),
            pltpu.SemaphoreType.DMA((2,)),
        ),
        2,
    )
    routed, route = call(
        functools.partial(route_kernel, lanes),
        "route",
        [shape((units, 2 * halves * width), bf16), shape((units, units), bf16)],
        (exchange(packed),),
        2 * square,
    )
    slots = rows // WIN * HEADS // 2
    total = width * 5
    vmem = pltpu.VMEM
    side = width // 2
    send, *stored = call(
        functools.partial(layer_kernel, lanes, (xs, ys)),
        "layer",
        [
            shape((side, total), bf16),
            shape((rows, 4 * width), bf16),
            shape((side, rows), bf16),
            shape((side, rows), bf16),
            shape((rows, width), bf16),
            shape((rows, width), bf16),
            shape((rows, 1), f32),
            shape((units, units), bf16),
        ],
        (
            me,
            own_x,
            source_device,
            source_offset,
            exchange(routed),
            segments,
            row_valid,
            joined_weight,
            output_weight,
        ),
        2 * rows * width * width * 10,
        4,
        (
            vmem((rows, width), bf16),
            vmem((rows, width), bf16),
            vmem((rows, 4 * width), bf16),
            vmem((rows, 4 * width), bf16),
            vmem((slots, WIN, 2 * WIN), bf16),
            vmem((slots, WIN, 2 * WIN), bf16),
            vmem((rows, width), f32),
            vmem((rows, 1), f32),
            vmem((rows, width), bf16),
            vmem((side, total), bf16),
            pltpu.SemaphoreType.DMA((5,)),
        ),
        loose=1,
    )
    own = width // (lanes * xs)
    quarters = [shape((ys * own, total), bf16)] * xs
    leaving, *keep = call(
        functools.partial(finish_kernel, lanes),
        "finish",
        [shape((units, halves * width), bf16)] + quarters,
        (joined_weight, *stored),
        2 * rows * width * width * 8,
        scratch=(vmem((units, halves * width), bf16), pltpu.SemaphoreType.DMA(())),
        loose=1,
    )
    swap = [(0, 1), (1, 0)]
    arrived = lax.ppermute(send, "c", swap)
    parts = call(
        add_kernel, "add", quarters, (arrived, *keep), aliases={k + 1: k for k in range(xs)}
    )
    arriving = {
        k: lax.ppermute(parts[k], "x", [(i, i ^ k) for i in range(xs)]) for k in sorted(range(1, xs), key=lambda k: (-(k & 2), k & 1))
    }
    parts = [parts[0], *arriving.values()]
    (merged,) = call(
        merge_kernel,
        "merge",
        [shape((ys, own, total + rows // (ys * own) * width), bf16)],
        (route, exchange(leaving), *parts),
        square,
    )
    merged = lax.all_to_all(merged, "y", 0, 0, tiled=True)
    piece = -(-total // (zs * 128)) * 128
    pieces, mine, other = call(
        fold_kernel,
        "fold",
        [shape((zs, own, piece), bf16)] + [shape((rows // 2, width), bf16)] * 2,
        (me, merged),
        0,
        1,
    )
    row_grad, token = call(
        functools.partial(unpack_kernel, lanes, blocks),
        "unpack",
        [shape((rows, width), bf16), shape((8, 128), f32)],
        (me, mine, lax.ppermute(other, "c", swap)),
        square,
        1,
    )
    pieces = lax.all_to_all(pieces, "z", 0, 0, tiled=True)
    (spread,) = call(
        functools.partial(total_kernel, scaling), "total", [shape((xs * zs, own, piece), bf16)], (pieces,)
    )
    spread = lax.all_to_all(spread, ("x", "z"), 0, 0, tiled=True)
    joined_grad, output_grad = call(
        result_kernel,
        "result",
        [shape((width // lanes, 4 * width), f32), shape((width // lanes, width), f32)],
        (spread.reshape(xs, zs, own, piece), token),
    )
    return (row_grad, joined_grad, output_grad)


def solution(mesh):
    torus = Mesh(mesh.devices.reshape(4, 12, 8, 2), ("x", "z", "y", "c"))
    everywhere = P(("x", "z", "y", "c"), None)
    return jax.shard_map(
        on_device,
        mesh=torus,
        in_specs=(everywhere,) * 7 + (P(), P()),
        out_specs=(everywhere, P(("y", "c"), None), P(("y", "c"), None)),
        check_vma=False,
    )
```

```python
import functools
import math

import jax
import jax.numpy as jnp
from jax import lax
from jax.experimental import pallas as pl
from jax.experimental.pallas import tpu as pltpu
from jax.sharding import Mesh, PartitionSpec as P

HEADS = 8
WIN = 128
epsilon = 1e-05
f32 = jnp.float32
bf16 = jnp.bfloat16
VMEM_LIMIT = 16 * 1024 * 1024
VMEM_MOST = 60 * 1024 * 1024
NT = (((1,), (1,)), ((), ()))
TN = (((0,), (0,)), ((), ()))


def dot(a, b, dims=(((1,), (0,)), ((), ()))):
    return lax.dot_general(a, b, dims, preferred_element_type=f32)


def row_norm(features):
    centred = features - jnp.mean(features, axis=-1, keepdims=True)
    spread = jnp.mean(centred * centred, axis=-1, keepdims=True)
    inverse = lax.rsqrt(spread + epsilon)
    return centred * inverse, inverse


def row_norm_back(cot, normed, inverse):
    mean_cot = jnp.mean(cot, axis=-1, keepdims=True)
    mean_both = jnp.mean(cot * normed, axis=-1, keepdims=True)
    return inverse * (cot - mean_cot - normed * mean_both)


def as_column(row, diagonal):
    return jnp.sum(jnp.where(diagonal, row, 0.0), axis=1, keepdims=True)


def forward_body(
    rows_ref,
    seg_ref,
    valid_ref,
    weight_ref,
    normed_ref,
    inverse_ref,
    active_ref,
    slope_ref,
    weighting_ref,
    score_slope_ref,
    mixed_ref,
    mix_inverse_ref,
    gated_ref,
):
    rows, width = rows_ref.shape
    head = width // HEADS
    pair = 2 * head
    normed, inverse = row_norm(rows_ref[...].astype(f32))
    normed = normed.astype(bf16)
    normed_ref[...] = normed
    inverse_ref[...] = inverse
    for quarter in range(4):
        columns = slice(quarter * width, (quarter + 1) * width)
        projected = dot(normed, weight_ref[:, columns])
        gate = jax.nn.sigmoid(projected)
        active_ref[:, columns] = (projected * gate).astype(bf16)
        slope_ref[:, columns] = (gate * (1.0 + projected * (1.0 - gate))).astype(bf16)
    left = lax.broadcasted_iota(jnp.int32, (WIN, pair), 1) < head
    place_i = lax.broadcasted_iota(jnp.int32, (WIN, WIN), 0)
    place_j = lax.broadcasted_iota(jnp.int32, (WIN, WIN), 1)
    zero = jnp.zeros((), bf16)

    def stacked(block):
        return jnp.concatenate([jnp.where(left, block, zero), jnp.where(left, zero, block)], axis=0)

    for window in range(rows // WIN):
        span = slice(window * WIN, (window + 1) * WIN)
        seg_row = seg_ref[:, span].astype(f32)
        seg_col = as_column(seg_row, place_i == place_j)
        allowed = (seg_col == seg_row) & (place_j <= place_i) & (valid_ref[:, span] == 1)
        allowed = jnp.where(allowed, 1.0, 0.0)
        weights = allowed / jnp.maximum(jnp.sum(allowed, axis=1, keepdims=True), 1.0)
        weights = jnp.concatenate([weights, weights], axis=1)
        pairs = [slice(p * pair, (p + 1) * pair) for p in range(HEADS // 2)]
        values, queries, keys = (
            [active_ref[span, k * width + at.start : k * width + at.stop] for at in pairs]
            for k in (1, 2, 3)
        )
        scores = [dot(query, stacked(key), NT) * head**-0.5 for query, key in zip(queries, keys)]
        gates = [jax.nn.sigmoid(score) for score in scores]
        weightings = [
            (score * gate * weights).astype(bf16) for score, gate in zip(scores, gates)
        ]
        mixture = [
            dot(weighting, stacked(value)) for weighting, value in zip(weightings, values)
        ]
        for p, (score, gate) in enumerate(zip(scores, gates)):
            slot = window * (HEADS // 2) + p
            weighting_ref[slot] = weightings[p]
            slope = gate * (1.0 + score * (1.0 - gate)) * (weights * head**-0.5)
            score_slope_ref[slot] = slope.astype(bf16)
        mixed, mix_inverse = row_norm(jnp.concatenate(mixture, axis=1))
        mixed_ref[span, :] = mixed
        mix_inverse_ref[span, :] = mix_inverse
        gated_ref[span, :] = (mixed * active_ref[span, :width].astype(f32)).astype(bf16)


def backward_body(
    cot_ref,
    valid_ref,
    out_weight_ref,
    normed_ref,
    active_ref,
    slope_ref,
    weighting_ref,
    score_slope_ref,
    mixed_ref,
    mix_inverse_ref,
    gated_ref,
    proj_cot_ref,
    masked_ref,
    normed_t_ref,
    gated_t_ref,
    spread,
    normed_t_early,
    send,
):
    rows, width = cot_ref.shape
    head = width // HEADS
    pair = 2 * head
    place_i = lax.broadcasted_iota(jnp.int32, (rows, rows), 0)
    place_j = lax.broadcasted_iota(jnp.int32, (rows, rows), 1)
    valid_col = as_column(valid_ref[...].astype(f32), place_i == place_j)
    masked = (cot_ref[...].astype(f32) * valid_col).astype(bf16)
    masked_ref[...] = masked
    side = width // 2
    gated_t = permute(spread, gated_ref[...], NT)
    gated_t_ref[...] = gated_t[:side]
    send(4, permute(gated_t[side:], masked))
    normed_t = normed_t_early
    normed_t_ref[...] = normed_t[:side]
    gated_cot = dot(masked, out_weight_ref[...], NT)
    mixed = mixed_ref[...]
    gate_cot = (gated_cot * mixed).astype(bf16).astype(f32)
    proj_cot_ref[:, :width] = (gate_cot * slope_ref[:, :width].astype(f32)).astype(bf16)
    send(0, permute(normed_t[side:], proj_cot_ref[:, :width]))
    mixture_cot = row_norm_back(
        gated_cot * active_ref[:, :width].astype(f32), mixed, mix_inverse_ref[...]
    ).astype(bf16)
    left = lax.broadcasted_iota(jnp.int32, (WIN, pair), 1) < head
    zero = jnp.zeros((), bf16)

    def stacked(block):
        return jnp.concatenate([jnp.where(left, block, zero), jnp.where(left, zero, block)], axis=0)

    def folded(block):
        return jnp.where(left, block[:WIN], block[WIN:])

    for window in range(rows // WIN):
        span = slice(window * WIN, (window + 1) * WIN)
        cots = []
        pairs = [slice(p * pair, (p + 1) * pair) for p in range(HEADS // 2)]
        values, queries, keys = (
            [active_ref[span, k * width + at.start : k * width + at.stop] for at in pairs]
            for k in (1, 2, 3)
        )
        mix_cots = [mixture_cot[span, at] for at in pairs]
        first = window * (HEADS // 2)
        score_cots = []
        for p in range(HEADS // 2):
            weighting_cot = dot(mix_cots[p], stacked(values[p]), NT).astype(bf16).astype(f32)
            score_cots.append((weighting_cot * score_slope_ref[first + p].astype(f32)).astype(bf16))
        value_cots = [
            folded(dot(weighting_ref[first + p], mix_cots[p], TN)) for p in range(HEADS // 2)
        ]
        query_cots = [dot(score_cots[p], stacked(keys[p])) for p in range(HEADS // 2)]
        key_cots = [folded(dot(score_cots[p], queries[p], TN)) for p in range(HEADS // 2)]
        for quarter, parts in ((1, value_cots), (2, query_cots), (3, key_cots)):
            for at, cot in zip(pairs, parts):
                columns = slice(quarter * width + at.start, quarter * width + at.stop)
                slope = slope_ref[span, columns].astype(f32)
                cots.append((columns, (cot.astype(bf16).astype(f32) * slope).astype(bf16)))
        for columns, cot in cots:
            proj_cot_ref[span, columns] = cot
    for quarter in range(1, 4):
        columns = slice(quarter * width, (quarter + 1) * width)
        send(quarter, permute(normed_t[side:], proj_cot_ref[:, columns]))


def permute(order, block, dims=(((1,), (0,)), ((), ()))):
    return dot(order, block, dims).astype(bf16)


def pack_kernel(lanes, dest_ref, me_ref, own_x_ref, rows_hbm, cot_hbm, out_ref, rows_ref, cot_ref, sems):
    del me_ref, own_x_ref
    copies = [
        pltpu.make_async_copy(rows_hbm, rows_ref, sems.at[0]),
        pltpu.make_async_copy(cot_hbm, cot_ref, sems.at[1]),
    ]
    for copy in copies:
        copy.start()
    rows, width = rows_ref.shape
    blocks = dest_ref.shape[1]
    units = lanes * blocks
    halves = rows // units
    place = lax.broadcasted_iota(jnp.int32, (units, 1), 0)
    loaded = lax.broadcasted_iota(jnp.int32, (units, rows), 1)
    orders = []
    for r in range(halves):
        source = place % blocks * (rows // blocks) + r * lanes + place // blocks
        orders.append(jnp.where(source == loaded, 1.0, 0.0).astype(bf16))
    extra = out_ref.shape[1] - 2 * halves * width
    block = lax.broadcasted_iota(jnp.int32, (units, extra), 0) % blocks
    dest = jnp.zeros((units, extra), f32)
    for j in range(blocks):
        dest = jnp.where(block == j, dest_ref[0, j].astype(f32), dest)
    out_ref[:, 2 * halves * width :] = dest.astype(bf16)
    for k, block_ref in enumerate((rows_ref, cot_ref)):
        copies[k].wait()
        for r in range(halves):
            at = (2 * r + k) * width
            out_ref[:, at : at + width] = permute(orders[r], block_ref[...])


def route_kernel(lanes, in_ref, out_ref, order_ref):
    units, payload = out_ref.shape
    blocks = units // lanes
    extra = in_ref.shape[1] - payload
    place = lax.broadcasted_iota(jnp.int32, (units, units), 0)
    other = lax.broadcasted_iota(jnp.int32, (units, units), 1)
    lane = lax.broadcasted_iota(jnp.int32, (units, extra), 1)
    dest = in_ref[:, payload:].astype(f32)
    chosen = jnp.where(dest == lane.astype(f32), 1.0, 0.0)
    earlier = jnp.where(other < place, 1.0, 0.0).astype(bf16)
    rank = jnp.sum(dot(earlier, chosen.astype(bf16)) * chosen, axis=1, keepdims=True)
    target = dest[:, :1] * blocks + rank
    order = jnp.where(target == other.astype(f32), 1.0, 0.0).astype(bf16)
    order_ref[...] = order
    out_ref[...] = permute(order, in_ref[:, :payload], TN)


def slots_of(sources_ref, offsets_ref):
    blocks = sources_ref.shape[1]
    keys = [sources_ref[0, t] * 2 + offsets_ref[0, t] for t in range(blocks)]
    return [
        sum(jnp.where(keys[u] < keys[t], 1, 0) for u in range(blocks) if u != t) for t in range(blocks)
    ]


def gather_order(lanes, sources_ref, offsets_ref, order_ref):
    units = order_ref.shape[0]
    blocks = sources_ref.shape[1]
    inside = lax.broadcasted_iota(jnp.int32, (lanes, 1), 0)
    column = lax.broadcasted_iota(jnp.int32, (lanes, units), 1)
    for t, slot in enumerate(slots_of(sources_ref, offsets_ref)):
        order = jnp.where(column == inside * blocks + slot, 1.0, 0.0)
        order_ref[t * lanes : (t + 1) * lanes, :] = order.astype(bf16)


def spread_order(parts, core, own_x, width):
    xs, ys = parts
    out = lax.broadcasted_iota(jnp.int32, (width, 1), 0)
    column = lax.broadcasted_iota(jnp.int32, (width, width), 1)
    side = width // 2
    block = width // ys // 2
    piece = block // xs
    y = out // piece % ys
    x = out % side // (piece * ys) ^ own_x
    parity = (out // side + core) % 2
    source = y * (2 * block) + parity * block + x * piece + out % piece
    return jnp.where(source == column, 1.0, 0.0).astype(bf16)


def layer_kernel(
    lanes,
    parts,
    me_ref,
    own_x_ref,
    sources_ref,
    offsets_ref,
    in_ref,
    seg_ref,
    valid_ref,
    weight_ref,
    out_weight_ref,
    send_ref,
    proj_cot_ref,
    normed_t_ref,
    gated_t_ref,
    masked_ref,
    rows_ref,
    inverse_ref,
    order_ref,
    cot_ref,
    normed_ref,
    active_ref,
    slope_ref,
    weighting_ref,
    score_slope_ref,
    mixed_ref,
    mix_inverse_ref,
    gated_ref,
    held_ref,
    sems,
):
    width = rows_ref.shape[1]
    copies = []

    def send(quarter, grad):
        columns = slice(quarter * width, (quarter + 1) * width)
        held_ref[:, columns] = grad
        copies.append(
            pltpu.make_async_copy(held_ref.at[:, columns], send_ref.at[:, columns], sems.at[quarter])
        )
        copies[-1].start()

    gather_order(lanes, sources_ref, offsets_ref, order_ref)
    halves = in_ref.shape[1] // (2 * width)
    for k, block_ref in enumerate((rows_ref, cot_ref)):
        for r in range(halves):
            at = (2 * r + k) * width
            block = permute(order_ref[...], in_ref[:, at : at + width])
            for t in range(order_ref.shape[0] // lanes):
                to = (t * halves + r) * lanes
                block_ref[to : to + lanes, :] = block[t * lanes : (t + 1) * lanes]
    stored = (
        active_ref,
        slope_ref,
        weighting_ref,
        score_slope_ref,
        mixed_ref,
        mix_inverse_ref,
        gated_ref,
    )
    spread = spread_order(parts, me_ref[0] % 2, own_x_ref[0], width)
    forward_body(rows_ref, seg_ref, valid_ref, weight_ref, normed_ref, inverse_ref, *stored)
    normed_t_early = permute(spread, normed_ref[...], NT)
    backward_body(
        cot_ref,
        valid_ref,
        out_weight_ref,
        normed_ref,
        *stored,
        proj_cot_ref,
        masked_ref,
        normed_t_ref,
        gated_t_ref,
        spread,
        normed_t_early,
        send,
    )
    for copy in copies:
        copy.wait()


def finish_kernel(
    lanes,
    weight_ref,
    proj_cot_ref,
    normed_t_ref,
    gated_t_ref,
    masked_ref,
    rows_ref,
    inverse_ref,
    order_ref,
    leave_hbm,
    *refs,
):
    *keep_refs, leave_ref, sem = refs
    rows, width = rows_ref.shape

    def put(grad, columns):
        size = keep_refs[0].shape[0]
        for k, keep_ref in enumerate(keep_refs):
            keep_ref[:, columns] = grad[k * size : (k + 1) * size]

    normed_cot = jnp.zeros((rows, width), f32)
    for quarter in range(4):
        columns = slice(quarter * width, (quarter + 1) * width)
        proj_cot = proj_cot_ref[:, columns]
        normed_cot += dot(proj_cot, weight_ref[:, columns], NT)
    masked = masked_ref[...]
    features = rows_ref[...].astype(f32)
    inverse = inverse_ref[...]
    normed_f = (features - jnp.mean(features, axis=-1, keepdims=True)) * inverse
    rows_cot = row_norm_back(normed_cot, normed_f, inverse)
    work_grad = (masked.astype(f32) + rows_cot).astype(bf16)
    units = order_ref.shape[0]
    halves = rows // units
    for r in range(halves):
        parts = [
            work_grad[(t * halves + r) * lanes : (t * halves + r + 1) * lanes]
            for t in range(units // lanes)
        ]
        grad = permute(order_ref[...], jnp.concatenate(parts, axis=0), TN)
        leave_ref[:, r * width : (r + 1) * width] = grad
    copy = pltpu.make_async_copy(leave_ref, leave_hbm, sem)
    copy.start()
    put(permute(gated_t_ref[...], masked), slice(4 * width, 5 * width))
    for quarter in range(4):
        columns = slice(quarter * width, (quarter + 1) * width)
        put(permute(normed_t_ref[...], proj_cot_ref[:, columns]), columns)
    copy.wait()


def add_kernel(arrived_ref, *refs):
    keep_refs, out_refs = refs[: len(refs) // 2], refs[len(refs) // 2 :]
    for k, out_ref in enumerate(out_refs):
        span = slice(k * out_ref.shape[0], (k + 1) * out_ref.shape[0])
        out_ref[...] = keep_refs[k][...] + arrived_ref[span, :]


def merge_kernel(order_ref, back_ref, *refs):
    *part_refs, out_ref = refs
    ys, own, _ = out_ref.shape
    total = part_refs[0].shape[1]
    partial = sum(part_ref[...].astype(f32) for part_ref in part_refs)
    out_ref[:, :, :total] = partial.reshape(ys, own, total).astype(bf16)
    units, width = back_ref.shape
    groups = units // (ys * own)
    back = dot(order_ref[...], back_ref[...]).reshape(ys, groups, own, width)
    for g in range(groups):
        at = total + g * width
        out_ref[:, :, at : at + width] = back[:, g].astype(bf16)


def fold_kernel(me_ref, in_ref, out_ref, mine_ref, other_ref):
    pieces, own, piece = out_ref.shape
    ys = in_ref.shape[0]
    width = mine_ref.shape[1]
    halves = mine_ref.shape[0] // (ys * own)
    total = in_ref.shape[2] - 2 * halves * width
    folded = jnp.sum(in_ref[:, :, :total].astype(f32), axis=0).astype(bf16)
    for k in range(pieces):
        at, end = k * piece, min((k + 1) * piece, total)
        if at < total:
            out_ref[k, :, : end - at] = folded[:, at:end]
        if end - at < piece:
            rest = max(end - at, 0)
            out_ref[k, :, rest:] = jnp.zeros((own, piece - rest), bf16)
    first = me_ref[0] % 2 == 0
    for r in range(halves):
        span = slice(r * ys * own, (r + 1) * ys * own)
        sets = []
        for g in (r, halves + r):
            at = total + g * width
            sets.append(in_ref[:, :, at : at + width].astype(f32).reshape(ys * own, width))
        mine_ref[span, :] = jnp.where(first, sets[0], sets[1]).astype(bf16)
        other_ref[span, :] = jnp.where(first, sets[1], sets[0]).astype(bf16)


def unpack_kernel(lanes, blocks, me_ref, mine_ref, arrived_ref, out_ref, token_ref):
    token_ref[...] = jnp.zeros_like(token_ref)
    rows = out_ref.shape[0]
    side = rows // 2
    out = lax.broadcasted_iota(jnp.int32, (rows, 1), 0)
    column = lax.broadcasted_iota(jnp.int32, (rows, rows), 1)
    block = out // (rows // blocks)
    half = out // lanes % (rows // blocks // lanes)
    piece = out % lanes
    place = half * (blocks * lanes // 2) + piece // 2 * blocks + block
    place += (piece + me_ref[0]) % 2 * side
    order = jnp.where(place == column, 1.0, 0.0).astype(bf16)
    got = dot(order[:, :side], mine_ref[...]) + dot(order[:, side:], arrived_ref[...])
    out_ref[...] = got.astype(bf16)


def total_kernel(scaling, in_ref, out_ref):
    total = jnp.sum(in_ref[...].astype(f32), axis=0, keepdims=True) * scaling
    out_ref[...] = jnp.broadcast_to(total.astype(bf16), out_ref.shape)


def result_kernel(in_ref, after_ref, joined_ref, output_ref):
    del after_ref
    _, xs, piece_rows, piece = in_ref.shape
    split = joined_ref.shape[1]
    step = math.gcd(piece, split)
    for x in range(xs):
        span = slice(x * piece_rows, (x + 1) * piece_rows)
        for at in range(0, split + output_ref.shape[1], step):
            block = in_ref[at // piece, x, :, at % piece : at % piece + step].astype(f32)
            if at < split:
                joined_ref[span, at : at + step] = block
            else:
                output_ref[span, at - split : at - split + step] = block


def call(kernel, name, out_shape, operands, flops=0, scalars=0, scratch=(), unmoved=0, aliases=None, loose=0):
    moved = sum(math.prod(a.shape) * a.dtype.itemsize for a in (*operands, *out_shape))
    smem = pl.BlockSpec(memory_space=pltpu.SMEM)
    vmem = pl.BlockSpec(memory_space=pltpu.VMEM)
    stay = pl.BlockSpec(memory_space=pl.ANY)
    blocked = len(operands) - scalars - unmoved
    return pl.pallas_call(
        kernel,
        out_shape=tuple(out_shape),
        in_specs=[smem] * scalars + [vmem] * blocked + [stay] * unmoved,
        out_specs=tuple(stay if k < loose else vmem for k in range(len(out_shape))),
        scratch_shapes=list(scratch),
        input_output_aliases=aliases or {},
        compiler_params=pltpu.CompilerParams(vmem_limit_bytes=VMEM_MOST if unmoved else VMEM_LIMIT),
        cost_estimate=pl.CostEstimate(flops=flops, bytes_accessed=moved, transcendentals=0),
        name=name,
    )(*operands)


def on_device(
    history_rows,
    cotangent,
    dest_device,
    source_device,
    source_offset,
    segments,
    row_valid,
    joined_weight,
    output_weight,
):
    shape = jax.ShapeDtypeStruct
    xs, zs, ys = lax.axis_size("x"), lax.axis_size("z"), lax.axis_size("y")
    lanes = ys * lax.axis_size("c")
    rows, width = history_rows.shape
    blocks = dest_device.shape[1]
    me = lax.axis_index(("y", "c")).astype(jnp.int32).reshape(1)
    own_x = lax.axis_index("x").astype(jnp.int32).reshape(1)
    scaling = 1.0 / math.sqrt(rows * lanes * xs * zs)

    def exchange(block):
        chunks = block.reshape(lanes, blocks, block.shape[1])
        return lax.all_to_all(chunks, ("y", "c"), 0, 0, tiled=True).reshape(block.shape)

    units = lanes * blocks
    halves = rows // units
    square = 2 * rows * units * width
    (packed,) = call(
        functools.partial(pack_kernel, lanes),
        "pack",
        [shape((units, 2 * halves * width + 128), bf16)],
        (dest_device, me, own_x, history_rows, cotangent),
        2 * square,
        3,
        (
            pltpu.VMEM((rows, width), bf16),
            pltpu.VMEM((rows, width), bf16),
            pltpu.SemaphoreType.DMA((2,)),
        ),
        2,
    )
    routed, route = call(
        functools.partial(route_kernel, lanes),
        "route",
        [shape((units, 2 * halves * width), bf16), shape((units, units), bf16)],
        (exchange(packed),),
        2 * square,
    )
    slots = rows // WIN * HEADS // 2
    total = width * 5
    vmem = pltpu.VMEM
    side = width // 2
    send, *stored = call(
        functools.partial(layer_kernel, lanes, (xs, ys)),
        "layer",
        [
            shape((side, total), bf16),
            shape((rows, 4 * width), bf16),
            shape((side, rows), bf16),
            shape((side, rows), bf16),
            shape((rows, width), bf16),
            shape((rows, width), bf16),
            shape((rows, 1), f32),
            shape((units, units), bf16),
        ],
        (
            me,
            own_x,
            source_device,
            source_offset,
            exchange(routed),
            segments,
            row_valid,
            joined_weight,
            output_weight,
        ),
        2 * rows * width * width * 10,
        4,
        (
            vmem((rows, width), bf16),
            vmem((rows, width), bf16),
            vmem((rows, 4 * width), bf16),
            vmem((rows, 4 * width), bf16),
            vmem((slots, WIN, 2 * WIN), bf16),
            vmem((slots, WIN, 2 * WIN), bf16),
            vmem((rows, width), f32),
            vmem((rows, 1), f32),
            vmem((rows, width), bf16),
            vmem((side, total), bf16),
            pltpu.SemaphoreType.DMA((5,)),
        ),
        loose=1,
    )
    own = width // (lanes * xs)
    quarters = [shape((ys * own, total), bf16)] * xs
    leaving, *keep = call(
        functools.partial(finish_kernel, lanes),
        "finish",
        [shape((units, halves * width), bf16)] + quarters,
        (joined_weight, *stored),
        2 * rows * width * width * 8,
        scratch=(vmem((units, halves * width), bf16), pltpu.SemaphoreType.DMA(())),
        loose=1,
    )
    swap = [(0, 1), (1, 0)]
    arrived = lax.ppermute(send, "c", swap)
    parts = call(
        add_kernel, "add", quarters, (arrived, *keep), aliases={k + 1: k for k in range(xs)}
    )
    arriving = {
        k: lax.ppermute(parts[k], "x", [(i, i ^ k) for i in range(xs)]) for k in sorted(range(1, xs), key=lambda k: (-(k & 2), k & 1))
    }
    parts = [parts[0], *arriving.values()]
    (merged,) = call(
        merge_kernel,
        "merge",
        [shape((ys, own, total + rows // (ys * own) * width), bf16)],
        (route, exchange(leaving), *parts),
        square,
    )
    merged = lax.all_to_all(merged, "y", 0, 0, tiled=True)
    piece = -(-total // (zs * 128)) * 128
    pieces, mine, other = call(
        fold_kernel,
        "fold",
        [shape((zs, own, piece), bf16)] + [shape((rows // 2, width), bf16)] * 2,
        (me, merged),
        0,
        1,
    )
    row_grad, token = call(
        functools.partial(unpack_kernel, lanes, blocks),
        "unpack",
        [shape((rows, width), bf16), shape((8, 128), f32)],
        (me, mine, lax.ppermute(other, "c", swap)),
        square,
        1,
    )
    pieces = lax.all_to_all(pieces, "z", 0, 0, tiled=True)
    (spread,) = call(
        functools.partial(total_kernel, scaling), "total", [shape((xs * zs, own, piece), bf16)], (pieces,)
    )
    spread = lax.all_to_all(spread, ("z", "x"), 0, 0, tiled=True)
    joined_grad, output_grad = call(
        result_kernel,
        "result",
        [shape((width // lanes, 4 * width), f32), shape((width // lanes, width), f32)],
        (spread.reshape(zs, xs, own, piece), token),
    )
    return (row_grad, joined_grad, output_grad)


def solution(mesh):
    torus = Mesh(mesh.devices.reshape(4, 12, 8, 2), ("x", "z", "y", "c"))
    everywhere = P(("x", "z", "y", "c"), None)
    return jax.shard_map(
        on_device,
        mesh=torus,
        in_specs=(everywhere,) * 7 + (P(), P()),
        out_specs=(everywhere, P(("y", "c"), None), P(("y", "c"), None)),
        check_vma=False,
    )
```
